256 devices in a mesh: span: 16 (over z, core), normal: 16 (over x, y).
Axes of the slice: x: 4, y: 4, z: 8, core: 2. Of those that a mesh axis runs over, the one named last changes fastest.
Arguments:
- populations: float32 [19, 4, 256, 2048], P(None, None, 'normal', 'span'), as said below
- wall_mask: int32 [4, 256, 2048], P(None, 'normal', 'span'), may hold values from 0 to 1, as said below
- crop_anchors: int32 [16, 16, 12, 3], P('normal', 'span'), may hold values from 0 to 2032, as said below
- trainers: int32 [16, 16, 12, 1], P('normal', 'span'), may hold values from 0 to 15; in each aligned block of 12 rows (0 to 11, 12 to 23, ..., all dimensions but the last counted through in order) at most 2 rows name the same one
- w_lift: bfloat16 [16, 64, 108], P('span'), may hold values from -0.625 to 0.625
- b_lift: bfloat16 [16, 64], P('span'), may hold values from -1.75 to 1.75
- w_mix: bfloat16 [16, 64, 64], P('span'), may hold values from -0.75 to 0.75
- b_mix: bfloat16 [16, 64], P('span'), may hold values from -1.75 to 1.75
- w_head: bfloat16 [16, 4, 64], P('span'), may hold values from -0.75 to 0.75
- b_head: bfloat16 [16, 4], P('span'), may hold values from -1.75 to 1.75
Outputs:
- final_populations: float32 [19, 4, 256, 2048], P(None, None, 'normal', 'span')
- grad_w_lift: float32 [16, 64, 108], P('span')
- grad_b_lift: float32 [16, 64], P('span')
- grad_w_mix: float32 [16, 64, 64], P('span')
- grad_b_mix: float32 [16, 64], P('span')
- grad_w_head: float32 [16, 4, 64], P('span')
- grad_b_head: float32 [16, 4], P('span')
- member_loss: float32 [16], P('span')
The draws below stay inside these ranges and needn't reach their ends.
Inputs may be any that keep to these rules, and one draw needn't show every extreme that they name: `populations`: every population is positive; density stays near 1 and flow speeds well below 0.3. `wall_mask`: 1 marks a solid cell; the first and the last wall-normal layer of cells are solid, and solid cells are scattered through the fluid. `crop_anchors`: entries are (along-flow, spanwise, wall-normal); a crop at row n of the first dimension and s of the second has along-flow anchor below 4, spanwise anchor at least s * 128 and at most (s + 1) * 128 - 16, wall-normal anchor at least n * 16 and at most (n + 1) * 16 - 16, so it lies inside that tile. `trainers`: among the 12 crops of one device no member is named more than 2 times, and in some device one member is named exactly 2 times.
All inputs are finite; a program needn't handle non-finite values.
Results may differ from the reference program's by a relative error of at most 0.0013.
Values may be sent and summed in bfloat16 or wider, within the bound.
A program may use at most 64 MiB of HBM per device.

```python
import math
import jax
import jax.numpy as jnp
import numpy as np
from jax import lax

SX = 4
CZ = 16
CY = 128
STEPS = 4
CROPS_DEV = 12
CAP = 2
CROP_X = 2
CROP_Z = 16
CROP_Y = 16
FEAT = 4
PATCH = 108
HID = 64
TILES_N = 16
TILES_S = 16
MEMBERS = 16
NZ = 256
NY = 2048
VOX = 512
LOAD = 192


VELOCITY = ((0, 0, 0), (1, 0, 0), (-1, 0, 0), (0, 1, 0), (0, -1, 0), (0, 0, 1), (0, 0, -1), (1, 1, 0), (-1, -1, 0), (1, -1, 0), (-1, 1, 0), (1, 0, 1), (-1, 0, -1), (1, 0, -1), (-1, 0, 1), (0, 1, 1), (0, -1, -1), (0, 1, -1), (0, -1, 1))


WEIGHTS = (1.0 / 3.0,) + (1.0 / 18.0,) * 6 + (1.0 / 36.0,) * 12


def clipped_normal(key, shape):
    return jnp.clip(jax.random.normal(key, shape, jnp.float32), -4.0, 4.0)


def draw_populations(key, part):
    keys = jax.random.split(key, 5)
    shape = (SX, NZ, NY)
    density = 1.0 + 0.02 * clipped_normal(keys[0], shape)
    flow_x = 0.03 + 0.03 * clipped_normal(keys[1], shape)
    flow_y = 0.03 * clipped_normal(keys[2], shape)
    flow_z = 0.03 * clipped_normal(keys[3], shape)
    noise = 0.05 * clipped_normal(keys[4], (19,) + shape)
    speed_sq = flow_x * flow_x + flow_y * flow_y + flow_z * flow_z
    result = []
    for number in range(19):
        step_x, step_y, step_z = VELOCITY[number]
        along = step_x * flow_x + step_y * flow_y + step_z * flow_z
        balance = WEIGHTS[number] * density * (1.0 + 3.0 * along + 4.5 * along * along - 1.5 * speed_sq)
        result.append(balance * (1.0 + noise[number]))
    return jnp.stack(result).astype(jnp.float32)


def draw_wall_mask(key, part):
    shape = (SX, NZ, NY)
    dice = jax.random.randint(key, shape, 0, 64)
    layer = jax.lax.broadcasted_iota(jnp.int32, shape, 1)
    solid = (layer == 0) | (layer == NZ - 1) | (dice == 0)
    return solid.astype(jnp.int32)


def draw_crop_anchors(key, part):
    keys = jax.random.split(key, 3)
    shape = (TILES_N, TILES_S, CROPS_DEV)
    tile_n = jax.lax.broadcasted_iota(jnp.int32, shape, 0)
    tile_s = jax.lax.broadcasted_iota(jnp.int32, shape, 1)
    crop_id = jax.lax.broadcasted_iota(jnp.int32, shape, 2)
    start_x = jax.random.randint(keys[0], shape, 0, SX)
    offset_y = jax.random.randint(keys[1], shape, 0, CY - CROP_Y + 1)
    offset_z = jax.random.randint(keys[2], shape, 0, CZ - CROP_Z + 1)
    highest = (tile_n == TILES_N - 1) & (tile_s == TILES_S - 1) & (crop_id == 0)
    lowest = (tile_n == 0) & (tile_s == 0) & (crop_id == CROPS_DEV - 1)
    offset_y = jnp.where(highest, CY - CROP_Y, jnp.where(lowest, 0, offset_y))
    offset_z = jnp.where(highest, CZ - CROP_Z, jnp.where(lowest, 0, offset_z))
    start_x = jnp.where(highest, SX - 1, jnp.where(lowest, 0, start_x))
    start_y = tile_s * CY + offset_y
    start_z = tile_n * CZ + offset_z
    return jnp.stack([start_x, start_y, start_z], axis=-1).astype(jnp.int32)


def block_scale(key, dims, cuts, least, largest):
    level, own = 1.0, jax.random.fold_in(key, 6)
    for dim, blocks in cuts:
        draws = jnp.exp(jax.random.uniform(jax.random.fold_in(own, dim), (blocks,), jnp.float32, least / len(cuts), largest / len(cuts)))
        level = level * jnp.repeat(draws, dims[dim] // blocks).reshape([-1 if axis == dim else 1 for axis in range(len(dims))])
    return level


def shared_out(key, own, number, rows, amount, top, bound, skew):
    sequence = jax.random.permutation(key, amount)
    heavy_load, ordinary = shares(amount, rows * top, bound, skew, True), shares(amount, rows * top, bound, skew, False)
    places = jnp.arange(amount)

    def named(tallies, rotation):
        used = int((tallies > 0).sum())
        fixed = max(1, used // 4)
        shifted = fixed + (places - fixed + rotation * (used - fixed)) % max(1, amount - fixed)
        return jnp.zeros((amount,), jnp.int32).at[sequence[jnp.where(places < fixed, places, shifted)]].set(jnp.asarray(tallies, jnp.int32))

    tallies = jnp.where(number % 4 == 0, named(heavy_load, number // 4), named(ordinary, number - number // 4 - 1))
    mixed = jax.random.permutation(jax.random.fold_in(own, 3), amount)
    giver, sink = mixed[0:amount // 2 * 2:2], mixed[1:amount // 2 * 2:2]
    room = jnp.minimum(tallies[giver] - 1, bound - tallies[sink]) // 2
    room = jnp.where((giver == sequence[0]) | (sink == sequence[0]) | (tallies[sink] == 0), 0, jnp.maximum(room, 0))
    shifted = jax.random.randint(jax.random.fold_in(own, 4), (amount // 2,), 0, 1 << 20) % (room + 1)
    tallies = tallies.at[giver].add(-shifted).at[sink].add(shifted)
    members = jnp.searchsorted(jnp.cumsum(tallies), jnp.arange(rows * top), side="right").astype(jnp.int32)
    table = members.reshape(top, rows).T
    table = table[jax.random.permutation(jax.random.fold_in(own, 1), rows)]
    rotation = jax.random.randint(jax.random.fold_in(own, 2), (rows, 1), 0, top)
    return jnp.take_along_axis(table, (jnp.arange(top)[None, :] + rotation) % top, axis=1)


def shares(number_of, total, reach, slope, full):
    portions = [(1 << 20) // math.isqrt(rank ** slope) + 1 for rank in range(1, number_of + 1)]
    largest = reach if full else min(reach, max(-(-total // number_of), total * portions[0] // sum(portions)))
    least = 1 if total - largest >= number_of - 1 else 0
    given, rest = [largest] + [least] * (number_of - 1), total - largest - least * (number_of - 1)
    while rest > 0:
        candidates = [i for i in range(1, number_of) if given[i] < largest] or [i for i in range(1, number_of) if given[i] < reach]
        whole, remaining = sum([portions[i] for i in candidates]), rest
        for i in candidates:
            more = min(reach - given[i], max(1, remaining * portions[i] // whole), rest)
            given[i] = given[i] + more
            rest = rest - more
    return np.array(given)


def scatter_about(key, shape, width, reach, shards=(), held_as=jnp.bfloat16):
    factor_of = block_scale(key, shape, shards, -0.22, 0.18) if shards else 1.0
    values = jax.random.normal(key, shape, jnp.float32) * width * factor_of
    return jnp.minimum(jnp.maximum(values, -reach), reach).astype(held_as)


def setup_inputs(seed: int = 0) -> dict:
    splits = jax.random.split(jax.random.key(seed), 11)
    populations = draw_populations(jax.random.fold_in(splits[10], 71), 0)
    wall_mask = draw_wall_mask(jax.random.fold_in(splits[10], 71), 0)
    crop_anchors = draw_crop_anchors(jax.random.fold_in(splits[10], 71), 0)
    trainers_keys = jax.random.split(jax.random.fold_in(splits[3], 1), TILES_N * TILES_S * CROPS_DEV // CROPS_DEV)
    trainers_turns = jax.random.permutation(jax.random.fold_in(splits[3], 3), TILES_N * TILES_S * CROPS_DEV // CROPS_DEV)
    trainers = jax.vmap(lambda own, number: shared_out(jax.random.fold_in(splits[3], 2), own, number, CROPS_DEV, MEMBERS, 1, CAP, 2))(trainers_keys, trainers_turns).reshape((TILES_N, TILES_S, CROPS_DEV, 1))
    w_lift = scatter_about(splits[4], (MEMBERS, HID, PATCH), PATCH ** -0.5, 0.625, ((0, 16),))
    b_lift = scatter_about(splits[5], (MEMBERS, HID), 0.3, 1.75, ((0, 16),))
    w_mix = scatter_about(splits[6], (MEMBERS, HID, HID), HID ** -0.5, 0.75, ((0, 16),))
    b_mix = scatter_about(splits[7], (MEMBERS, HID), 0.3, 1.75, ((0, 16),))
    w_head = scatter_about(splits[8], (MEMBERS, FEAT, HID), HID ** -0.5, 0.75, ((0, 16),))
    b_head = scatter_about(splits[9], (MEMBERS, FEAT), 0.3, 1.75, ((0, 16),))
    return dict(populations=populations, wall_mask=wall_mask, crop_anchors=crop_anchors, trainers=trainers, w_lift=w_lift, b_lift=b_lift, w_mix=w_mix, b_mix=b_mix, w_head=w_head, b_head=b_head)


VELOCITY = ((0, 0, 0), (1, 0, 0), (-1, 0, 0), (0, 1, 0), (0, -1, 0), (0, 0, 1), (0, 0, -1), (1, 1, 0), (-1, -1, 0), (1, -1, 0), (-1, 1, 0), (1, 0, 1), (-1, 0, -1), (1, 0, -1), (-1, 0, 1), (0, 1, 1), (0, -1, -1), (0, 1, -1), (0, -1, 1))
WEIGHTS = (1.0 / 3.0,) + (1.0 / 18.0,) * 6 + (1.0 / 36.0,) * 12
OPPOSITE = (0, 2, 1, 4, 3, 6, 5, 8, 7, 10, 9, 12, 11, 14, 13, 16, 15, 18, 17)
OMEGA = 1.25
SCALE_DENSITY = 50.0
SCALE_FLOW = 30.0

def signed_sum(entries, factors):
    running = None
    for entry, factor in zip(entries, factors):
        if factor == 0:
            continue
        addend = entry if factor > 0 else -entry
        running = addend if running is None else running + addend
    return running

def moments(states):
    density = states[0]
    for number in range(1, 19):
        density = density + states[number]
    flows = []
    for axis_id in range(3):
        summed = signed_sum([states[number] for number in range(19)], [VELOCITY[number][axis_id] for number in range(19)])
        flows.append(summed / density)
    return (density, flows[0], flows[1], flows[2])

def collide(states, wet_cells):
    density, flow_x, flow_y, flow_z = moments(states)
    speed_sq = flow_x * flow_x + flow_y * flow_y + flow_z * flow_z
    result = []
    for number in range(19):
        along = signed_sum((flow_x, flow_y, flow_z), VELOCITY[number])
        if along is None:
            along = jnp.zeros_like(density)
        balance = WEIGHTS[number] * density * (1.0 + 3.0 * along + 4.5 * along * along - 1.5 * speed_sq)
        relaxed = states[number] - OMEGA * (states[number] - balance)
        result.append(jnp.where(wet_cells, relaxed, states[OPPOSITE[number]]))
    return result

def features(states, fluid):
    density, flow_x, flow_y, flow_z = moments(states)
    stacked = jnp.stack([(density - 1.0) * SCALE_DENSITY, flow_x * SCALE_FLOW, flow_y * SCALE_FLOW, flow_z * SCALE_FLOW])
    return stacked * fluid

def cut_crop(field, start_x, start_z, start_y):
    depth = field.shape[0]
    zero_start = jnp.zeros((), jnp.int32)
    piece = lax.dynamic_slice(field, (zero_start, zero_start, start_z.astype(jnp.int32), start_y.astype(jnp.int32)), (depth, field.shape[1], CROP_Z, CROP_Y))
    rows_x = (start_x.astype(jnp.int32) + jnp.arange(CROP_X, dtype=jnp.int32)) % field.shape[1]
    piece = jnp.take(piece, rows_x.astype(jnp.int32), axis=1)
    return piece.reshape(depth, VOX)

def crop_sample(before, after, fluid, anchor):
    start_x, start_y, start_z = (anchor[0], anchor[1], anchor[2])
    early = cut_crop(before, start_x, start_z, start_y)
    late = cut_crop(after, start_x, start_z, start_y)
    wet_part = cut_crop(fluid[None], start_x, start_z, start_y)
    return (early.astype(jnp.bfloat16), (late - early).astype(jnp.bfloat16), wet_part.astype(jnp.bfloat16))

def make_patches(inputs):
    plane = CROP_Z * CROP_Y
    margin = plane + CROP_Y + 1
    padded = jnp.pad(inputs, ((0, 0), (margin, margin)))
    voxel = jnp.arange(VOX, dtype=jnp.int32)
    row_z = voxel // CROP_Y % CROP_Z
    row_y = voxel % CROP_Y
    pieces = []
    for shift_x in (-1, 0, 1):
        for shift_z in (-1, 0, 1):
            for shift_y in (-1, 0, 1):
                offset = shift_x * plane + shift_z * CROP_Y + shift_y
                moved = padded[:, margin + offset:margin + offset + VOX]
                inside = (row_z + shift_z >= 0) & (row_z + shift_z < CROP_Z) & (row_y + shift_y >= 0) & (row_y + shift_y < CROP_Y)
                pieces.append(jnp.where(inside[None, :], moved, jnp.zeros_like(moved)))
    return jnp.concatenate(pieces, axis=0)

def crop_loss(params, inputs, target, wet_part):
    w_one, b_one, w_two, b_two, w_three, b_three = params
    patched = make_patches(inputs)
    first = jnp.dot(w_one.astype(jnp.bfloat16), patched, preferred_element_type=jnp.float32) + b_one[:, None]
    hidden_one = jax.nn.gelu(first, approximate=True).astype(jnp.bfloat16)
    second = jnp.dot(w_two.astype(jnp.bfloat16), hidden_one, preferred_element_type=jnp.float32) + b_two[:, None]
    hidden_two = (hidden_one.astype(jnp.float32) + jax.nn.gelu(second, approximate=True)).astype(jnp.bfloat16)
    predicted = jnp.dot(w_three.astype(jnp.bfloat16), hidden_two, preferred_element_type=jnp.float32) + b_three[:, None]
    missed = predicted - target.astype(jnp.float32)
    return jnp.sum(wet_part.astype(jnp.float32) * missed * missed) / (4.0 * VOX)

def reference(populations, wall_mask, crop_anchors, trainers, w_lift, b_lift, w_mix, b_mix, w_head, b_head):
    fluid = (1 - wall_mask).astype(jnp.float32)
    wet_cells = wall_mask == 0
    before = features(populations, fluid)
    states = populations
    for step in range(STEPS):
        post = collide(states, wet_cells)
        moved = [jnp.roll(post[number], (VELOCITY[number][0], VELOCITY[number][2], VELOCITY[number][1]), axis=(0, 1, 2)) for number in range(19)]
        states = jnp.stack(moved)
    after = features(states, fluid)
    params = tuple((param.astype(jnp.float32) for param in (w_lift, b_lift, w_mix, b_mix, w_head, b_head)))
    anchor_rows = crop_anchors.reshape(TILES_N, TILES_S * CROPS_DEV, 3)
    trainer_rows = trainers.reshape(TILES_N, TILES_S * CROPS_DEV)

    def row_terms(packed):
        anchor_row, trainer_row = packed
        inputs, target, wet_part = jax.vmap(lambda anchor: crop_sample(before, after, fluid, anchor))(anchor_row)
        chosen = tuple((param[trainer_row] for param in params))
        losses, grads = jax.vmap(jax.value_and_grad(crop_loss))(chosen, inputs, target, wet_part)
        bucketed = tuple((jax.ops.segment_sum(grad_part, trainer_row, num_segments=MEMBERS) for grad_part in grads))
        return bucketed + (jax.ops.segment_sum(losses, trainer_row, num_segments=MEMBERS),)
    terms = lax.map(row_terms, (anchor_rows, trainer_rows))
    totals = tuple((lax.optimization_barrier(jnp.sum(part_sum, axis=0)) / float(LOAD) for part_sum in terms))
    return (states, totals[0], totals[1], totals[2], totals[3], totals[4], totals[5], totals[6])
```

```python
import functools

import jax
import jax.numpy as jnp
import numpy as np
from jax import lax
from jax.experimental import pallas as pl
from jax.experimental.pallas import tpu as pltpu
from jax.sharding import PartitionSpec as P

STEPS = 4
CROPS_DEV = 12
SX, CZ, CY = 4, 16, 128
EZ, EY = 24, 256
HID = 64
VOX = 512

VELOCITY = (
    (0, 0, 0),
    (1, 0, 0),
    (-1, 0, 0),
    (0, 1, 0),
    (0, -1, 0),
    (0, 0, 1),
    (0, 0, -1),
    (1, 1, 0),
    (-1, -1, 0),
    (1, -1, 0),
    (-1, 1, 0),
    (1, 0, 1),
    (-1, 0, -1),
    (1, 0, -1),
    (-1, 0, 1),
    (0, 1, 1),
    (0, -1, -1),
    (0, 1, -1),
    (0, -1, 1),
)
WEIGHTS = (1.0 / 3.0,) + (1.0 / 18.0,) * 6 + (1.0 / 36.0,) * 12
OPPOSITE = (0, 2, 1, 4, 3, 6, 5, 8, 7, 10, 9, 12, 11, 14, 13, 16, 15, 18, 17)
OMEGA = 1.25
SCALE_DENSITY = 50.0
SCALE_FLOW = 30.0
F32 = jnp.float32
BF16 = jnp.bfloat16
MESH = pl.DeviceIdType.MESH


def signed_sum(entries, factors):
    running = None
    for entry, factor in zip(entries, factors):
        if factor == 0:
            continue
        if running is None:
            running = entry if factor > 0 else -entry
        else:
            running = running + entry if factor > 0 else running - entry
    return running


def moments(states):
    density = states[0]
    for number in range(1, 19):
        density = density + states[number]
    inverse = 1.0 / density
    flows = []
    for axis_id in range(3):
        summed = signed_sum(states, [VELOCITY[number][axis_id] for number in range(19)])
        flows.append(summed * inverse)
    return (density, flows[0], flows[1], flows[2])


def collide(states, wet_cells):
    density, flow_x, flow_y, flow_z = moments(states)
    flows = (flow_x, flow_y, flow_z)
    speed_sq = flow_x * flow_x + flow_y * flow_y + flow_z * flow_z
    base = 1.0 - 1.5 * speed_sq
    result = [None] * 19
    kept = 1.0 - OMEGA
    scaled = {w: (OMEGA * w) * density for w in set(WEIGHTS)}
    relaxed = kept * states[0] + scaled[WEIGHTS[0]] * base
    result[0] = jnp.where(wet_cells, relaxed, states[0])
    for number in range(1, 19, 2):
        other = OPPOSITE[number]
        along = signed_sum(flows, VELOCITY[number])
        weight = scaled[WEIGHTS[number]]
        even = weight * (base + (4.5 * along) * along)
        odd = weight * (3.0 * along)
        forth = kept * states[number] + (even + odd)
        back = kept * states[other] + (even - odd)
        result[number] = jnp.where(wet_cells, forth, states[other])
        result[other] = jnp.where(wet_cells, back, states[number])
    return result


def features(states, fluid):
    density, flow_x, flow_y, flow_z = moments(states)
    return [
        (density - 1.0) * SCALE_DENSITY * fluid,
        flow_x * SCALE_FLOW * fluid,
        flow_y * SCALE_FLOW * fluid,
        flow_z * SCALE_FLOW * fluid,
    ]


def lattice_kernel(
    ns,
    nn,
    pop,
    wall,
    wb,
    fin,
    feat,
    wall_w,
    pack_l,
    pack_r,
    pack_u,
    pack_d,
    got_l,
    got_r,
    got_u,
    got_d,
    got_c,
    weights,
    cells,
    post,
    halo_send,
    halo_recv,
    ag_send,
    ag_recv,
    fw_send,
    fw_recv,
):
    s = lax.axis_index("span")
    n = lax.axis_index("normal")
    chips = ns // 2
    chip = s // 2
    core = s % 2
    right, left = (s + 1) % ns, (s + ns - 1) % ns
    up, down = (n + 1) % nn, (n + nn - 1) % nn
    sibling = chip * 2 + (1 - core)

    def place(nn_, ss_):
        return {"normal": nn_, "span": ss_}

    peers = [
        place(n, right),
        place(n, left),
        place(up, s),
        place(down, s),
        place(up, right),
        place(up, left),
        place(down, right),
        place(down, left),
        place(n, sibling),
    ]
    z_peers = [((chip + k) % chips) * 2 + core for k in range(1, chips)]
    peers += [place(n, peer) for peer in z_peers]
    barrier = pltpu.get_barrier_semaphore()
    for peer in peers:
        pl.semaphore_signal(barrier, inc=1, device_id=peer, device_id_type=MESH)

    sub = lax.broadcasted_iota(jnp.int32, (8, 128), 0)
    low = sub < 4

    def field_of(k):
        return pop[k] if k < 19 else wall[...].astype(F32)

    for k in range(20):
        f = field_of(k)
        for j in range(2):
            t0, t1 = f[2 * j], f[2 * j + 1]
            pack_u[k, j] = jnp.where(low, pltpu.roll(t1[8:16], 4, 0), t0[8:16])
            pack_d[k, j] = jnp.where(low, t0[0:8], pltpu.roll(t1[0:8], 4, 0))
    pl.semaphore_wait(barrier, len(peers))

    def halo(i, src, dst, peer):
        return pltpu.make_async_remote_copy(
            src_ref=src,
            dst_ref=dst,
            send_sem=halo_send.at[i],
            recv_sem=halo_recv.at[i],
            device_id=peer,
            device_id_type=MESH,
        )

    sends = [
        halo(0, pack_u, got_u, place(up, s)),
        halo(1, pack_d, got_d, place(down, s)),
    ]
    for copy in sends:
        copy.start()

    slot = lax.broadcasted_iota(jnp.int32, (64, 128), 1) // 4
    pl_val = jnp.ones((64, 128), F32)
    pr_val = jnp.ones((64, 128), F32)
    for k in range(20):
        f = field_of(k).reshape(64, 128)
        rolled = pltpu.roll(f, 4 * k, 1) if k else f
        pl_val = jnp.where(slot == k, rolled, pl_val)
        pr_val = jnp.where(slot == (k - 1) % 32, rolled, pr_val)
    pack_l[...] = pl_val.reshape(SX, CZ, CY)
    pack_r[...] = pr_val.reshape(SX, CZ, CY)
    top, bottom = pl.ds(8, 8), pl.ds(0, 8)
    more = [
        halo(2, pack_l, got_l, place(n, left)),
        halo(3, pack_r, got_r, place(n, right)),
        halo(4, pack_l.at[:, bottom, :], got_c.at[0], place(down, left)),
        halo(5, pack_l.at[:, top, :], got_c.at[1], place(up, left)),
        halo(6, pack_r.at[:, bottom, :], got_c.at[2], place(down, right)),
        halo(7, pack_r.at[:, top, :], got_c.at[3], place(up, right)),
    ]
    for copy in more:
        copy.start()
    sends += more

    gathers = []
    for k, peer in enumerate(z_peers):
        gathers.append(
            pltpu.make_async_remote_copy(
                src_ref=wb,
                dst_ref=weights.at[s],
                send_sem=ag_send.at[k],
                recv_sem=ag_recv.at[k],
                device_id=place(n, peer),
                device_id_type=MESH,
            )
        )
    for copy in gathers:
        copy.start()

    def forward(i, src, owner):
        return pltpu.make_async_remote_copy(
            src_ref=src,
            dst_ref=weights.at[owner],
            send_sem=fw_send.at[i],
            recv_sem=fw_recv.at[i],
            device_id=place(n, sibling),
            device_id_type=MESH,
        )

    forwards = [forward(0, wb, s)]
    forwards[0].start()
    wall_w[s] = wb[...]

    for k in range(20):
        cells[k, :, 0:CZ, 0:CY] = field_of(k)
    fluid = (1 - wall[...]).astype(F32)
    before = features([pop[k] for k in range(19)], fluid)

    for copy in sends:
        copy.wait()

    low4 = jnp.broadcast_to(low[None], (SX, 8, 128))
    edge_l = jnp.concatenate([got_l[...], jnp.where(low4, got_c[0], got_c[1])], axis=1)
    edge_r = jnp.concatenate([got_r[...], jnp.where(low4, got_c[2], got_c[3])], axis=1)
    edge_l = edge_l.reshape(SX * EZ, 128)
    edge_r = edge_r.reshape(SX * EZ, 128)
    odd = (lax.broadcasted_iota(jnp.int32, (SX * EZ, 128), 1) // 4) % 2 == 1
    mixed = (jnp.where(odd, edge_r, edge_l), jnp.where(odd, edge_l, edge_r))
    for k in range(20):
        side = mixed[k % 2]
        if k:
            side = pltpu.roll(side, 128 - 4 * k, 1)
        cells[k, :, :, CY:EY] = side.reshape(SX, EZ, 128)
        for j in range(2):
            u, d = got_u[k, j], got_d[k, j]
            cells[k, 2 * j, CZ:EZ, 0:CY] = jnp.where(low, d, u)
            cells[k, 2 * j + 1, CZ:EZ, 0:CY] = pltpu.roll(jnp.where(low, u, d), 4, 0)

    def one_step(step, carry):
        def one_chunk(i, inner):
            x = i // 3
            rows = pl.ds(pl.multiple_of((i % 3) * 8, 8), 8)
            states = [cells[q, x, rows, :] for q in range(19)]
            wet = cells[19, x, rows, :] < 0.5
            for q, value in enumerate(collide(states, wet)):
                post[q, x, rows, :] = value
            return inner

        lax.fori_loop(0, 12, one_chunk, 0)

        def one_slab(x, inner):
            for q in range(19):
                cx, cy, cz = VELOCITY[q]
                slab = post[q, (x + SX - cx) % SX]
                if cz:
                    slab = pltpu.roll(slab, cz % EZ, 0)
                if cy:
                    slab = pltpu.roll(slab, cy % EY, 1)
                cells[q, x] = slab
            return inner

        lax.fori_loop(0, SX, one_slab, 0)
        return carry

    lax.fori_loop(0, 2, one_step, 0)
    for k in range(1, chips):
        gathers[k - 1].wait()
        owner = ((chip + chips - k) % chips) * 2 + core
        copy = forward(k, weights.at[owner], owner)
        copy.start()
        forwards.append(copy)
        wall_w[owner] = weights[owner]
    lax.fori_loop(2, STEPS, one_step, 0)

    final = [cells[q, :, 0:CZ, 0:CY] for q in range(19)]
    for q in range(19):
        fin[q] = final[q]
    after = features(final, fluid)
    for c in range(4):
        feat[:, c] = before[c].astype(BF16)
        feat[:, 4 + c] = (after[c] - before[c]).astype(BF16)
    feat[:, 8] = fluid.astype(BF16)
    for copy in forwards:
        copy.wait()
    for k in range(chips):
        owner = ((chip + chips - k) % chips) * 2 + (1 - core)
        wall_w[owner] = weights[owner]


def gelu_both(x):
    c1, c2 = 0.7978845608028654, 0.7978845608028654 * 0.044715
    sq = x * x
    half = 0.5 * jnp.tanh(x * (c1 + c2 * sq)) + 0.5
    value = x * half
    slope = half + value * (1.0 - half) * (2.0 * c1 + 6.0 * c2 * sq)
    return value, slope


NT = (((1,), (1,)), ((), ()))
TN = (((0,), (0,)), ((), ()))


def dot(a, b, dims=(((1,), (0,)), ((), ()))):
    return lax.dot_general(a, b, dims, preferred_element_type=F32)


SHIFTS = [(a, b, c) for a in (-1, 0, 1) for b in (-1, 0, 1) for c in (-1, 0, 1)]


def constants():
    row = np.arange(288)
    lane = np.arange(256)
    spread = (lane[None, :] // 16 == row[:, None] % 16).astype(np.float32)
    select = np.zeros((48, 576), np.float32)
    for kind in range(3):
        for xi in range(2):
            for i in range(8):
                crop, channel = i // 4, i % 4
                f = (channel, 4 + channel, 8)[kind]
                start = crop * 288 + xi * 144 + f * 16
                select[kind * 16 + xi * 8 + i, start : start + 16] = 1.0
    expand = np.zeros((2, 128, 256), np.float32)
    for pos in range(2):
        for k in range(27):
            for c in range(4):
                expand[pos, 4 * k + c, 8 * k + 4 * pos + c] = 1.0
        expand[pos, 108, 216] = 1.0
    voxel = np.arange(VOX)
    vx, vz, vy = voxel // 256, voxel // 16 % 16, voxel % 16
    inside = np.ones((256, VOX), np.float32)
    for k, (dx, dz, dy) in enumerate(SHIFTS):
        good = (
            (vx + dx >= 0)
            & (vx + dx < 2)
            & (vz + dz >= 0)
            & (vz + dz < 16)
            & (vy + dy >= 0)
            & (vy + dy < 16)
        )
        inside[8 * k : 8 * k + 8] = good[None]
    return (
        jnp.asarray(spread),
        jnp.asarray(select, BF16),
        jnp.asarray(expand, BF16),
        jnp.asarray(np.transpose(expand, (0, 2, 1)), BF16),
        jnp.asarray(inside, BF16),
    )


def train_kernel(
    anchors, trainers, feat, wall_w, spread, select, expand, shrink, inside, grads
):
    def clear(i, carry):
        grads[i % 2, i // 2] = jnp.zeros((128, 128), F32)
        return carry

    lax.fori_loop(0, grads.shape[0] * grads.shape[1], clear, 0)
    unit_row = (lax.broadcasted_iota(jnp.int32, (64, VOX), 0) == 0).astype(F32)
    unit = unit_row.astype(BF16)
    lane64 = lax.broadcasted_iota(jnp.int32, (64, 128), 1)
    lane128 = lax.broadcasted_iota(jnp.int32, (128, 128), 1)
    pick_row = lax.broadcasted_iota(jnp.int32, (128, 256), 0)
    pick_lane = lax.broadcasted_iota(jnp.int32, (128, 256), 1) % 16
    ahead = pick_row - pick_lane

    def one_pair(i, carry):
        parts, owners = [], []
        for j in range(2):
            crop = 2 * i + j
            ox = anchors[0, 0, crop, 0]
            oy = anchors[0, 0, crop, 1] % CY
            owners.append(trainers[0, 0, crop, 0])
            near = feat[ox].reshape(144, 128)
            far = feat[(ox + 1) % SX].reshape(144, 128)
            window = (ahead == oy).astype(F32).astype(BF16)
            wide = dot(jnp.concatenate([near, far], axis=0), window)
            parts.append((wide * spread[...]).astype(BF16))
        rows = dot(select[...], jnp.concatenate(parts, axis=0))
        x8 = jnp.concatenate([rows[0:8], rows[8:16]], axis=1)
        t8 = jnp.concatenate([rows[16:24], rows[24:32]], axis=1)
        w8 = jnp.concatenate([rows[32:40], rows[40:48]], axis=1)
        moved = []
        for dx, dz, dy in SHIFTS:
            shift = (-(dx * 256 + dz * 16 + dy)) % VOX
            moved.append(pltpu.roll(x8, shift, 1) if shift else x8)
        moved.append(unit_row[0:40])
        patches = jnp.concatenate(moved, axis=0).astype(BF16) * inside[...]
        mats = [wall_w[owner] for owner in owners]
        lift = jnp.concatenate(
            [dot(mats[j][0:64], expand[j]) for j in range(2)], axis=0
        ).astype(BF16)
        h1f, slope1 = gelu_both(dot(lift, patches))
        h1 = h1f.astype(BF16)
        slopes2, h1s, h2s, pred = [], [], [], None
        for j in range(2):
            own = h1[64 * j : 64 * j + 64]
            ext = jnp.concatenate([own, unit], axis=0)
            z2 = dot(mats[j][64:128], ext)
            g2, slope2 = gelu_both(z2)
            h2 = (own.astype(F32) + g2).astype(BF16)
            ext2 = jnp.concatenate([h2, unit], axis=0)
            out = dot(mats[j][128:144], ext2)[8 * j : 8 * j + 8]
            pred = out if pred is None else pred + out
            slopes2.append(slope2)
            h1s.append(ext)
            h2s.append(ext2)
        missed = pred - t8
        weighted = w8 * missed
        loss8 = weighted * missed * (1.0 / (4.0 * VOX))
        dpred = weighted * (2.0 / (4.0 * VOX))
        errors = jnp.concatenate([dpred, loss8], axis=0).astype(BF16)
        errors = jnp.concatenate([jnp.zeros((112, VOX), BF16), errors], axis=0)
        dh1s, firsts = [], []
        for j in range(2):
            low = 112 + 4 * j
            keep = (lane64 >= low) & (lane64 < low + 4)
            head = jnp.where(keep, mats[j][0:64].astype(F32), 0.0).astype(BF16)
            dh2 = dot(head, errors)
            dz2 = (dh2 * slopes2[j]).astype(BF16)
            back = dot(mats[j][64:128, 0:64], dz2, TN)
            dh1s.append(dh2 + back)
            mixed = dot(dz2, h1s[j], NT)
            heads = dot(h2s[j], errors, NT)
            mine = (lane128 // 4) % 2 == j
            firsts.append((mixed, jnp.where(mine, heads, 0.0)))
        dz1 = (jnp.concatenate(dh1s, axis=0) * slope1).astype(BF16)
        lifted = dot(dz1, patches, NT).astype(BF16)
        for j in range(2):
            mixed, heads = firsts[j]
            small = dot(lifted[64 * j : 64 * j + 64], shrink[j])
            upper = (small + heads[0:64]).astype(BF16).astype(F32)
            lower = mixed + heads[64:128]
            lower = jnp.where(lane64 < 64, lower.astype(BF16).astype(F32), lower)
            owner = owners[j]
            both = jnp.concatenate([upper, lower], axis=0)
            grads[owner % 2, owner // 2] = grads[owner % 2, owner // 2] + both
        return carry

    lax.fori_loop(0, CROPS_DEV // 2, one_pair, 0)


def reduce_kernel(
    ns,
    nn,
    grads,
    out,
    pair,
    held,
    parts,
    zparts,
    mine,
    whole,
    pair_send,
    pair_recv,
    rs_send,
    rs_recv,
    z_send,
    z_recv,
    ag_send,
    ag_recv,
):
    s = lax.axis_index("span")
    n = lax.axis_index("normal")
    chips = ns // 2
    chip = s // 2
    core = s % 2
    sibling = chip * 2 + (1 - core)
    rows = 128 // nn
    n_peers = [(n + k) % nn for k in range(1, nn)]
    z_peers = [(chip + k) % chips for k in range(1, chips)]
    barrier = pltpu.get_barrier_semaphore()

    def at_span(other):
        return {"span": other, "normal": n}

    def at_normal(other):
        return {"span": s, "normal": other}

    peers = [at_span(sibling)]
    peers += [at_normal(other) for other in n_peers]
    peers += [at_span(other * 2 + core) for other in z_peers]
    for peer in peers:
        pl.semaphore_signal(barrier, inc=1, device_id=peer, device_id_type=MESH)
    pl.semaphore_wait(barrier, len(peers))

    def remote(src, dst, send, recv, peer):
        copy = pltpu.make_async_remote_copy(
            src_ref=src,
            dst_ref=dst,
            send_sem=send,
            recv_sem=recv,
            device_id=peer,
            device_id_type=MESH,
        )
        copy.start()
        return copy

    first = remote(
        grads.at[1 - core], pair, pair_send.at[0], pair_recv.at[0], at_span(sibling)
    )
    first.wait()
    for z in range(chips):
        held[z] = grads[core, z] + pair[z]
    seconds = []
    for k, other in enumerate(n_peers):
        chunk = pl.ds(pl.multiple_of(other * rows, 8), rows)
        seconds.append(
            remote(
                held.at[:, chunk, :],
                parts.at[k],
                rs_send.at[k],
                rs_recv.at[k],
                at_normal(other),
            )
        )
    own = held[:, pl.ds(pl.multiple_of(n * rows, 8), rows), :]
    for k in range(nn - 1):
        seconds[k].wait()
        own = own + parts[k]
    mine[...] = own
    thirds = []
    for k, other in enumerate(z_peers):
        thirds.append(
            remote(
                mine.at[other],
                zparts.at[k],
                z_send.at[k],
                z_recv.at[k],
                at_span(other * 2 + core),
            )
        )
    total = mine[chip]
    for k in range(chips - 1):
        thirds[k].wait()
        total = total + zparts[k]
    whole[n] = total * (1.0 / (CROPS_DEV * nn))
    fourths = []
    for k, other in enumerate(n_peers):
        fourths.append(
            remote(
                whole.at[n], whole.at[n], ag_send.at[k], ag_recv.at[k], at_normal(other)
            )
        )
    for copy in fourths:
        copy.wait()
    out[...] = whole[...]


def local(
    populations, wall_mask, crop_anchors, trainers, w_lift, b_lift, w_mix, b_mix, w_head, b_head
):
    ns, nn = lax.axis_size("span"), lax.axis_size("normal")
    chips = ns // 2
    vmem = pl.BlockSpec(memory_space=pltpu.VMEM)
    smem = pl.BlockSpec(memory_space=pltpu.SMEM)
    dma = pltpu.SemaphoreType.DMA
    turned = w_head[0].T
    zeros = functools.partial(jnp.zeros, dtype=BF16)
    heads = jnp.concatenate([w_head[0], b_head[0][:, None], zeros((4, 63))], axis=1)
    wb = jnp.concatenate(
        [
            jnp.concatenate(
                [w_lift[0], b_lift[0][:, None], zeros((64, 3)), turned, turned, zeros((64, 8))],
                axis=1,
            ),
            jnp.concatenate([w_mix[0], b_mix[0][:, None], zeros((64, 63))], axis=1),
            heads,
            zeros((8, 128)),
            heads,
        ],
        axis=0,
    )
    final, feat, wall_w = pl.pallas_call(
        functools.partial(lattice_kernel, ns, nn),
        out_shape=(
            jax.ShapeDtypeStruct((19, SX, CZ, CY), F32),
            jax.ShapeDtypeStruct((SX, 9, CZ, CY), BF16),
            jax.ShapeDtypeStruct((ns, 144, 128), BF16),
        ),
        in_specs=[vmem] * 3,
        out_specs=(vmem,) * 3,
        scratch_shapes=[
            pltpu.VMEM((SX, CZ, CY), F32),
            pltpu.VMEM((SX, CZ, CY), F32),
            pltpu.VMEM((20, 2, 8, 128), F32),
            pltpu.VMEM((20, 2, 8, 128), F32),
            pltpu.VMEM((SX, CZ, CY), F32),
            pltpu.VMEM((SX, CZ, CY), F32),
            pltpu.VMEM((20, 2, 8, 128), F32),
            pltpu.VMEM((20, 2, 8, 128), F32),
            pltpu.VMEM((4, SX, 8, 128), F32),
            pltpu.VMEM((ns, 144, 128), BF16),
            pltpu.VMEM((20, SX, EZ, EY), F32),
            pltpu.VMEM((19, SX, EZ, EY), F32),
            dma((8,)),
            dma((8,)),
            dma((chips,)),
            dma((chips,)),
            dma((chips,)),
            dma((chips,)),
        ],
        compiler_params=pltpu.CompilerParams(
            collective_id=0, has_side_effects=True, vmem_limit_bytes=48 << 20
        ),
        name="lattice",
    )(populations, wall_mask, wb)

    grads = pl.pallas_call(
        train_kernel,
        out_shape=jax.ShapeDtypeStruct((2, chips, 128, 128), F32),
        in_specs=[smem, smem] + [vmem] * 7,
        out_specs=vmem,
        compiler_params=pltpu.CompilerParams(vmem_limit_bytes=48 << 20),
        name="train",
    )(crop_anchors, trainers, feat, wall_w, *constants())

    rows = 128 // nn
    total = pl.pallas_call(
        functools.partial(reduce_kernel, ns, nn),
        out_shape=jax.ShapeDtypeStruct((nn, rows, 128), F32),
        in_specs=[vmem],
        out_specs=vmem,
        scratch_shapes=[
            pltpu.VMEM((chips, 128, 128), F32),
            pltpu.VMEM((chips, 128, 128), F32),
            pltpu.VMEM((nn - 1, chips, rows, 128), F32),
            pltpu.VMEM((chips - 1, rows, 128), F32),
            pltpu.VMEM((chips, rows, 128), F32),
            pltpu.VMEM((nn, rows, 128), F32),
            dma((1,)),
            dma((1,)),
            dma((nn - 1,)),
            dma((nn - 1,)),
            dma((chips - 1,)),
            dma((chips - 1,)),
            dma((nn - 1,)),
            dma((nn - 1,)),
        ],
        compiler_params=pltpu.CompilerParams(
            collective_id=1, has_side_effects=True, vmem_limit_bytes=48 << 20
        ),
        name="reduce",
    )(grads)
    total = total.reshape(128, 128)
    heads = total[:65, 112:116] + total[:65, 116:120]
    return (
        final,
        total[None, :64, :108],
        total[None, :64, 108],
        total[None, 64:, :64],
        total[None, 64:, 64],
        heads[:64].T[None],
        heads[64][None],
        jnp.sum(total[64, 120:128])[None],
    )


def solution(mesh):
    return jax.shard_map(
        local,
        mesh=mesh,
        in_specs=(
            P(None, None, "normal", "span"),
            P(None, "normal", "span"),
            P("normal", "span", None, None),
            P("normal", "span", None, None),
            P("span", None, None),
            P("span", None),
            P("span", None, None),
            P("span", None),
            P("span", None, None),
            P("span", None),
        ),
        out_specs=(
            P(None, None, "normal", "span"),
            P("span", None, None),
            P("span", None),
            P("span", None, None),
            P("span", None),
            P("span", None, None),
            P("span", None),
            P("span"),
        ),
        check_vma=False,
    )
```

```python
import functools

import jax
import jax.numpy as jnp
import numpy as np
from jax import lax
from jax.experimental import pallas as pl
from jax.experimental.pallas import tpu as pltpu
from jax.sharding import PartitionSpec as P

STEPS = 4
CROPS_DEV = 12
SX, CZ, CY = 4, 16, 128
EZ, EY = 24, 256
HID = 64
VOX = 512

VELOCITY = (
    (0, 0, 0),
    (1, 0, 0),
    (-1, 0, 0),
    (0, 1, 0),
    (0, -1, 0),
    (0, 0, 1),
    (0, 0, -1),
    (1, 1, 0),
    (-1, -1, 0),
    (1, -1, 0),
    (-1, 1, 0),
    (1, 0, 1),
    (-1, 0, -1),
    (1, 0, -1),
    (-1, 0, 1),
    (0, 1, 1),
    (0, -1, -1),
    (0, 1, -1),
    (0, -1, 1),
)
WEIGHTS = (1.0 / 3.0,) + (1.0 / 18.0,) * 6 + (1.0 / 36.0,) * 12
OPPOSITE = (0, 2, 1, 4, 3, 6, 5, 8, 7, 10, 9, 12, 11, 14, 13, 16, 15, 18, 17)
OMEGA = 1.25
SCALE_DENSITY = 50.0
SCALE_FLOW = 30.0
F32 = jnp.float32
BF16 = jnp.bfloat16
MESH = pl.DeviceIdType.MESH


def signed_sum(entries, factors):
    running = None
    for entry, factor in zip(entries, factors):
        if factor == 0:
            continue
        if running is None:
            running = entry if factor > 0 else -entry
        else:
            running = running + entry if factor > 0 else running - entry
    return running


def moments(states):
    density = states[0]
    for number in range(1, 19):
        density = density + states[number]
    inverse = 1.0 / density
    flows = []
    for axis_id in range(3):
        summed = signed_sum(states, [VELOCITY[number][axis_id] for number in range(19)])
        flows.append(summed * inverse)
    return (density, flows[0], flows[1], flows[2])


def collide(states, wet_cells):
    density, flow_x, flow_y, flow_z = moments(states)
    flows = (flow_x, flow_y, flow_z)
    speed_sq = flow_x * flow_x + flow_y * flow_y + flow_z * flow_z
    base = 1.0 - 1.5 * speed_sq
    result = [None] * 19
    kept = 1.0 - OMEGA
    scaled = {w: (OMEGA * w) * density for w in set(WEIGHTS)}
    relaxed = kept * states[0] + scaled[WEIGHTS[0]] * base
    result[0] = jnp.where(wet_cells, relaxed, states[0])
    for number in range(1, 19, 2):
        other = OPPOSITE[number]
        along = signed_sum(flows, VELOCITY[number])
        weight = scaled[WEIGHTS[number]]
        even = weight * (base + (4.5 * along) * along)
        odd = weight * (3.0 * along)
        forth = kept * states[number] + (even + odd)
        back = kept * states[other] + (even - odd)
        result[number] = jnp.where(wet_cells, forth, states[other])
        result[other] = jnp.where(wet_cells, back, states[number])
    return result


def features(states, fluid):
    density, flow_x, flow_y, flow_z = moments(states)
    return [
        (density - 1.0) * SCALE_DENSITY * fluid,
        flow_x * SCALE_FLOW * fluid,
        flow_y * SCALE_FLOW * fluid,
        flow_z * SCALE_FLOW * fluid,
    ]


NT = (((1,), (1,)), ((), ()))
TN = (((0,), (0,)), ((), ()))


def dot(a, b, dims=(((1,), (0,)), ((), ()))):
    return lax.dot_general(a, b, dims, preferred_element_type=F32)


SHIFTS = [(a, b, c) for a in (-1, 0, 1) for b in (-1, 0, 1) for c in (-1, 0, 1)]


def lattice_kernel(
    ns,
    nn,
    pop_hbm,
    wall_hbm,
    w_lift,
    b_lift,
    w_mix,
    b_mix,
    w_head,
    b_head,
    anchors_hbm,
    spread_hbm,
    select_hbm,
    choose_hbm,
    inside_hbm,
    fin,
    patches,
    targets,
    wets,
    wall_w,
    wall,
    v_lift,
    v_blift,
    v_mix,
    v_bmix,
    v_head,
    v_bhead,
    anchors,
    spread,
    select,
    choose,
    inside,
    wb,
    small,
    early,
    late,
    windows,
    pack_l,
    pack_r,
    pack_u,
    pack_d,
    got_l,
    got_r,
    got_u,
    got_d,
    got_c,
    weights,
    cells,
    post,
    loads,
    halo_send,
    halo_recv,
    ag_send,
    ag_recv,
    fw_send,
    fw_recv,
):
    s = lax.axis_index("span")
    n = lax.axis_index("normal")
    chips = ns // 2
    chip = s // 2
    core = s % 2
    right, left = (s + 1) % ns, (s + ns - 1) % ns
    up, down = (n + 1) % nn, (n + nn - 1) % nn
    sibling = chip * 2 + (1 - core)

    def place(nn_, ss_):
        return {"normal": nn_, "span": ss_}

    fetches = [
        pltpu.make_async_copy(src, dst, loads.at[i])
        for i, (src, dst) in enumerate(
            (
                (pop_hbm, cells.at[0:19, :, 0:CZ, 0:CY]),
                (wall_hbm, wall),
                (w_lift, v_lift),
                (b_lift, v_blift),
                (w_mix, v_mix),
                (b_mix, v_bmix),
                (w_head, v_head),
                (b_head, v_bhead),
                (anchors_hbm, anchors),
                (spread_hbm, spread),
                (select_hbm, select),
                (choose_hbm, choose),
                (inside_hbm, inside),
            )
        )
    ]
    for copy in fetches:
        copy.start()

    peers = [
        place(n, right),
        place(n, left),
        place(up, s),
        place(down, s),
        place(up, right),
        place(up, left),
        place(down, right),
        place(down, left),
        place(n, sibling),
    ]
    z_peers = [((chip + k) % chips) * 2 + core for k in range(1, chips)]
    peers += [place(n, peer) for peer in z_peers]
    barrier = pltpu.get_barrier_semaphore()
    for peer in peers:
        pl.semaphore_signal(barrier, inc=1, device_id=peer, device_id_type=MESH)

    sub = lax.broadcasted_iota(jnp.int32, (8, 128), 0)
    low = sub < 4
    wb[...] = jnp.zeros((144, 128), F32)
    small[...] = jnp.zeros((16, 128), F32)
    fetches[0].wait()
    fetches[1].wait()
    cells[19, :, 0:CZ, 0:CY] = wall[...].astype(F32)

    for k in range(20):
        for j in range(2):
            t0, t1 = cells[k, 2 * j, 0:CZ, 0:CY], cells[k, 2 * j + 1, 0:CZ, 0:CY]
            pack_u[k, j] = jnp.where(low, pltpu.roll(t1[8:16], 4, 0), t0[8:16])
            pack_d[k, j] = jnp.where(low, t0[0:8], pltpu.roll(t1[0:8], 4, 0))
    slot = lax.broadcasted_iota(jnp.int32, (64, 128), 1) // 4
    pl_val = jnp.ones((64, 128), F32)
    pr_val = jnp.ones((64, 128), F32)
    for k in range(20):
        f = cells[k, :, 0:CZ, 0:CY].reshape(64, 128)
        rolled = pltpu.roll(f, 4 * k, 1) if k else f
        pl_val = jnp.where(slot == k, rolled, pl_val)
        pr_val = jnp.where(slot == (k - 1) % 32, rolled, pr_val)
    pack_l[...] = pl_val.reshape(SX, CZ, CY)
    pack_r[...] = pr_val.reshape(SX, CZ, CY)

    for copy in fetches[2:8]:
        copy.wait()
    wb[0:64, 0:108] = v_lift[0].astype(F32)
    wb[64:128, 0:64] = v_mix[0].astype(F32)
    small[0:1, 0:64] = v_blift[...].astype(F32)
    small[1:2, 0:64] = v_bmix[...].astype(F32)
    small[2:3, 0:4] = v_bhead[...].astype(F32)
    small[4:8, 0:64] = v_head[0].astype(F32)
    row16 = lax.broadcasted_iota(jnp.int32, (16, 128), 0)
    lane16 = lax.broadcasted_iota(jnp.int32, (16, 128), 1)
    head_at = (row16 >= 4) & (row16 < 8)
    head_at = head_at & ((lane16 == row16 + 108) | (lane16 == row16 + 112))
    to_top = ((row16 == 0) & (lane16 == 108)) | head_at
    to_mix = (row16 == 1) & (lane16 == 64)
    to_head = (row16 == 2) & (lane16 == 64)
    rows = small[...].astype(BF16)

    def turned(mask):
        return dot(rows, mask.astype(F32).astype(BF16), TN)

    seat = lax.broadcasted_iota(jnp.int32, (16, 128), 1)
    first = row16 % 12
    held = (row16 < 4) | (row16 >= 12)
    picks = (held & (seat == first)).astype(F32).astype(BF16)
    seat4 = lax.broadcasted_iota(jnp.int32, (16, 16), 1)
    row4 = lax.broadcasted_iota(jnp.int32, (16, 16), 0)
    picks4 = (((row4 < 4) | (row4 >= 12)) & (seat4 == row4 % 12 + 4)).astype(F32).astype(BF16)
    wb[0:64] = wb[0:64] + turned(to_top)[0:64]
    wb[64:128] = wb[64:128] + turned(to_mix)[0:64]
    wb[128:144] = dot(picks4, rows) + dot(picks, turned(to_head).astype(BF16))
    mine = wb[...].astype(BF16)
    weights[s] = mine
    wall_w[s] = mine

    pl.semaphore_wait(barrier, len(peers))

    def halo(i, src, dst, peer):
        return pltpu.make_async_remote_copy(
            src_ref=src,
            dst_ref=dst,
            send_sem=halo_send.at[i],
            recv_sem=halo_recv.at[i],
            device_id=peer,
            device_id_type=MESH,
        )

    top, bottom = pl.ds(8, 8), pl.ds(0, 8)
    sends = [
        halo(0, pack_u, got_u, place(up, s)),
        halo(1, pack_d, got_d, place(down, s)),
        halo(2, pack_l, got_l, place(n, left)),
        halo(3, pack_r, got_r, place(n, right)),
        halo(4, pack_l.at[:, bottom, :], got_c.at[0], place(down, left)),
        halo(5, pack_l.at[:, top, :], got_c.at[1], place(up, left)),
        halo(6, pack_r.at[:, bottom, :], got_c.at[2], place(down, right)),
        halo(7, pack_r.at[:, top, :], got_c.at[3], place(up, right)),
    ]
    for copy in sends:
        copy.start()

    gathers = []
    for k, peer in enumerate(z_peers):
        gathers.append(
            pltpu.make_async_remote_copy(
                src_ref=weights.at[s],
                dst_ref=weights.at[s],
                send_sem=ag_send.at[k],
                recv_sem=ag_recv.at[k],
                device_id=place(n, peer),
                device_id_type=MESH,
            )
        )
    for copy in gathers:
        copy.start()

    def forward(i, owner):
        return pltpu.make_async_remote_copy(
            src_ref=weights.at[owner],
            dst_ref=weights.at[owner],
            send_sem=fw_send.at[i],
            recv_sem=fw_recv.at[i],
            device_id=place(n, sibling),
            device_id_type=MESH,
        )

    forwards = [forward(0, s)]
    forwards[0].start()

    fluid = (1 - wall[...]).astype(F32)
    before = features([cells[q, :, 0:CZ, 0:CY] for q in range(19)], fluid)
    for c in range(4):
        early[:, c] = before[c].astype(BF16)
    early[:, 4] = fluid.astype(BF16)
    for copy in fetches[8:]:
        copy.wait()

    ahead = lax.broadcasted_iota(jnp.int32, (128, 256), 0)
    ahead = ahead - lax.broadcasted_iota(jnp.int32, (128, 256), 1) % 16
    unit_row = (lax.broadcasted_iota(jnp.int32, (40, VOX), 0) == 0).astype(F32)

    def cut(field, count, crop, window):
        ox = anchors[0, 0, crop, 0]
        near = field[ox].reshape(count * CZ, 128)
        far = field[(ox + 1) % SX].reshape(count * CZ, 128)
        wide = dot(jnp.concatenate([near, far], axis=0), window)
        return (wide * spread[0 : count * CZ * 2]).astype(BF16)

    def early_pair(i, carry):
        parts = []
        for j in range(2):
            crop = 2 * i + j
            oy = anchors[0, 0, crop, 1] % CY
            window = (ahead == oy).astype(F32).astype(BF16)
            windows[crop] = window
            parts.append(cut(early, 5, crop, window))
        got = dot(select[...], jnp.concatenate(parts, axis=0))
        x8 = jnp.concatenate([got[0:8], got[8:16]], axis=1)
        wets[i] = jnp.concatenate([got[16:24], got[24:32]], axis=1)
        moved = []
        for dx, dz, dy in SHIFTS:
            shift = (-(dx * 256 + dz * 16 + dy)) % VOX
            moved.append(pltpu.roll(x8, shift, 1) if shift else x8)
        moved.append(unit_row)
        patches[i] = jnp.concatenate(moved, axis=0).astype(BF16) * inside[...]
        return carry

    lax.fori_loop(0, CROPS_DEV // 2, early_pair, 0)

    for copy in sends:
        copy.wait()

    low4 = jnp.broadcast_to(low[None], (SX, 8, 128))
    edge_l = jnp.concatenate([got_l[...], jnp.where(low4, got_c[0], got_c[1])], axis=1)
    edge_r = jnp.concatenate([got_r[...], jnp.where(low4, got_c[2], got_c[3])], axis=1)
    edge_l = edge_l.reshape(SX * EZ, 128)
    edge_r = edge_r.reshape(SX * EZ, 128)
    odd = (lax.broadcasted_iota(jnp.int32, (SX * EZ, 128), 1) // 4) % 2 == 1
    mixed = (jnp.where(odd, edge_r, edge_l), jnp.where(odd, edge_l, edge_r))
    for k in range(20):
        side = mixed[k % 2]
        if k:
            side = pltpu.roll(side, 128 - 4 * k, 1)
        cells[k, :, :, CY:EY] = side.reshape(SX, EZ, 128)
        for j in range(2):
            u, d = got_u[k, j], got_d[k, j]
            cells[k, 2 * j, CZ:EZ, 0:CY] = jnp.where(low, d, u)
            cells[k, 2 * j + 1, CZ:EZ, 0:CY] = pltpu.roll(jnp.where(low, u, d), 4, 0)

    def one_step(step, carry):
        def one_chunk(i, inner):
            x = i // 3
            part = pl.ds(pl.multiple_of((i % 3) * 8, 8), 8)
            states = [cells[q, x, part, :] for q in range(19)]
            wet = cells[19, x, part, :] < 0.5
            for q, value in enumerate(collide(states, wet)):
                post[q, x, part, :] = value
            return inner

        lax.fori_loop(0, 12, one_chunk, 0)

        def one_slab(x, inner):
            for q in range(19):
                cx, cy, cz = VELOCITY[q]
                slab = post[q, (x + SX - cx) % SX]
                if cz:
                    slab = pltpu.roll(slab, cz % EZ, 0)
                if cy:
                    slab = pltpu.roll(slab, cy % EY, 1)
                cells[q, x] = slab
            return inner

        lax.fori_loop(0, SX, one_slab, 0)
        return carry

    lax.fori_loop(0, 2, one_step, 0)
    for k in range(1, chips):
        gathers[k - 1].wait()
        owner = ((chip + chips - k) % chips) * 2 + core
        copy = forward(k, owner)
        copy.start()
        forwards.append(copy)
        wall_w[owner] = weights[owner]
    lax.fori_loop(2, STEPS, one_step, 0)

    final = [cells[q, :, 0:CZ, 0:CY] for q in range(19)]
    for q in range(19):
        fin[q] = final[q]
    after = features(final, fluid)
    for c in range(4):
        late[:, c] = (after[c] - before[c]).astype(BF16)

    def late_pair(i, carry):
        parts = [cut(late, 4, 2 * i + j, windows[2 * i + j]) for j in range(2)]
        got = dot(choose[...], jnp.concatenate(parts, axis=0))
        targets[i] = jnp.concatenate([got[0:8], got[8:16]], axis=1)
        return carry

    lax.fori_loop(0, CROPS_DEV // 2, late_pair, 0)
    for copy in forwards:
        copy.wait()
    for k in range(chips):
        owner = ((chip + chips - k) % chips) * 2 + (1 - core)
        wall_w[owner] = weights[owner]


def gelu_both(x):
    c1, c2 = 0.7978845608028654, 0.7978845608028654 * 0.044715
    sq = x * x
    half = 0.5 * jnp.tanh(x * (c1 + c2 * sq)) + 0.5
    value = x * half
    slope = half + value * (1.0 - half) * (2.0 * c1 + 6.0 * c2 * sq)
    return value, slope


def constants():
    row = np.arange(160)
    lane = np.arange(256)
    spread = (lane[None, :] // 16 == row[:, None] % 16).astype(np.float32)
    select = np.zeros((32, 320), np.float32)
    choose = np.zeros((16, 256), np.float32)
    for xi in range(2):
        for i in range(8):
            crop, channel = i // 4, i % 4
            start = crop * 160 + xi * 80 + channel * 16
            select[xi * 8 + i, start : start + 16] = 1.0
            start = crop * 160 + xi * 80 + 64
            select[16 + xi * 8 + i, start : start + 16] = 1.0
            start = crop * 128 + xi * 64 + channel * 16
            choose[xi * 8 + i, start : start + 16] = 1.0
    expand = np.zeros((2, 128, 256), np.float32)
    for pos in range(2):
        for k in range(27):
            for c in range(4):
                expand[pos, 4 * k + c, 8 * k + 4 * pos + c] = 1.0
        expand[pos, 108, 216] = 1.0
    voxel = np.arange(VOX)
    vx, vz, vy = voxel // 256, voxel // 16 % 16, voxel % 16
    inside = np.ones((256, VOX), np.float32)
    for k, (dx, dz, dy) in enumerate(SHIFTS):
        good = (
            (vx + dx >= 0)
            & (vx + dx < 2)
            & (vz + dz >= 0)
            & (vz + dz < 16)
            & (vy + dy >= 0)
            & (vy + dy < 16)
        )
        inside[8 * k : 8 * k + 8] = good[None]
    return (
        (
            jnp.asarray(spread),
            jnp.asarray(select, BF16),
            jnp.asarray(choose, BF16),
            jnp.asarray(inside, BF16),
        ),
        (
            jnp.asarray(expand, BF16),
            jnp.asarray(np.transpose(expand, (0, 2, 1)), BF16),
        ),
    )


def train_kernel(
    ns,
    nn,
    trainers,
    patches_ref,
    targets,
    wets,
    wall_w,
    expand,
    shrink,
    out,
    crops,
    index,
    grads,
    pair,
    held,
    parts,
    zparts,
    mine,
    whole,
    pair_send,
    pair_recv,
    rs_send,
    rs_recv,
    z_send,
    z_recv,
    ag_send,
    ag_recv,
):
    s = lax.axis_index("span")
    n = lax.axis_index("normal")
    chips = ns // 2
    chip = s // 2
    core = s % 2
    sibling = chip * 2 + (1 - core)
    rows = 128 // nn
    n_peers = [(n + k) % nn for k in range(1, nn)]
    z_peers = [(chip + k) % chips for k in range(1, chips)]
    barrier = pltpu.get_barrier_semaphore()

    def at_span(other):
        return {"span": other, "normal": n}

    def at_normal(other):
        return {"span": s, "normal": other}

    peers = [at_span(sibling)]
    peers += [at_normal(other) for other in n_peers]
    peers += [at_span(other * 2 + core) for other in z_peers]
    for peer in peers:
        pl.semaphore_signal(barrier, inc=1, device_id=peer, device_id_type=MESH)

    def remember(m, carry):
        last, before = jnp.int32(CROPS_DEV), jnp.int32(CROPS_DEV)
        for c in range(CROPS_DEV):
            match = trainers[0, 0, c, 0] == m
            before = jnp.where(match, last, before)
            last = jnp.where(match, c, last)
        index[m, 0] = last
        index[m, 1] = before
        return carry

    lax.fori_loop(0, ns, remember, 0)
    crops[CROPS_DEV] = jnp.zeros((128, 128), F32)
    unit = (lax.broadcasted_iota(jnp.int32, (64, VOX), 0) == 0).astype(F32).astype(BF16)
    lane64 = lax.broadcasted_iota(jnp.int32, (64, 128), 1)
    lane128 = lax.broadcasted_iota(jnp.int32, (128, 128), 1)

    def one_pair(i, carry):
        owners = [trainers[0, 0, 2 * i + j, 0] for j in range(2)]
        t8, w8 = targets[i], wets[i]
        patches = patches_ref[i]
        mats = [wall_w[owner] for owner in owners]
        lift = jnp.concatenate(
            [dot(mats[j][0:64], expand[j]) for j in range(2)], axis=0
        ).astype(BF16)
        h1f, slope1 = gelu_both(dot(lift, patches))
        h1 = h1f.astype(BF16)
        slopes2, h1s, h2s, pred = [], [], [], None
        for j in range(2):
            own = h1[64 * j : 64 * j + 64]
            ext = jnp.concatenate([own, unit], axis=0)
            z2 = dot(mats[j][64:128], ext)
            g2, slope2 = gelu_both(z2)
            h2 = (own.astype(F32) + g2).astype(BF16)
            ext2 = jnp.concatenate([h2, unit], axis=0)
            got = dot(mats[j][128:144], ext2)[8 * j : 8 * j + 8]
            pred = got if pred is None else pred + got
            slopes2.append(slope2)
            h1s.append(ext)
            h2s.append(ext2)
        missed = pred - t8
        weighted = w8 * missed
        loss8 = weighted * missed * (1.0 / (4.0 * VOX))
        dpred = weighted * (2.0 / (4.0 * VOX))
        errors = jnp.concatenate([dpred, loss8], axis=0).astype(BF16)
        errors = jnp.concatenate([jnp.zeros((112, VOX), BF16), errors], axis=0)
        dh1s, firsts = [], []
        for j in range(2):
            low = 112 + 4 * j
            keep = (lane64 >= low) & (lane64 < low + 4)
            head = jnp.where(keep, mats[j][0:64].astype(F32), 0.0).astype(BF16)
            dh2 = dot(head, errors)
            dz2 = (dh2 * slopes2[j]).astype(BF16)
            back = dot(mats[j][64:128, 0:64], dz2, TN)
            dh1s.append(dh2 + back)
            mixed = dot(dz2, h1s[j], NT)
            heads = dot(h2s[j], errors, NT)
            own = (lane128 // 4) % 2 == j
            firsts.append((mixed, jnp.where(own, heads, 0.0)))
        dz1 = (jnp.concatenate(dh1s, axis=0) * slope1).astype(BF16)
        lifted = dot(dz1, patches, NT).astype(BF16)
        for j in range(2):
            mixed, heads = firsts[j]
            less = dot(lifted[64 * j : 64 * j + 64], shrink[j])
            upper = (less + heads[0:64]).astype(BF16).astype(F32)
            lower = mixed + heads[64:128]
            lower = jnp.where(lane64 < 64, lower.astype(BF16).astype(F32), lower)
            crops[2 * i + j, 0:64] = upper
            crops[2 * i + j, 64:128] = lower
        return carry

    lax.fori_loop(0, CROPS_DEV // 2, one_pair, 0)

    def member(m):
        return crops[index[m, 0]] + crops[index[m, 1]]

    def theirs(z, carry):
        grads[z] = member(2 * z + 1 - core)
        return carry

    lax.fori_loop(0, chips, theirs, 0)
    pl.semaphore_wait(barrier, len(peers))

    def remote(src, dst, send, recv, peer):
        copy = pltpu.make_async_remote_copy(
            src_ref=src,
            dst_ref=dst,
            send_sem=send,
            recv_sem=recv,
            device_id=peer,
            device_id_type=MESH,
        )
        copy.start()
        return copy

    first = remote(grads, pair, pair_send.at[0], pair_recv.at[0], at_span(sibling))

    def ours(z, carry):
        held[z] = member(2 * z + core)
        return carry

    lax.fori_loop(0, chips, ours, 0)
    first.wait()
    for z in range(chips):
        held[z] = held[z] + pair[z]
    seconds = []
    for k, other in enumerate(n_peers):
        chunk = pl.ds(pl.multiple_of(other * rows, 8), rows)
        seconds.append(
            remote(
                held.at[:, chunk, :],
                parts.at[k],
                rs_send.at[k],
                rs_recv.at[k],
                at_normal(other),
            )
        )
    own = held[:, pl.ds(pl.multiple_of(n * rows, 8), rows), :]
    for k in range(nn - 1):
        seconds[k].wait()
        own = own + parts[k]
    mine[...] = own
    thirds = []
    for k, other in enumerate(z_peers):
        thirds.append(
            remote(
                mine.at[other],
                zparts.at[k],
                z_send.at[k],
                z_recv.at[k],
                at_span(other * 2 + core),
            )
        )
    total = mine[chip]
    for k in range(chips - 1):
        thirds[k].wait()
        total = total + zparts[k]
    whole[n] = total * (1.0 / (CROPS_DEV * nn))
    fourths = []
    for k, other in enumerate(n_peers):
        fourths.append(
            remote(
                whole.at[n], whole.at[n], ag_send.at[k], ag_recv.at[k], at_normal(other)
            )
        )
    for copy in fourths:
        copy.wait()
    out[...] = whole[...]


def unpack_kernel(fin, total, o_fin, o_lift, o_blift, o_mix, o_bmix, o_head, o_bhead, o_loss, sem):
    copy = pltpu.make_async_copy(fin, o_fin, sem)
    copy.start()
    whole = total[...]
    turned = whole.T
    o_lift[0] = whole[0:64, 0:108]
    o_mix[0] = whole[64:128, 0:64]
    o_blift[...] = turned[108:109, 0:64]
    o_bmix[...] = turned[64:65, 64:128]
    heads = turned[112:120, 0:64]
    o_head[0] = heads[0:4] + heads[4:8]
    line = whole[64:65]
    o_bhead[...] = line[:, 112:116] + line[:, 116:120]
    lane = lax.broadcasted_iota(jnp.int32, (1, 128), 1)
    o_loss[...] = jnp.sum(jnp.where(lane >= 120, line, 0.0), axis=1, keepdims=True)
    copy.wait()


def local(
    populations, wall_mask, crop_anchors, trainers, w_lift, b_lift, w_mix, b_mix, w_head, b_head
):
    ns, nn = lax.axis_size("span"), lax.axis_size("normal")
    chips = ns // 2
    pairs = CROPS_DEV // 2
    vmem = pl.BlockSpec(memory_space=pltpu.VMEM)
    smem = pl.BlockSpec(memory_space=pltpu.SMEM)
    hbm = pl.BlockSpec(memory_space=pltpu.HBM)
    dma = pltpu.SemaphoreType.DMA
    shape = jax.ShapeDtypeStruct
    cutting, weighing = constants()
    spread, select, choose, inside = cutting
    edge = pltpu.VMEM((SX, CZ, CY), F32)
    flat = pltpu.VMEM((20, 2, 8, 128), F32)
    final, patches, targets, wets, wall_w = pl.pallas_call(
        functools.partial(lattice_kernel, ns, nn),
        out_shape=(
            shape((19, SX, CZ, CY), F32),
            shape((pairs, 256, VOX), BF16),
            shape((pairs, 8, VOX), F32),
            shape((pairs, 8, VOX), F32),
            shape((ns, 144, 128), BF16),
        ),
        in_specs=[hbm] * 13,
        out_specs=(vmem,) * 5,
        scratch_shapes=[
            pltpu.VMEM((SX, CZ, CY), jnp.int32),
            pltpu.VMEM(w_lift.shape, BF16),
            pltpu.VMEM(b_lift.shape, BF16),
            pltpu.VMEM(w_mix.shape, BF16),
            pltpu.VMEM(b_mix.shape, BF16),
            pltpu.VMEM(w_head.shape, BF16),
            pltpu.VMEM(b_head.shape, BF16),
            pltpu.SMEM(crop_anchors.shape, jnp.int32),
            pltpu.VMEM(spread.shape, F32),
            pltpu.VMEM(select.shape, BF16),
            pltpu.VMEM(choose.shape, BF16),
            pltpu.VMEM(inside.shape, BF16),
            pltpu.VMEM((144, 128), F32),
            pltpu.VMEM((16, 128), F32),
            pltpu.VMEM((SX, 5, CZ, CY), BF16),
            pltpu.VMEM((SX, 4, CZ, CY), BF16),
            pltpu.VMEM((CROPS_DEV, 128, 256), BF16),
            edge,
            edge,
            flat,
            flat,
            edge,
            edge,
            flat,
            flat,
            pltpu.VMEM((4, SX, 8, 128), F32),
            pltpu.VMEM((ns, 144, 128), BF16),
            pltpu.VMEM((20, SX, EZ, EY), F32),
            pltpu.VMEM((19, SX, EZ, EY), F32),
            dma((13,)),
            dma((8,)),
            dma((8,)),
            dma((chips,)),
            dma((chips,)),
            dma((chips,)),
            dma((chips,)),
        ],
        compiler_params=pltpu.CompilerParams(
            collective_id=0, has_side_effects=True, vmem_limit_bytes=32 << 20
        ),
        name="lattice",
    )(
        populations,
        wall_mask,
        w_lift,
        b_lift,
        w_mix,
        b_mix,
        w_head,
        b_head,
        crop_anchors,
        spread,
        select,
        choose,
        inside,
    )

    rows = 128 // nn
    total = pl.pallas_call(
        functools.partial(train_kernel, ns, nn),
        out_shape=shape((nn, rows, 128), F32),
        in_specs=[smem] + [vmem] * 6,
        out_specs=vmem,
        scratch_shapes=[
            pltpu.VMEM((CROPS_DEV + 1, 128, 128), F32),
            pltpu.SMEM((ns, 2), jnp.int32),
            pltpu.VMEM((chips, 128, 128), F32),
            pltpu.VMEM((chips, 128, 128), F32),
            pltpu.VMEM((chips, 128, 128), F32),
            pltpu.VMEM((nn - 1, chips, rows, 128), F32),
            pltpu.VMEM((chips - 1, rows, 128), F32),
            pltpu.VMEM((chips, rows, 128), F32),
            pltpu.VMEM((nn, rows, 128), F32),
            dma((1,)),
            dma((1,)),
            dma((nn - 1,)),
            dma((nn - 1,)),
            dma((chips - 1,)),
            dma((chips - 1,)),
            dma((nn - 1,)),
            dma((nn - 1,)),
        ],
        compiler_params=pltpu.CompilerParams(
            collective_id=1, has_side_effects=True, vmem_limit_bytes=32 << 20
        ),
        name="train",
    )(trainers, patches, targets, wets, wall_w, *weighing)

    outs = pl.pallas_call(
        unpack_kernel,
        out_shape=(
            shape(populations.shape, F32),
            shape(w_lift.shape, F32),
            shape(b_lift.shape, F32),
            shape(w_mix.shape, F32),
            shape(b_mix.shape, F32),
            shape(w_head.shape, F32),
            shape(b_head.shape, F32),
            shape((1, 1), F32),
        ),
        in_specs=[pl.BlockSpec(memory_space=pl.ANY), vmem],
        out_specs=(hbm,) + (vmem,) * 7,
        scratch_shapes=[pltpu.SemaphoreType.DMA],
        name="unpack",
    )(final, total.reshape(128, 128))
    return outs[:7] + (outs[7].reshape(1),)


def solution(mesh):
    return jax.shard_map(
        local,
        mesh=mesh,
        in_specs=(
            P(None, None, "normal", "span"),
            P(None, "normal", "span"),
            P("normal", "span", None, None),
            P("normal", "span", None, None),
            P("span", None, None),
            P("span", None),
            P("span", None, None),
            P("span", None),
            P("span", None, None),
            P("span", None),
        ),
        out_specs=(
            P(None, None, "normal", "span"),
            P("span", None, None),
            P("span", None),
            P("span", None, None),
            P("span", None),
            P("span", None, None),
            P("span", None),
            P("span"),
        ),
        check_vma=False,
    )
```

```python
import functools

import jax
import jax.numpy as jnp
import numpy as np
from jax import lax
from jax.experimental import pallas as pl
from jax.experimental.pallas import tpu as pltpu
from jax.sharding import PartitionSpec as P

STEPS = 4
CROPS_DEV = 12
SX, CZ, CY = 4, 16, 128
EZ, EY = 24, 256
HID = 64
VOX = 512

VELOCITY = (
    (0, 0, 0),
    (1, 0, 0),
    (-1, 0, 0),
    (0, 1, 0),
    (0, -1, 0),
    (0, 0, 1),
    (0, 0, -1),
    (1, 1, 0),
    (-1, -1, 0),
    (1, -1, 0),
    (-1, 1, 0),
    (1, 0, 1),
    (-1, 0, -1),
    (1, 0, -1),
    (-1, 0, 1),
    (0, 1, 1),
    (0, -1, -1),
    (0, 1, -1),
    (0, -1, 1),
)
WEIGHTS = (1.0 / 3.0,) + (1.0 / 18.0,) * 6 + (1.0 / 36.0,) * 12
OPPOSITE = (0, 2, 1, 4, 3, 6, 5, 8, 7, 10, 9, 12, 11, 14, 13, 16, 15, 18, 17)
OMEGA = 1.25
SCALE_DENSITY = 50.0
SCALE_FLOW = 30.0
F32 = jnp.float32
BF16 = jnp.bfloat16
MESH = pl.DeviceIdType.MESH


def signed_sum(entries, factors):
    running = None
    for entry, factor in zip(entries, factors):
        if factor == 0:
            continue
        if running is None:
            running = entry if factor > 0 else -entry
        else:
            running = running + entry if factor > 0 else running - entry
    return running


def moments(states):
    density = states[0]
    for number in range(1, 19):
        density = density + states[number]
    inverse = 1.0 / density
    flows = []
    for axis_id in range(3):
        summed = signed_sum(states, [VELOCITY[number][axis_id] for number in range(19)])
        flows.append(summed * inverse)
    return (density, flows[0], flows[1], flows[2])


def collide(states, wet_cells):
    density, flow_x, flow_y, flow_z = moments(states)
    flows = (flow_x, flow_y, flow_z)
    speed_sq = flow_x * flow_x + flow_y * flow_y + flow_z * flow_z
    base = 1.0 - 1.5 * speed_sq
    result = [None] * 19
    kept = 1.0 - OMEGA
    scaled = {w: (OMEGA * w) * density for w in set(WEIGHTS)}
    relaxed = kept * states[0] + scaled[WEIGHTS[0]] * base
    result[0] = jnp.where(wet_cells, relaxed, states[0])
    for number in range(1, 19, 2):
        other = OPPOSITE[number]
        along = signed_sum(flows, VELOCITY[number])
        weight = scaled[WEIGHTS[number]]
        even = weight * (base + (4.5 * along) * along)
        odd = weight * (3.0 * along)
        forth = kept * states[number] + (even + odd)
        back = kept * states[other] + (even - odd)
        result[number] = jnp.where(wet_cells, forth, states[other])
        result[other] = jnp.where(wet_cells, back, states[number])
    return result


def features(states, fluid):
    density, flow_x, flow_y, flow_z = moments(states)
    return [
        (density - 1.0) * SCALE_DENSITY * fluid,
        flow_x * SCALE_FLOW * fluid,
        flow_y * SCALE_FLOW * fluid,
        flow_z * SCALE_FLOW * fluid,
    ]


NT = (((1,), (1,)), ((), ()))
TN = (((0,), (0,)), ((), ()))


def dot(a, b, dims=(((1,), (0,)), ((), ()))):
    return lax.dot_general(a, b, dims, preferred_element_type=F32)


SHIFTS = [(a, b, c) for a in (-1, 0, 1) for b in (-1, 0, 1) for c in (-1, 0, 1)]


def lattice_part(
    ns,
    nn,
    pop_hbm,
    wall_hbm,
    w_lift,
    b_lift,
    w_mix,
    b_mix,
    w_head,
    b_head,
    anchors_hbm,
    spread_hbm,
    select_hbm,
    choose_hbm,
    inside_hbm,
    more_fetches,
    n_peers,
    fin,
    fin_sem,
    patches,
    targets,
    wets,
    wall,
    v_lift,
    v_blift,
    v_mix,
    v_bmix,
    v_head,
    v_bhead,
    anchors,
    spread,
    select,
    choose,
    inside,
    wb,
    small,
    early,
    late,
    windows,
    pack_l,
    pack_r,
    pack_u,
    pack_d,
    got_l,
    got_r,
    got_u,
    got_d,
    got_c,
    weights,
    cells,
    post,
    loads,
    halo_send,
    halo_recv,
    ag_send,
    ag_recv,
    fw_send,
    fw_recv,
):
    s = lax.axis_index("span")
    n = lax.axis_index("normal")
    chips = ns // 2
    chip = s // 2
    core = s % 2
    right, left = (s + 1) % ns, (s + ns - 1) % ns
    up, down = (n + 1) % nn, (n + nn - 1) % nn
    sibling = chip * 2 + (1 - core)

    def place(nn_, ss_):
        return {"normal": nn_, "span": ss_}

    fetches = [
        pltpu.make_async_copy(src, dst, loads.at[i])
        for i, (src, dst) in enumerate(
            (
                (pop_hbm, cells.at[0:19, :, 0:CZ, 0:CY]),
                (wall_hbm, wall),
                (w_lift, v_lift),
                (b_lift, v_blift),
                (w_mix, v_mix),
                (b_mix, v_bmix),
                (w_head, v_head),
                (b_head, v_bhead),
                (anchors_hbm, anchors),
                (spread_hbm, spread),
                (select_hbm, select),
                (choose_hbm, choose),
                (inside_hbm, inside),
                *more_fetches,
            )
        )
    ]
    for copy in fetches:
        copy.start()

    peers = [
        place(n, right),
        place(n, left),
        place(up, right),
        place(up, left),
        place(down, right),
        place(down, left),
        place(n, sibling),
    ]
    z_peers = [((chip + k) % chips) * 2 + core for k in range(1, chips)]
    peers += [place(n, peer) for peer in z_peers]
    peers += [place(other, s) for other in n_peers]
    barrier = pltpu.get_barrier_semaphore()
    for peer in peers:
        pl.semaphore_signal(barrier, inc=1, device_id=peer, device_id_type=MESH)

    sub = lax.broadcasted_iota(jnp.int32, (8, 128), 0)
    low = sub < 4
    wb[...] = jnp.zeros((144, 128), F32)
    small[...] = jnp.zeros((16, 128), F32)
    fetches[0].wait()
    fetches[1].wait()
    cells[19, :, 0:CZ, 0:CY] = wall[...].astype(F32)

    for k in range(20):
        for j in range(2):
            t0, t1 = cells[k, 2 * j, 0:CZ, 0:CY], cells[k, 2 * j + 1, 0:CZ, 0:CY]
            pack_u[k, j] = jnp.where(low, pltpu.roll(t1[8:16], 4, 0), t0[8:16])
            pack_d[k, j] = jnp.where(low, t0[0:8], pltpu.roll(t1[0:8], 4, 0))
    slot = lax.broadcasted_iota(jnp.int32, (64, 128), 1) // 4
    pl_val = jnp.ones((64, 128), F32)
    pr_val = jnp.ones((64, 128), F32)
    for k in range(20):
        f = cells[k, :, 0:CZ, 0:CY].reshape(64, 128)
        rolled = pltpu.roll(f, 4 * k, 1) if k else f
        pl_val = jnp.where(slot == k, rolled, pl_val)
        pr_val = jnp.where(slot == (k - 1) % 32, rolled, pr_val)
    pack_l[...] = pl_val.reshape(SX, CZ, CY)
    pack_r[...] = pr_val.reshape(SX, CZ, CY)

    for copy in fetches[2:8]:
        copy.wait()
    wb[0:64, 0:108] = v_lift[0].astype(F32)
    wb[64:128, 0:64] = v_mix[0].astype(F32)
    small[0:1, 0:64] = v_blift[...].astype(F32)
    small[1:2, 0:64] = v_bmix[...].astype(F32)
    small[2:3, 0:4] = v_bhead[...].astype(F32)
    small[4:8, 0:64] = v_head[0].astype(F32)
    row16 = lax.broadcasted_iota(jnp.int32, (16, 128), 0)
    lane16 = lax.broadcasted_iota(jnp.int32, (16, 128), 1)
    head_at = (row16 >= 4) & (row16 < 8)
    head_at = head_at & ((lane16 == row16 + 108) | (lane16 == row16 + 112))
    to_top = ((row16 == 0) & (lane16 == 108)) | head_at
    to_mix = (row16 == 1) & (lane16 == 64)
    to_head = (row16 == 2) & (lane16 == 64)
    rows = small[...].astype(BF16)

    def turned(mask):
        return dot(rows, mask.astype(F32).astype(BF16), TN)

    seat = lax.broadcasted_iota(jnp.int32, (16, 128), 1)
    first = row16 % 12
    held = (row16 < 4) | (row16 >= 12)
    picks = (held & (seat == first)).astype(F32).astype(BF16)
    seat4 = lax.broadcasted_iota(jnp.int32, (16, 16), 1)
    row4 = lax.broadcasted_iota(jnp.int32, (16, 16), 0)
    picks4 = (((row4 < 4) | (row4 >= 12)) & (seat4 == row4 % 12 + 4)).astype(F32).astype(BF16)
    wb[0:64] = wb[0:64] + turned(to_top)[0:64]
    wb[64:128] = wb[64:128] + turned(to_mix)[0:64]
    wb[128:144] = dot(picks4, rows) + dot(picks, turned(to_head).astype(BF16))
    mine = wb[...].astype(BF16)
    weights[s] = mine

    pl.semaphore_wait(barrier, len(peers))

    def halo(i, src, dst, peer):
        return pltpu.make_async_remote_copy(
            src_ref=src,
            dst_ref=dst,
            send_sem=halo_send.at[i],
            recv_sem=halo_recv.at[i],
            device_id=peer,
            device_id_type=MESH,
        )

    top, bottom = pl.ds(8, 8), pl.ds(0, 8)
    sends = [
        halo(0, pack_u, got_u, place(up, s)),
        halo(1, pack_d, got_d, place(down, s)),
        halo(2, pack_l, got_l, place(n, left)),
        halo(3, pack_r, got_r, place(n, right)),
        halo(4, pack_l.at[:, bottom, :], got_c.at[0], place(down, left)),
        halo(5, pack_l.at[:, top, :], got_c.at[1], place(up, left)),
        halo(6, pack_r.at[:, bottom, :], got_c.at[2], place(down, right)),
        halo(7, pack_r.at[:, top, :], got_c.at[3], place(up, right)),
    ]
    for copy in sends:
        copy.start()

    gathers = []
    for k, peer in enumerate(z_peers):
        gathers.append(
            pltpu.make_async_remote_copy(
                src_ref=weights.at[s],
                dst_ref=weights.at[s],
                send_sem=ag_send.at[k],
                recv_sem=ag_recv.at[k],
                device_id=place(n, peer),
                device_id_type=MESH,
            )
        )
    for copy in gathers:
        copy.start()

    def forward(i, owner):
        return pltpu.make_async_remote_copy(
            src_ref=weights.at[owner],
            dst_ref=weights.at[owner],
            send_sem=fw_send.at[i],
            recv_sem=fw_recv.at[i],
            device_id=place(n, sibling),
            device_id_type=MESH,
        )

    forwards = [forward(0, s)]
    forwards[0].start()

    fluid = (1 - wall[...]).astype(F32)
    before = features([cells[q, :, 0:CZ, 0:CY] for q in range(19)], fluid)
    for c in range(4):
        early[:, c] = before[c].astype(BF16)
    early[:, 4] = fluid.astype(BF16)
    for copy in fetches[8:]:
        copy.wait()

    ahead = lax.broadcasted_iota(jnp.int32, (128, 256), 0)
    ahead = ahead - lax.broadcasted_iota(jnp.int32, (128, 256), 1) % 16
    unit_row = (lax.broadcasted_iota(jnp.int32, (40, VOX), 0) == 0).astype(F32)

    def cut(field, count, crop, window):
        ox = anchors[0, 0, 0, crop]
        near = field[ox].reshape(count * CZ, 128)
        far = field[(ox + 1) % SX].reshape(count * CZ, 128)
        wide = dot(jnp.concatenate([near, far], axis=0), window)
        return (wide * spread[0 : count * CZ * 2]).astype(BF16)

    def early_pair(i, carry):
        parts = []
        for j in range(2):
            crop = 2 * i + j
            oy = anchors[0, 0, 1, crop] % CY
            window = (ahead == oy).astype(F32).astype(BF16)
            windows[crop] = window
            parts.append(cut(early, 5, crop, window))
        got = dot(select[...], jnp.concatenate(parts, axis=0))
        x8 = jnp.concatenate([got[0:8], got[8:16]], axis=1)
        wets[i] = jnp.concatenate([got[16:24], got[24:32]], axis=1)
        moved = []
        for dx, dz, dy in SHIFTS:
            shift = (-(dx * 256 + dz * 16 + dy)) % VOX
            moved.append(pltpu.roll(x8, shift, 1) if shift else x8)
        moved.append(unit_row)
        patches[i] = jnp.concatenate(moved, axis=0).astype(BF16) * inside[...]
        return carry

    lax.fori_loop(0, CROPS_DEV // 2, early_pair, 0)

    for copy in sends:
        copy.wait()

    low4 = jnp.broadcast_to(low[None], (SX, 8, 128))
    edge_l = jnp.concatenate([got_l[...], jnp.where(low4, got_c[0], got_c[1])], axis=1)
    edge_r = jnp.concatenate([got_r[...], jnp.where(low4, got_c[2], got_c[3])], axis=1)
    edge_l = edge_l.reshape(SX * EZ, 128)
    edge_r = edge_r.reshape(SX * EZ, 128)
    odd = (lax.broadcasted_iota(jnp.int32, (SX * EZ, 128), 1) // 4) % 2 == 1
    mixed = (jnp.where(odd, edge_r, edge_l), jnp.where(odd, edge_l, edge_r))
    for k in range(20):
        side = mixed[k % 2]
        if k:
            side = pltpu.roll(side, 128 - 4 * k, 1)
        cells[k, :, :, CY:EY] = side.reshape(SX, EZ, 128)
        for j in range(2):
            u, d = got_u[k, j], got_d[k, j]
            cells[k, 2 * j, CZ:EZ, 0:CY] = jnp.where(low, d, u)
            cells[k, 2 * j + 1, CZ:EZ, 0:CY] = pltpu.roll(jnp.where(low, u, d), 4, 0)

    def one_step(step, carry):
        def one_chunk(i, inner):
            x = i // 3
            part = pl.ds(pl.multiple_of((i % 3) * 8, 8), 8)
            states = [cells[q, x, part, :] for q in range(19)]
            wet = cells[19, x, part, :] < 0.5
            for q, value in enumerate(collide(states, wet)):
                post[q, x, part, :] = value
            return inner

        lax.fori_loop(0, 12, one_chunk, 0)

        def one_slab(x, inner):
            for q in range(19):
                cx, cy, cz = VELOCITY[q]
                slab = post[q, (x + SX - cx) % SX]
                if cz:
                    slab = pltpu.roll(slab, cz % EZ, 0)
                if cy:
                    slab = pltpu.roll(slab, cy % EY, 1)
                cells[q, x] = slab
            return inner

        lax.fori_loop(0, SX, one_slab, 0)
        return carry

    lax.fori_loop(0, 2, one_step, 0)
    for k in range(1, chips):
        gathers[k - 1].wait()
        owner = ((chip + chips - k) % chips) * 2 + core
        copy = forward(k, owner)
        copy.start()
        forwards.append(copy)
    lax.fori_loop(2, STEPS, one_step, 0)

    store = pltpu.make_async_copy(cells.at[0:19, :, 0:CZ, 0:CY], fin, fin_sem)
    store.start()
    final = [cells[q, :, 0:CZ, 0:CY] for q in range(19)]
    after = features(final, fluid)
    for c in range(4):
        late[:, c] = (after[c] - before[c]).astype(BF16)

    def late_pair(i, carry):
        parts = [cut(late, 4, 2 * i + j, windows[2 * i + j]) for j in range(2)]
        got = dot(choose[...], jnp.concatenate(parts, axis=0))
        targets[i] = jnp.concatenate([got[0:8], got[8:16]], axis=1)
        return carry

    lax.fori_loop(0, CROPS_DEV // 2, late_pair, 0)
    for copy in forwards:
        copy.wait()
    return store


def gelu_both(x):
    c1, c2 = 0.7978845608028654, 0.7978845608028654 * 0.044715
    sq = x * x
    half = 0.5 * jnp.tanh(x * (c1 + c2 * sq)) + 0.5
    value = x * half
    slope = half + value * (1.0 - half) * (2.0 * c1 + 6.0 * c2 * sq)
    return value, slope


def constants():
    row = np.arange(160)
    lane = np.arange(256)
    spread = (lane[None, :] // 16 == row[:, None] % 16).astype(np.float32)
    select = np.zeros((32, 320), np.float32)
    choose = np.zeros((16, 256), np.float32)
    for xi in range(2):
        for i in range(8):
            crop, channel = i // 4, i % 4
            start = crop * 160 + xi * 80 + channel * 16
            select[xi * 8 + i, start : start + 16] = 1.0
            start = crop * 160 + xi * 80 + 64
            select[16 + xi * 8 + i, start : start + 16] = 1.0
            start = crop * 128 + xi * 64 + channel * 16
            choose[xi * 8 + i, start : start + 16] = 1.0
    expand = np.zeros((2, 128, 256), np.float32)
    for pos in range(2):
        for k in range(27):
            for c in range(4):
                expand[pos, 4 * k + c, 8 * k + 4 * pos + c] = 1.0
        expand[pos, 108, 216] = 1.0
    voxel = np.arange(VOX)
    vx, vz, vy = voxel // 256, voxel // 16 % 16, voxel % 16
    inside = np.ones((256, VOX), np.float32)
    for k, (dx, dz, dy) in enumerate(SHIFTS):
        good = (
            (vx + dx >= 0)
            & (vx + dx < 2)
            & (vz + dz >= 0)
            & (vz + dz < 16)
            & (vy + dy >= 0)
            & (vy + dy < 16)
        )
        inside[8 * k : 8 * k + 8] = good[None]
    return (
        (
            jnp.asarray(spread),
            jnp.asarray(select, BF16),
            jnp.asarray(choose, BF16),
            jnp.asarray(inside, BF16),
        ),
        (
            jnp.asarray(expand, BF16),
            jnp.asarray(np.transpose(expand, (0, 2, 1)), BF16),
        ),
    )


def train_part(
    ns,
    nn,
    trainers,
    patches_ref,
    targets,
    wets,
    wall_w,
    expand,
    shrink,
    out,
    crops,
    index,
    grads,
    pair,
    held,
    parts,
    zparts,
    mine,
    whole,
    pair_send,
    pair_recv,
    rs_send,
    rs_recv,
    z_send,
    z_recv,
    ag_send,
    ag_recv,
):
    s = lax.axis_index("span")
    n = lax.axis_index("normal")
    chips = ns // 2
    chip = s // 2
    core = s % 2
    sibling = chip * 2 + (1 - core)
    rows = 128 // nn
    n_peers = [(n + k) % nn for k in range(1, nn)]
    z_peers = [(chip + k) % chips for k in range(1, chips)]

    def at_span(other):
        return {"span": other, "normal": n}

    def at_normal(other):
        return {"span": s, "normal": other}

    def remember(m, carry):
        last, before = jnp.int32(CROPS_DEV), jnp.int32(CROPS_DEV)
        for c in range(CROPS_DEV):
            match = trainers[0, 0, 0, c] == m
            before = jnp.where(match, last, before)
            last = jnp.where(match, c, last)
        index[m, 0] = last
        index[m, 1] = before
        return carry

    lax.fori_loop(0, ns, remember, 0)
    crops[CROPS_DEV] = jnp.zeros((128, 128), F32)
    unit = (lax.broadcasted_iota(jnp.int32, (64, VOX), 0) == 0).astype(F32).astype(BF16)
    lane64 = lax.broadcasted_iota(jnp.int32, (64, 128), 1)
    lane128 = lax.broadcasted_iota(jnp.int32, (128, 128), 1)

    def one_pair(i, carry):
        owners = [trainers[0, 0, 0, 2 * i + j] for j in range(2)]
        t8, w8 = targets[i], wets[i]
        patches = patches_ref[i]
        mats = [wall_w[owner] for owner in owners]
        lift = jnp.concatenate(
            [dot(mats[j][0:64], expand[j]) for j in range(2)], axis=0
        ).astype(BF16)
        h1f, slope1 = gelu_both(dot(lift, patches))
        h1 = h1f.astype(BF16)
        slopes2, h1s, h2s, pred = [], [], [], None
        for j in range(2):
            own = h1[64 * j : 64 * j + 64]
            ext = jnp.concatenate([own, unit], axis=0)
            z2 = dot(mats[j][64:128], ext)
            g2, slope2 = gelu_both(z2)
            h2 = (own.astype(F32) + g2).astype(BF16)
            ext2 = jnp.concatenate([h2, unit], axis=0)
            got = dot(mats[j][128:144], ext2)[8 * j : 8 * j + 8]
            pred = got if pred is None else pred + got
            slopes2.append(slope2)
            h1s.append(ext)
            h2s.append(ext2)
        missed = pred - t8
        weighted = w8 * missed
        loss8 = weighted * missed * (1.0 / (4.0 * VOX))
        dpred = weighted * (2.0 / (4.0 * VOX))
        errors = jnp.concatenate([dpred, loss8], axis=0).astype(BF16)
        errors = jnp.concatenate([jnp.zeros((112, VOX), BF16), errors], axis=0)
        dh1s, firsts = [], []
        for j in range(2):
            low = 112 + 4 * j
            keep = (lane64 >= low) & (lane64 < low + 4)
            head = jnp.where(keep, mats[j][0:64].astype(F32), 0.0).astype(BF16)
            dh2 = dot(head, errors)
            dz2 = (dh2 * slopes2[j]).astype(BF16)
            back = dot(mats[j][64:128, 0:64], dz2, TN)
            dh1s.append(dh2 + back)
            mixed = dot(dz2, h1s[j], NT)
            heads = dot(h2s[j], errors, NT)
            own = (lane128 // 4) % 2 == j
            firsts.append((mixed, jnp.where(own, heads, 0.0)))
        dz1 = (jnp.concatenate(dh1s, axis=0) * slope1).astype(BF16)
        lifted = dot(dz1, patches, NT).astype(BF16)
        for j in range(2):
            mixed, heads = firsts[j]
            less = dot(lifted[64 * j : 64 * j + 64], shrink[j])
            upper = (less + heads[0:64]).astype(BF16).astype(F32)
            lower = mixed + heads[64:128]
            lower = jnp.where(lane64 < 64, lower.astype(BF16).astype(F32), lower)
            crops[2 * i + j, 0:64] = upper
            crops[2 * i + j, 64:128] = lower
        return carry

    lax.fori_loop(0, CROPS_DEV // 2, one_pair, 0)

    def member(m):
        return crops[index[m, 0]] + crops[index[m, 1]]

    def theirs(z, carry):
        grads[z] = member(2 * z + 1 - core)
        return carry

    lax.fori_loop(0, chips, theirs, 0)
    def remote(src, dst, send, recv, peer):
        copy = pltpu.make_async_remote_copy(
            src_ref=src,
            dst_ref=dst,
            send_sem=send,
            recv_sem=recv,
            device_id=peer,
            device_id_type=MESH,
        )
        copy.start()
        return copy

    first = remote(grads, pair, pair_send.at[0], pair_recv.at[0], at_span(sibling))

    def ours(z, carry):
        held[z] = member(2 * z + core)
        return carry

    lax.fori_loop(0, chips, ours, 0)
    first.wait()
    for z in range(chips):
        held[z] = held[z] + pair[z]
    seconds = []
    for k, other in enumerate(n_peers):
        chunk = pl.ds(pl.multiple_of(other * rows, 8), rows)
        seconds.append(
            remote(
                held.at[:, chunk, :],
                parts.at[k],
                rs_send.at[k],
                rs_recv.at[k],
                at_normal(other),
            )
        )
    own = held[:, pl.ds(pl.multiple_of(n * rows, 8), rows), :]
    for k in range(nn - 1):
        seconds[k].wait()
        own = own + parts[k]
    mine[...] = own
    thirds = []
    for k, other in enumerate(z_peers):
        thirds.append(
            remote(
                mine.at[other],
                zparts.at[k],
                z_send.at[k],
                z_recv.at[k],
                at_span(other * 2 + core),
            )
        )
    total = mine[chip]
    for k in range(chips - 1):
        thirds[k].wait()
        total = total + zparts[k]
    whole[n] = total * (1.0 / (CROPS_DEV * nn))
    fourths = []
    for k, other in enumerate(n_peers):
        fourths.append(
            remote(
                whole.at[n], whole.at[n], ag_send.at[k], ag_recv.at[k], at_normal(other)
            )
        )
    for copy in fourths:
        copy.wait()
    out[...] = whole[...]


def fused_kernel(ns, nn, *refs):
    (
        pop,
        wall,
        w_lift,
        b_lift,
        w_mix,
        b_mix,
        w_head,
        b_head,
        anchors,
        trainers,
        spread,
        select,
        choose,
        inside,
        expand,
        shrink,
        fin,
        total,
    ) = refs[:18]
    fin_sem, v_trainers, v_expand, v_shrink, patches, targets, wets, weights = refs[18:26]
    lattice_refs, train_refs = refs[26:61], refs[61:]
    n = lax.axis_index("normal")
    n_peers = [(n + k) % nn for k in range(1, nn)]
    store = lattice_part(
        ns,
        nn,
        pop,
        wall,
        w_lift,
        b_lift,
        w_mix,
        b_mix,
        w_head,
        b_head,
        anchors,
        spread,
        select,
        choose,
        inside,
        ((trainers, v_trainers), (expand, v_expand), (shrink, v_shrink)),
        n_peers,
        fin,
        fin_sem,
        patches,
        targets,
        wets,
        *lattice_refs[:26],
        weights,
        *lattice_refs[26:],
    )
    train_part(
        ns,
        nn,
        v_trainers,
        patches,
        targets,
        wets,
        weights,
        v_expand,
        v_shrink,
        total,
        *train_refs,
    )
    store.wait()


def unpack_kernel(total, o_lift, o_blift, o_mix, o_bmix, o_head, o_bhead, o_loss):
    whole = total[...]
    turned = whole.T
    o_lift[0] = whole[0:64, 0:108]
    o_mix[0] = whole[64:128, 0:64]
    o_blift[...] = turned[108:109, 0:64]
    o_bmix[...] = turned[64:65, 64:128]
    heads = turned[112:120, 0:64]
    o_head[0] = heads[0:4] + heads[4:8]
    line = whole[64:65]
    o_bhead[...] = line[:, 112:116] + line[:, 116:120]
    lane = lax.broadcasted_iota(jnp.int32, (1, 128), 1)
    o_loss[...] = jnp.sum(jnp.where(lane >= 120, line, 0.0), axis=1, keepdims=True)


def local(
    populations, wall_mask, crop_anchors, trainers, w_lift, b_lift, w_mix, b_mix, w_head, b_head
):
    ns, nn = lax.axis_size("span"), lax.axis_size("normal")
    chips = ns // 2
    pairs = CROPS_DEV // 2
    vmem = pl.BlockSpec(memory_space=pltpu.VMEM)
    hbm = pl.BlockSpec(memory_space=pltpu.HBM)
    dma = pltpu.SemaphoreType.DMA
    shape = jax.ShapeDtypeStruct
    cutting, weighing = constants()
    spread, select, choose, inside = cutting
    edge = pltpu.VMEM((SX, CZ, CY), F32)
    flat = pltpu.VMEM((20, 2, 8, 128), F32)
    rows = 128 // nn
    final, total = pl.pallas_call(
        functools.partial(fused_kernel, ns, nn),
        out_shape=(shape((19, SX, CZ, CY), F32), shape((nn, rows, 128), F32)),
        in_specs=[hbm] * 16,
        out_specs=(hbm, vmem),
        scratch_shapes=[
            dma,
            pltpu.SMEM((1, 1, 1, CROPS_DEV), jnp.int32),
            pltpu.VMEM((2, 128, 256), BF16),
            pltpu.VMEM((2, 256, 128), BF16),
            pltpu.VMEM((pairs, 256, VOX), BF16),
            pltpu.VMEM((pairs, 8, VOX), F32),
            pltpu.VMEM((pairs, 8, VOX), F32),
            pltpu.VMEM((ns, 144, 128), BF16),
            pltpu.VMEM((SX, CZ, CY), jnp.int32),
            pltpu.VMEM(w_lift.shape, BF16),
            pltpu.VMEM(b_lift.shape, BF16),
            pltpu.VMEM(w_mix.shape, BF16),
            pltpu.VMEM(b_mix.shape, BF16),
            pltpu.VMEM(w_head.shape, BF16),
            pltpu.VMEM(b_head.shape, BF16),
            pltpu.SMEM((1, 1, 3, CROPS_DEV), jnp.int32),
            pltpu.VMEM(spread.shape, F32),
            pltpu.VMEM(select.shape, BF16),
            pltpu.VMEM(choose.shape, BF16),
            pltpu.VMEM(inside.shape, BF16),
            pltpu.VMEM((144, 128), F32),
            pltpu.VMEM((16, 128), F32),
            pltpu.VMEM((SX, 5, CZ, CY), BF16),
            pltpu.VMEM((SX, 4, CZ, CY), BF16),
            pltpu.VMEM((CROPS_DEV, 128, 256), BF16),
            edge,
            edge,
            flat,
            flat,
            edge,
            edge,
            flat,
            flat,
            pltpu.VMEM((4, SX, 8, 128), F32),
            pltpu.VMEM((20, SX, EZ, EY), F32),
            pltpu.VMEM((19, SX, EZ, EY), F32),
            dma((16,)),
            dma((8,)),
            dma((8,)),
            dma((chips,)),
            dma((chips,)),
            dma((chips,)),
            dma((chips,)),
            pltpu.VMEM((CROPS_DEV + 1, 128, 128), F32),
            pltpu.SMEM((ns, 2), jnp.int32),
            pltpu.VMEM((chips, 128, 128), F32),
            pltpu.VMEM((chips, 128, 128), F32),
            pltpu.VMEM((chips, 128, 128), F32),
            pltpu.VMEM((nn - 1, chips, rows, 128), F32),
            pltpu.VMEM((chips - 1, rows, 128), F32),
            pltpu.VMEM((chips, rows, 128), F32),
            pltpu.VMEM((nn, rows, 128), F32),
            dma((1,)),
            dma((1,)),
            dma((nn - 1,)),
            dma((nn - 1,)),
            dma((chips - 1,)),
            dma((chips - 1,)),
            dma((nn - 1,)),
            dma((nn - 1,)),
        ],
        compiler_params=pltpu.CompilerParams(
            collective_id=0, has_side_effects=True, vmem_limit_bytes=60 << 20
        ),
        name="channel",
    )(
        populations,
        wall_mask,
        w_lift,
        b_lift,
        w_mix,
        b_mix,
        w_head,
        b_head,
        jnp.swapaxes(crop_anchors, 2, 3),
        jnp.swapaxes(trainers, 2, 3),
        spread,
        select,
        choose,
        inside,
        *weighing,
    )
    outs = pl.pallas_call(
        unpack_kernel,
        out_shape=(
            shape(w_lift.shape, F32),
            shape(b_lift.shape, F32),
            shape(w_mix.shape, F32),
            shape(b_mix.shape, F32),
            shape(w_head.shape, F32),
            shape(b_head.shape, F32),
            shape((1, 1), F32),
        ),
        in_specs=[vmem],
        out_specs=(vmem,) * 7,
        name="unpack",
    )(total.reshape(128, 128))
    return (final,) + outs[:6] + (outs[6].reshape(1),)


def solution(mesh):
    return jax.shard_map(
        local,
        mesh=mesh,
        in_specs=(
            P(None, None, "normal", "span"),
            P(None, "normal", "span"),
            P("normal", "span", None, None),
            P("normal", "span", None, None),
            P("span", None, None),
            P("span", None),
            P("span", None, None),
            P("span", None),
            P("span", None, None),
            P("span", None),
        ),
        out_specs=(
            P(None, None, "normal", "span"),
            P("span", None, None),
            P("span", None),
            P("span", None, None),
            P("span", None),
            P("span", None, None),
            P("span", None),
            P("span"),
        ),
        check_vma=False,
    )
```

```python
import functools

import jax
import jax.numpy as jnp
import numpy as np
from jax import lax
from jax.experimental import pallas as pl
from jax.experimental.pallas import tpu as pltpu
from jax.sharding import PartitionSpec as P

STEPS = 4
CROPS_DEV = 12
GROUP = 6
SX, CZ, CY = 4, 16, 128
EZ, EY = 24, 256
HID = 64
VOX = 512

VELOCITY = (
    (0, 0, 0),
    (1, 0, 0),
    (-1, 0, 0),
    (0, 1, 0),
    (0, -1, 0),
    (0, 0, 1),
    (0, 0, -1),
    (1, 1, 0),
    (-1, -1, 0),
    (1, -1, 0),
    (-1, 1, 0),
    (1, 0, 1),
    (-1, 0, -1),
    (1, 0, -1),
    (-1, 0, 1),
    (0, 1, 1),
    (0, -1, -1),
    (0, 1, -1),
    (0, -1, 1),
)
WEIGHTS = (1.0 / 3.0,) + (1.0 / 18.0,) * 6 + (1.0 / 36.0,) * 12
OPPOSITE = (0, 2, 1, 4, 3, 6, 5, 8, 7, 10, 9, 12, 11, 14, 13, 16, 15, 18, 17)
OMEGA = 1.25
SCALE_DENSITY = 50.0
SCALE_FLOW = 30.0
F32 = jnp.float32
BF16 = jnp.bfloat16
MESH = pl.DeviceIdType.MESH


def signed_sum(entries, factors):
    running = None
    for entry, factor in zip(entries, factors):
        if factor == 0:
            continue
        if running is None:
            running = entry if factor > 0 else -entry
        else:
            running = running + entry if factor > 0 else running - entry
    return running


def moments(states):
    density = states[0]
    for number in range(1, 19):
        density = density + states[number]
    inverse = 1.0 / density
    flows = []
    for axis_id in range(3):
        summed = signed_sum(states, [VELOCITY[number][axis_id] for number in range(19)])
        flows.append(summed * inverse)
    return (density, flows[0], flows[1], flows[2])


def collide(states, wet_cells):
    density, flow_x, flow_y, flow_z = moments(states)
    flows = (flow_x, flow_y, flow_z)
    speed_sq = flow_x * flow_x + flow_y * flow_y + flow_z * flow_z
    base = 1.0 - 1.5 * speed_sq
    result = [None] * 19
    kept = 1.0 - OMEGA
    scaled = {w: (OMEGA * w) * density for w in set(WEIGHTS)}
    relaxed = kept * states[0] + scaled[WEIGHTS[0]] * base
    result[0] = jnp.where(wet_cells, relaxed, states[0])
    for number in range(1, 19, 2):
        other = OPPOSITE[number]
        along = signed_sum(flows, VELOCITY[number])
        weight = scaled[WEIGHTS[number]]
        even = weight * (base + (4.5 * along) * along)
        odd = weight * (3.0 * along)
        forth = kept * states[number] + (even + odd)
        back = kept * states[other] + (even - odd)
        result[number] = jnp.where(wet_cells, forth, states[other])
        result[other] = jnp.where(wet_cells, back, states[number])
    return result


def features(states, fluid):
    density, flow_x, flow_y, flow_z = moments(states)
    return [
        (density - 1.0) * SCALE_DENSITY * fluid,
        flow_x * SCALE_FLOW * fluid,
        flow_y * SCALE_FLOW * fluid,
        flow_z * SCALE_FLOW * fluid,
    ]


NT = (((1,), (1,)), ((), ()))
TN = (((0,), (0,)), ((), ()))


def dot(a, b, dims=(((1,), (0,)), ((), ()))):
    return lax.dot_general(a, b, dims, preferred_element_type=F32)


SHIFTS = [(a, b, c) for a in (-1, 0, 1) for b in (-1, 0, 1) for c in (-1, 0, 1)]


def lattice_part(
    ns,
    nn,
    pop_hbm,
    wall_hbm,
    w_lift,
    b_lift,
    w_mix,
    b_mix,
    w_head,
    b_head,
    anchors_hbm,
    spread_hbm,
    select_hbm,
    choose_hbm,
    inside_hbm,
    more_fetches,
    n_peers,
    meanwhile,
    fin,
    fin_sem,
    patches,
    targets,
    wets,
    wall,
    v_lift,
    v_blift,
    v_mix,
    v_bmix,
    v_head,
    v_bhead,
    anchors,
    spread,
    select,
    choose,
    inside,
    wb,
    small,
    early,
    late,
    windows,
    pack_l,
    pack_r,
    pack_u,
    pack_d,
    got_l,
    got_r,
    got_u,
    got_d,
    got_c,
    weights,
    cells,
    post,
    loads,
    halo_send,
    halo_recv,
    ag_send,
    ag_recv,
    fw_send,
    fw_recv,
):
    s = lax.axis_index("span")
    n = lax.axis_index("normal")
    chips = ns // 2
    chip = s // 2
    core = s % 2
    right, left = (s + 1) % ns, (s + ns - 1) % ns
    up, down = (n + 1) % nn, (n + nn - 1) % nn
    sibling = chip * 2 + (1 - core)

    def place(nn_, ss_):
        return {"normal": nn_, "span": ss_}

    fetches = [
        pltpu.make_async_copy(src, dst, loads.at[i])
        for i, (src, dst) in enumerate(
            (
                (pop_hbm, cells.at[0:19, :, 0:CZ, 0:CY]),
                (wall_hbm, wall),
                (w_lift, v_lift),
                (b_lift, v_blift),
                (w_mix, v_mix),
                (b_mix, v_bmix),
                (w_head, v_head),
                (b_head, v_bhead),
                (anchors_hbm, anchors),
                (spread_hbm, spread),
                (select_hbm, select),
                (choose_hbm, choose),
                (inside_hbm, inside),
                *more_fetches,
            )
        )
    ]
    for copy in fetches:
        copy.start()

    peers = [
        place(n, right),
        place(n, left),
        place(up, right),
        place(up, left),
        place(down, right),
        place(down, left),
        place(n, sibling),
    ]
    z_peers = [((chip + k) % chips) * 2 + core for k in range(1, chips)]
    peers += [place(n, peer) for peer in z_peers]
    peers += [place(other, s) for other in n_peers]
    barrier = pltpu.get_barrier_semaphore()
    for peer in peers:
        pl.semaphore_signal(barrier, inc=1, device_id=peer, device_id_type=MESH)

    sub = lax.broadcasted_iota(jnp.int32, (8, 128), 0)
    low = sub < 4
    wb[...] = jnp.zeros((144, 128), F32)
    small[...] = jnp.zeros((16, 128), F32)
    fetches[0].wait()
    fetches[1].wait()
    cells[19, :, 0:CZ, 0:CY] = wall[...].astype(F32)

    for k in range(20):
        for j in range(2):
            t0, t1 = cells[k, 2 * j, 0:CZ, 0:CY], cells[k, 2 * j + 1, 0:CZ, 0:CY]
            pack_u[k, j] = jnp.where(low, pltpu.roll(t1[8:16], 4, 0), t0[8:16])
            pack_d[k, j] = jnp.where(low, t0[0:8], pltpu.roll(t1[0:8], 4, 0))
    pl.semaphore_wait(barrier, len(peers))

    def halo(i, src, dst, peer):
        return pltpu.make_async_remote_copy(
            src_ref=src,
            dst_ref=dst,
            send_sem=halo_send.at[i],
            recv_sem=halo_recv.at[i],
            device_id=peer,
            device_id_type=MESH,
        )

    sends = [
        halo(0, pack_u, got_u, place(up, s)),
        halo(1, pack_d, got_d, place(down, s)),
    ]
    for copy in sends:
        copy.start()
    slot = lax.broadcasted_iota(jnp.int32, (64, 128), 1) // 4
    pl_val = jnp.ones((64, 128), F32)
    pr_val = jnp.ones((64, 128), F32)
    for k in range(20):
        f = cells[k, :, 0:CZ, 0:CY].reshape(64, 128)
        rolled = pltpu.roll(f, 4 * k, 1) if k else f
        pl_val = jnp.where(slot == k, rolled, pl_val)
        pr_val = jnp.where(slot == (k - 1) % 32, rolled, pr_val)
    pack_l[...] = pl_val.reshape(SX, CZ, CY)
    pack_r[...] = pr_val.reshape(SX, CZ, CY)

    top, bottom = pl.ds(8, 8), pl.ds(0, 8)
    more = [
        halo(2, pack_l, got_l, place(n, left)),
        halo(3, pack_r, got_r, place(n, right)),
        halo(4, pack_l.at[:, bottom, :], got_c.at[0], place(down, left)),
        halo(5, pack_l.at[:, top, :], got_c.at[1], place(up, left)),
        halo(6, pack_r.at[:, bottom, :], got_c.at[2], place(down, right)),
        halo(7, pack_r.at[:, top, :], got_c.at[3], place(up, right)),
    ]
    for copy in more:
        copy.start()
    sends += more

    for copy in fetches[2:8]:
        copy.wait()
    wb[0:64, 0:108] = v_lift[0].astype(F32)
    wb[64:128, 0:64] = v_mix[0].astype(F32)
    small[0:1, 0:64] = v_blift[...].astype(F32)
    small[1:2, 0:64] = v_bmix[...].astype(F32)
    small[2:3, 0:4] = v_bhead[...].astype(F32)
    small[4:8, 0:64] = v_head[0].astype(F32)
    row16 = lax.broadcasted_iota(jnp.int32, (16, 128), 0)
    lane16 = lax.broadcasted_iota(jnp.int32, (16, 128), 1)
    head_at = (row16 >= 4) & (row16 < 8)
    head_at = head_at & ((lane16 == row16 + 108) | (lane16 == row16 + 112))
    to_top = ((row16 == 0) & (lane16 == 108)) | head_at
    to_mix = (row16 == 1) & (lane16 == 64)
    to_head = (row16 == 2) & (lane16 == 64)
    rows = small[...].astype(BF16)

    def turned(mask):
        return dot(rows, mask.astype(F32).astype(BF16), TN)

    seat = lax.broadcasted_iota(jnp.int32, (16, 128), 1)
    first = row16 % 12
    held = (row16 < 4) | (row16 >= 12)
    picks = (held & (seat == first)).astype(F32).astype(BF16)
    seat4 = lax.broadcasted_iota(jnp.int32, (16, 16), 1)
    row4 = lax.broadcasted_iota(jnp.int32, (16, 16), 0)
    picks4 = (((row4 < 4) | (row4 >= 12)) & (seat4 == row4 % 12 + 4)).astype(F32).astype(BF16)
    wb[0:64] = wb[0:64] + turned(to_top)[0:64]
    wb[64:128] = wb[64:128] + turned(to_mix)[0:64]
    wb[128:144] = dot(picks4, rows) + dot(picks, turned(to_head).astype(BF16))
    mine = wb[...].astype(BF16)
    weights[s] = mine

    gathers = []
    for k, peer in enumerate(z_peers):
        gathers.append(
            pltpu.make_async_remote_copy(
                src_ref=weights.at[s],
                dst_ref=weights.at[s],
                send_sem=ag_send.at[k],
                recv_sem=ag_recv.at[k],
                device_id=place(n, peer),
                device_id_type=MESH,
            )
        )
    for copy in gathers:
        copy.start()

    def forward(i, owner):
        return pltpu.make_async_remote_copy(
            src_ref=weights.at[owner],
            dst_ref=weights.at[owner],
            send_sem=fw_send.at[i],
            recv_sem=fw_recv.at[i],
            device_id=place(n, sibling),
            device_id_type=MESH,
        )

    forwards = [forward(0, s)]
    forwards[0].start()

    fluid = (1 - wall[...]).astype(F32)
    before = features([cells[q, :, 0:CZ, 0:CY] for q in range(19)], fluid)
    for c in range(4):
        early[:, c] = before[c].astype(BF16)
    early[:, 4] = fluid.astype(BF16)
    for copy in fetches[8:]:
        copy.wait()

    ahead = lax.broadcasted_iota(jnp.int32, (128, 256), 0)
    ahead = ahead - lax.broadcasted_iota(jnp.int32, (128, 256), 1) % 16
    unit_row = (lax.broadcasted_iota(jnp.int32, (40, VOX), 0) == 0).astype(F32)

    def cut(field, count, crop, window):
        ox = anchors[0, 0, 0, crop]
        near = field[ox].reshape(count * CZ, 128)
        far = field[(ox + 1) % SX].reshape(count * CZ, 128)
        wide = dot(jnp.concatenate([near, far], axis=0), window)
        return (wide * spread[0 : count * CZ * 2]).astype(BF16)

    def early_pair(i, carry):
        parts = []
        for j in range(2):
            crop = 2 * i + j
            oy = anchors[0, 1, 0, crop] % CY
            window = (ahead == oy).astype(F32).astype(BF16)
            windows[crop] = window
            parts.append(cut(early, 5, crop, window))
        got = dot(select[...], jnp.concatenate(parts, axis=0))
        x8 = jnp.concatenate([got[0:8], got[8:16]], axis=1)
        wets[i] = jnp.concatenate([got[16:24], got[24:32]], axis=1)
        moved = []
        for dx, dz, dy in SHIFTS:
            shift = (-(dx * 256 + dz * 16 + dy)) % VOX
            moved.append(pltpu.roll(x8, shift, 1) if shift else x8)
        moved.append(unit_row)
        patches[i] = jnp.concatenate(moved, axis=0).astype(BF16) * inside[...]
        return carry

    lax.fori_loop(0, CROPS_DEV // 2, early_pair, 0)

    meanwhile()
    for copy in sends:
        copy.wait()

    low4 = jnp.broadcast_to(low[None], (SX, 8, 128))
    edge_l = jnp.concatenate([got_l[...], jnp.where(low4, got_c[0], got_c[1])], axis=1)
    edge_r = jnp.concatenate([got_r[...], jnp.where(low4, got_c[2], got_c[3])], axis=1)
    edge_l = edge_l.reshape(SX * EZ, 128)
    edge_r = edge_r.reshape(SX * EZ, 128)
    odd = (lax.broadcasted_iota(jnp.int32, (SX * EZ, 128), 1) // 4) % 2 == 1
    mixed = (jnp.where(odd, edge_r, edge_l), jnp.where(odd, edge_l, edge_r))
    for k in range(20):
        side = mixed[k % 2]
        if k:
            side = pltpu.roll(side, 128 - 4 * k, 1)
        cells[k, :, :, CY:EY] = side.reshape(SX, EZ, 128)
        for j in range(2):
            u, d = got_u[k, j], got_d[k, j]
            cells[k, 2 * j, CZ:EZ, 0:CY] = jnp.where(low, d, u)
            cells[k, 2 * j + 1, CZ:EZ, 0:CY] = pltpu.roll(jnp.where(low, u, d), 4, 0)

    def one_step(step, carry):
        def one_chunk(i, inner):
            x = i // 3
            part = pl.ds(pl.multiple_of((i % 3) * 8, 8), 8)
            states = [cells[q, x, part, :] for q in range(19)]
            wet = cells[19, x, part, :] < 0.5
            for q, value in enumerate(collide(states, wet)):
                post[q, x, part, :] = value
            return inner

        lax.fori_loop(0, 12, one_chunk, 0)

        def one_slab(x, inner):
            for q in range(19):
                cx, cy, cz = VELOCITY[q]
                slab = post[q, (x + SX - cx) % SX]
                if cz:
                    slab = pltpu.roll(slab, cz % EZ, 0)
                if cy:
                    slab = pltpu.roll(slab, cy % EY, 1)
                cells[q, x] = slab
            return inner

        lax.fori_loop(0, SX, one_slab, 0)
        return carry

    lax.fori_loop(0, 2, one_step, 0)
    for k in range(1, chips):
        gathers[k - 1].wait()
        owner = ((chip + chips - k) % chips) * 2 + core
        copy = forward(k, owner)
        copy.start()
        forwards.append(copy)
    lax.fori_loop(2, STEPS, one_step, 0)

    store = pltpu.make_async_copy(cells.at[0:19, :, 0:CZ, 0:CY], fin, fin_sem)
    store.start()
    final = [cells[q, :, 0:CZ, 0:CY] for q in range(19)]
    after = features(final, fluid)
    for c in range(4):
        late[:, c] = (after[c] - before[c]).astype(BF16)

    def late_pair(i, carry):
        parts = [cut(late, 4, 2 * i + j, windows[2 * i + j]) for j in range(2)]
        got = dot(choose[...], jnp.concatenate(parts, axis=0))
        targets[i] = jnp.concatenate([got[0:8], got[8:16]], axis=1)
        return carry

    lax.fori_loop(0, CROPS_DEV // 2, late_pair, 0)
    for copy in forwards:
        copy.wait()
    return store


def gelu_both(x):
    c1, c2 = 0.7978845608028654, 0.7978845608028654 * 0.044715
    sq = x * x
    half = 0.5 * jnp.tanh(x * (c1 + c2 * sq)) + 0.5
    value = x * half
    slope = half + value * (1.0 - half) * (2.0 * c1 + 6.0 * c2 * sq)
    return value, slope


def constants():
    row = np.arange(160)
    lane = np.arange(256)
    spread = (lane[None, :] // 16 == row[:, None] % 16).astype(np.float32)
    select = np.zeros((32, 320), np.float32)
    choose = np.zeros((16, 256), np.float32)
    for xi in range(2):
        for i in range(8):
            crop, channel = i // 4, i % 4
            start = crop * 160 + xi * 80 + channel * 16
            select[xi * 8 + i, start : start + 16] = 1.0
            start = crop * 160 + xi * 80 + 64
            select[16 + xi * 8 + i, start : start + 16] = 1.0
            start = crop * 128 + xi * 64 + channel * 16
            choose[xi * 8 + i, start : start + 16] = 1.0
    expand = np.zeros((2, 128, 256), np.float32)
    for pos in range(2):
        for k in range(27):
            for c in range(4):
                expand[pos, 4 * k + c, 8 * k + 4 * pos + c] = 1.0
        expand[pos, 108, 216] = 1.0
    voxel = np.arange(VOX)
    vx, vz, vy = voxel // 256, voxel // 16 % 16, voxel % 16
    inside = np.ones((256, VOX), np.float32)
    for k, (dx, dz, dy) in enumerate(SHIFTS):
        good = (
            (vx + dx >= 0)
            & (vx + dx < 2)
            & (vz + dz >= 0)
            & (vz + dz < 16)
            & (vy + dy >= 0)
            & (vy + dy < 16)
        )
        inside[8 * k : 8 * k + 8] = good[None]
    return (
        (
            jnp.asarray(spread),
            jnp.asarray(select, BF16),
            jnp.asarray(choose, BF16),
            jnp.asarray(inside, BF16),
        ),
        (
            jnp.asarray(expand, BF16),
            jnp.asarray(np.transpose(expand, (0, 2, 1)), BF16),
        ),
    )


def train_part(
    ns,
    nn,
    trainers,
    patches_ref,
    targets,
    wets,
    wall_w,
    expand,
    shrink,
    out,
    crops,
    index,
    grads,
    pair,
    held,
    sent,
    parts,
    zparts,
    mine,
    whole,
    pair_send,
    pair_recv,
    rs_send,
    rs_recv,
    z_send,
    z_recv,
    ag_send,
    ag_recv,
):
    s = lax.axis_index("span")
    n = lax.axis_index("normal")
    chips = ns // 2
    chip = s // 2
    core = s % 2
    sibling = chip * 2 + (1 - core)
    rows = 128 // nn
    n_peers = normal_peers(n, nn)
    z_peers = [(chip + k) % chips for k in far_first(chips)]

    def at_span(other):
        return {"span": other, "normal": n}

    def at_normal(other):
        return {"span": s, "normal": other}

    crops[CROPS_DEV] = jnp.zeros((128, 128), F32)
    unit = (lax.broadcasted_iota(jnp.int32, (64, VOX), 0) == 0).astype(F32).astype(BF16)
    lane64 = lax.broadcasted_iota(jnp.int32, (64, 128), 1)
    lane128 = lax.broadcasted_iota(jnp.int32, (128, 128), 1)

    def one_group(g, carry):
        wide = range(GROUP)
        both = range(2)
        pairs = [g * GROUP + p for p in wide]
        mats = [[wall_w[trainers[0, 0, 0, 2 * i + j]] for j in both] for i in pairs]
        patches = [patches_ref[i] for i in pairs]
        lift = [[dot(mats[p][j][0:64], expand[j]) for j in both] for p in wide]
        lift = [jnp.concatenate(lift[p], axis=0).astype(BF16) for p in wide]
        z1 = [dot(lift[p], patches[p]) for p in wide]
        h1, slope1 = [], []
        for p in wide:
            value, slope = gelu_both(z1[p])
            h1.append(value.astype(BF16))
            slope1.append(slope)
        own = [[h1[p][64 * j : 64 * j + 64] for j in both] for p in wide]
        ext1 = [[jnp.concatenate([own[p][j], unit], axis=0) for j in both] for p in wide]
        z2 = [[dot(mats[p][j][64:128], ext1[p][j]) for j in both] for p in wide]
        ext2 = [[None, None] for p in wide]
        slope2 = [[None, None] for p in wide]
        for p in wide:
            for j in both:
                value, slope2[p][j] = gelu_both(z2[p][j])
                h2 = (own[p][j].astype(F32) + value).astype(BF16)
                ext2[p][j] = jnp.concatenate([h2, unit], axis=0)
        pred = [
            [dot(mats[p][j][128:144], ext2[p][j])[8 * j : 8 * j + 8] for j in both] for p in wide
        ]
        errors = []
        for p in wide:
            missed = pred[p][0] + pred[p][1] - targets[pairs[p]]
            weighted = wets[pairs[p]] * missed
            loss8 = weighted * missed * (1.0 / (4.0 * VOX))
            dpred = weighted * (2.0 / (4.0 * VOX))
            tail = jnp.concatenate([dpred, loss8], axis=0).astype(BF16)
            errors.append(jnp.concatenate([jnp.zeros((112, VOX), BF16), tail], axis=0))
        head = [
            [jnp.where(keeps[j], mats[p][j][0:64].astype(F32), 0.0).astype(BF16) for j in both]
            for p in wide
        ]
        dh2 = [[dot(head[p][j], errors[p]) for j in both] for p in wide]
        dz2 = [[(dh2[p][j] * slope2[p][j]).astype(BF16) for j in both] for p in wide]
        back = [[dot(mats[p][j][64:128, 0:64], dz2[p][j], TN) for j in both] for p in wide]
        dh1 = [jnp.concatenate([dh2[p][j] + back[p][j] for j in both], axis=0) for p in wide]
        dz1 = [(dh1[p] * slope1[p]).astype(BF16) for p in wide]
        lifted = [dot(dz1[p], patches[p], NT).astype(BF16) for p in wide]
        mixed = [[dot(dz2[p][j], ext1[p][j], NT) for j in both] for p in wide]
        heads = [[dot(ext2[p][j], errors[p], NT) for j in both] for p in wide]
        less = [[dot(lifted[p][64 * j : 64 * j + 64], shrink[j]) for j in both] for p in wide]
        for p in wide:
            for j in both:
                mine_only = jnp.where(owned[j], heads[p][j], 0.0)
                upper = (less[p][j] + mine_only[0:64]).astype(BF16).astype(F32)
                lower = mixed[p][j] + mine_only[64:128]
                lower = jnp.where(lane64 < 64, lower.astype(BF16).astype(F32), lower)
                crops[2 * pairs[p] + j, 0:64] = upper
                crops[2 * pairs[p] + j, 64:128] = lower
        return carry

    keeps = [(lane64 >= 112 + 4 * j) & (lane64 < 116 + 4 * j) for j in range(2)]
    owned = [(lane128 // 4) % 2 == j for j in range(2)]
    lax.fori_loop(0, CROPS_DEV // 2 // GROUP, one_group, 0)

    def member(m):
        return crops[index[m, 0]] + crops[index[m, 1]]

    def theirs(z, carry):
        grads[z] = member(2 * z + 1 - core).astype(BF16)
        return carry

    lax.fori_loop(0, chips, theirs, 0)

    def remote(src, dst, send, recv, peer):
        copy = pltpu.make_async_remote_copy(
            src_ref=src,
            dst_ref=dst,
            send_sem=send,
            recv_sem=recv,
            device_id=peer,
            device_id_type=MESH,
        )
        copy.start()
        return copy

    first = remote(grads, pair, pair_send.at[0], pair_recv.at[0], at_span(sibling))

    def ours(z, carry):
        held[z] = member(2 * z + core)
        return carry

    lax.fori_loop(0, chips, ours, 0)
    first.wait()
    for z in range(0, chips, 2):
        two = [held[z + i] + pair[z + i].astype(F32) for i in range(2)]
        two = jnp.concatenate([v.reshape(nn, rows, 128) for v in two], axis=1)
        sent[:, z * rows : (z + 2) * rows, :] = two.astype(BF16)
    seconds = []
    for k, other in enumerate(n_peers):
        seconds.append(
            remote(sent.at[other], parts.at[k], rs_send.at[k], rs_recv.at[k], at_normal(other))
        )
    own = sent[n].astype(F32)
    for k in range(nn - 1):
        seconds[k].wait()
        own = own + parts[k].astype(F32)
    mine[...] = own.reshape(chips, rows, 128)
    thirds = []
    for k, other in enumerate(z_peers):
        thirds.append(
            remote(
                mine.at[other],
                zparts.at[k],
                z_send.at[k],
                z_recv.at[k],
                at_span(other * 2 + core),
            )
        )
    total = mine[chip]
    for k in range(chips - 1):
        thirds[k].wait()
        total = total + zparts[k]
    whole[n] = total * (1.0 / (CROPS_DEV * nn))
    fourths = []
    for k, other in enumerate(n_peers):
        fourths.append(
            remote(
                whole.at[n], whole.at[n], ag_send.at[k], ag_recv.at[k], at_normal(other)
            )
        )
    for copy in fourths:
        copy.wait()
    out[...] = whole[...]


def far_first(count):
    return sorted(range(1, count), key=lambda k: -min(k, count - k))


def normal_peers(n, nn):
    if nn != 16:
        return [(n + k) % nn for k in range(1, nn)]
    moves = [(i, j) for i in range(4) for j in range(4) if i or j]
    moves.sort(key=lambda m: -(min(m[0], 4 - m[0]) + min(m[1], 4 - m[1])))
    return [(n // 4 + i) % 4 * 4 + (n % 4 + j) % 4 for i, j in moves]


def fused_kernel(ns, nn, *refs):
    (
        pop,
        wall,
        w_lift,
        b_lift,
        w_mix,
        b_mix,
        w_head,
        b_head,
        anchors,
        trainers,
        spread,
        select,
        choose,
        inside,
        expand,
        shrink,
        fin,
        total,
    ) = refs[:18]
    fin_sem, v_trainers, v_expand, v_shrink, patches, targets, wets, weights = refs[18:26]
    lattice_refs, train_refs = refs[26:61], refs[61:]
    n = lax.axis_index("normal")
    n_peers = normal_peers(n, nn)
    def meanwhile():
        def remember(m, carry):
            last, before = jnp.int32(CROPS_DEV), jnp.int32(CROPS_DEV)
            for c in range(CROPS_DEV):
                match = v_trainers[0, 0, 0, c] == m
                before = jnp.where(match, last, before)
                last = jnp.where(match, c, last)
            train_refs[1][m, 0] = last
            train_refs[1][m, 1] = before
            return carry

        lax.fori_loop(0, ns, remember, 0)

    store = lattice_part(
        ns,
        nn,
        pop,
        wall,
        w_lift,
        b_lift,
        w_mix,
        b_mix,
        w_head,
        b_head,
        anchors,
        spread,
        select,
        choose,
        inside,
        ((trainers, v_trainers), (expand, v_expand), (shrink, v_shrink)),
        n_peers,
        meanwhile,
        fin,
        fin_sem,
        patches,
        targets,
        wets,
        *lattice_refs[:26],
        weights,
        *lattice_refs[26:],
    )
    train_part(
        ns,
        nn,
        v_trainers,
        patches,
        targets,
        wets,
        weights,
        v_expand,
        v_shrink,
        total,
        *train_refs,
    )
    store.wait()


def unpack_kernel(
    fin, total, o_fin, o_lift, o_blift, o_mix, o_bmix, o_head, o_bhead, o_loss, stage, whole_v, sems
):
    def hop(i, src, dst):
        copy = pltpu.make_async_copy(src, dst, sems.at[i])
        copy.start()
        return copy

    first = hop(8, total, whole_v)
    edges = (0, 5, 10, 15, 19)
    spans = [pl.ds(a, b - a) for a, b in zip(edges[:-1], edges[1:])]
    reads = [hop(i, fin.at[span], stage.at[span]) for i, span in enumerate(spans)]
    first.wait()
    writes = []
    for i, span in enumerate(spans):
        reads[i].wait()
        writes.append(hop(4 + i, stage.at[span], o_fin.at[span]))
    whole = whole_v[...]
    turned = whole.T
    o_lift[0] = whole[0:64, 0:108]
    o_mix[0] = whole[64:128, 0:64]
    o_blift[...] = turned[108:109, 0:64]
    o_bmix[...] = turned[64:65, 64:128]
    heads = turned[112:120, 0:64]
    o_head[0] = heads[0:4] + heads[4:8]
    line = whole[64:65]
    o_bhead[...] = line[:, 112:116] + line[:, 116:120]
    lane = lax.broadcasted_iota(jnp.int32, (1, 128), 1)
    o_loss[...] = jnp.sum(jnp.where(lane >= 120, line, 0.0), axis=1, keepdims=True)
    for copy in writes:
        copy.wait()


def local(
    populations, wall_mask, crop_anchors, trainers, w_lift, b_lift, w_mix, b_mix, w_head, b_head
):
    ns, nn = lax.axis_size("span"), lax.axis_size("normal")
    chips = ns // 2
    pairs = CROPS_DEV // 2
    vmem = pl.BlockSpec(memory_space=pltpu.VMEM)
    hbm = pl.BlockSpec(memory_space=pltpu.HBM)
    dma = pltpu.SemaphoreType.DMA
    shape = jax.ShapeDtypeStruct
    cutting, weighing = constants()
    spread, select, choose, inside = cutting
    edge = pltpu.VMEM((SX, CZ, CY), F32)
    flat = pltpu.VMEM((20, 2, 8, 128), F32)
    rows = 128 // nn
    final, total = pl.pallas_call(
        functools.partial(fused_kernel, ns, nn),
        out_shape=(shape((19, SX, CZ, CY), F32), shape((nn, rows, 128), F32)),
        in_specs=[hbm] * 16,
        out_specs=(hbm, vmem),
        scratch_shapes=[
            dma,
            pltpu.SMEM((1, 1, 1, CROPS_DEV), jnp.int32),
            pltpu.VMEM((2, 128, 256), BF16),
            pltpu.VMEM((2, 256, 128), BF16),
            pltpu.VMEM((pairs, 256, VOX), BF16),
            pltpu.VMEM((pairs, 8, VOX), F32),
            pltpu.VMEM((pairs, 8, VOX), F32),
            pltpu.VMEM((ns, 144, 128), BF16),
            pltpu.VMEM((SX, CZ, CY), jnp.int32),
            pltpu.VMEM(w_lift.shape, BF16),
            pltpu.VMEM(b_lift.shape, BF16),
            pltpu.VMEM(w_mix.shape, BF16),
            pltpu.VMEM(b_mix.shape, BF16),
            pltpu.VMEM(w_head.shape, BF16),
            pltpu.VMEM(b_head.shape, BF16),
            pltpu.SMEM((1, 3, 1, CROPS_DEV), jnp.int32),
            pltpu.VMEM(spread.shape, F32),
            pltpu.VMEM(select.shape, BF16),
            pltpu.VMEM(choose.shape, BF16),
            pltpu.VMEM(inside.shape, BF16),
            pltpu.VMEM((144, 128), F32),
            pltpu.VMEM((16, 128), F32),
            pltpu.VMEM((SX, 5, CZ, CY), BF16),
            pltpu.VMEM((SX, 4, CZ, CY), BF16),
            pltpu.VMEM((CROPS_DEV, 128, 256), BF16),
            edge,
            edge,
            flat,
            flat,
            edge,
            edge,
            flat,
            flat,
            pltpu.VMEM((4, SX, 8, 128), F32),
            pltpu.VMEM((20, SX, EZ, EY), F32),
            pltpu.VMEM((19, SX, EZ, EY), F32),
            dma((16,)),
            dma((8,)),
            dma((8,)),
            dma((chips,)),
            dma((chips,)),
            dma((chips,)),
            dma((chips,)),
            pltpu.VMEM((CROPS_DEV + 1, 128, 128), F32),
            pltpu.SMEM((ns, 2), jnp.int32),
            pltpu.VMEM((chips, 128, 128), BF16),
            pltpu.VMEM((chips, 128, 128), BF16),
            pltpu.VMEM((chips, 128, 128), F32),
            pltpu.VMEM((nn, chips * rows, 128), BF16),
            pltpu.VMEM((nn - 1, chips * rows, 128), BF16),
            pltpu.VMEM((chips - 1, rows, 128), F32),
            pltpu.VMEM((chips, rows, 128), F32),
            pltpu.VMEM((nn, rows, 128), F32),
            dma((1,)),
            dma((1,)),
            dma((nn - 1,)),
            dma((nn - 1,)),
            dma((chips - 1,)),
            dma((chips - 1,)),
            dma((nn - 1,)),
            dma((nn - 1,)),
        ],
        compiler_params=pltpu.CompilerParams(
            collective_id=0, has_side_effects=True, vmem_limit_bytes=60 << 20
        ),
        name="channel",
    )(
        populations,
        wall_mask,
        w_lift,
        b_lift,
        w_mix,
        b_mix,
        w_head,
        b_head,
        jnp.transpose(crop_anchors, (0, 3, 1, 2)),
        jnp.swapaxes(trainers, 2, 3),
        spread,
        select,
        choose,
        inside,
        *weighing,
    )
    outs = pl.pallas_call(
        unpack_kernel,
        out_shape=(
            shape(populations.shape, F32),
            shape(w_lift.shape, F32),
            shape(b_lift.shape, F32),
            shape(w_mix.shape, F32),
            shape(b_mix.shape, F32),
            shape(w_head.shape, F32),
            shape(b_head.shape, F32),
            shape((1, 1), F32),
        ),
        in_specs=[hbm, hbm],
        out_specs=(hbm,) + (vmem,) * 7,
        scratch_shapes=[
            pltpu.VMEM(populations.shape, F32),
            pltpu.VMEM((128, 128), F32),
            dma((9,)),
        ],
        compiler_params=pltpu.CompilerParams(vmem_limit_bytes=60 << 20),
        name="unpack",
    )(final, total.reshape(128, 128))
    return outs[:7] + (outs[7].reshape(1),)


def solution(mesh):
    return jax.shard_map(
        local,
        mesh=mesh,
        in_specs=(
            P(None, None, "normal", "span"),
            P(None, "normal", "span"),
            P("normal", "span", None, None),
            P("normal", "span", None, None),
            P("span", None, None),
            P("span", None),
            P("span", None, None),
            P("span", None),
            P("span", None, None),
            P("span", None),
        ),
        out_specs=(
            P(None, None, "normal", "span"),
            P("span", None, None),
            P("span", None),
            P("span", None, None),
            P("span", None),
            P("span", None, None),
            P("span", None),
            P("span"),
        ),
        check_vma=False,
    )
```

```python
import functools

import jax
import jax.numpy as jnp
import numpy as np
from jax import lax
from jax.experimental import pallas as pl
from jax.experimental.pallas import tpu as pltpu
from jax.sharding import PartitionSpec as P

STEPS = 4
CROPS_DEV = 12
GROUP = 6
SX, CZ, CY = 4, 16, 128
EZ, EY = 24, 256
HID = 64
VOX = 512

VELOCITY = (
    (0, 0, 0),
    (1, 0, 0),
    (-1, 0, 0),
    (0, 1, 0),
    (0, -1, 0),
    (0, 0, 1),
    (0, 0, -1),
    (1, 1, 0),
    (-1, -1, 0),
    (1, -1, 0),
    (-1, 1, 0),
    (1, 0, 1),
    (-1, 0, -1),
    (1, 0, -1),
    (-1, 0, 1),
    (0, 1, 1),
    (0, -1, -1),
    (0, 1, -1),
    (0, -1, 1),
)
WEIGHTS = (1.0 / 3.0,) + (1.0 / 18.0,) * 6 + (1.0 / 36.0,) * 12
OPPOSITE = (0, 2, 1, 4, 3, 6, 5, 8, 7, 10, 9, 12, 11, 14, 13, 16, 15, 18, 17)
OMEGA = 1.25
SCALE_DENSITY = 50.0
SCALE_FLOW = 30.0
F32 = jnp.float32
BF16 = jnp.bfloat16
MESH = pl.DeviceIdType.MESH


def signed_sum(entries, factors):
    running = None
    for entry, factor in zip(entries, factors):
        if factor == 0:
            continue
        if running is None:
            running = entry if factor > 0 else -entry
        else:
            running = running + entry if factor > 0 else running - entry
    return running


def moments(states):
    density = states[0]
    for number in range(1, 19):
        density = density + states[number]
    inverse = 1.0 / density
    flows = []
    for axis_id in range(3):
        summed = signed_sum(states, [VELOCITY[number][axis_id] for number in range(19)])
        flows.append(summed * inverse)
    return (density, flows[0], flows[1], flows[2])


def collide(states, wet_cells):
    density, flow_x, flow_y, flow_z = moments(states)
    flows = (flow_x, flow_y, flow_z)
    speed_sq = flow_x * flow_x + flow_y * flow_y + flow_z * flow_z
    base = 1.0 - 1.5 * speed_sq
    result = [None] * 19
    kept = 1.0 - OMEGA
    scaled = {w: (OMEGA * w) * density for w in set(WEIGHTS)}
    relaxed = kept * states[0] + scaled[WEIGHTS[0]] * base
    result[0] = jnp.where(wet_cells, relaxed, states[0])
    for number in range(1, 19, 2):
        other = OPPOSITE[number]
        along = signed_sum(flows, VELOCITY[number])
        weight = scaled[WEIGHTS[number]]
        even = weight * (base + (4.5 * along) * along)
        odd = weight * (3.0 * along)
        forth = kept * states[number] + (even + odd)
        back = kept * states[other] + (even - odd)
        result[number] = jnp.where(wet_cells, forth, states[other])
        result[other] = jnp.where(wet_cells, back, states[number])
    return result


def features(states, fluid):
    density, flow_x, flow_y, flow_z = moments(states)
    return [
        (density - 1.0) * SCALE_DENSITY * fluid,
        flow_x * SCALE_FLOW * fluid,
        flow_y * SCALE_FLOW * fluid,
        flow_z * SCALE_FLOW * fluid,
    ]


NT = (((1,), (1,)), ((), ()))
TN = (((0,), (0,)), ((), ()))


def dot(a, b, dims=(((1,), (0,)), ((), ()))):
    return lax.dot_general(a, b, dims, preferred_element_type=F32)


SHIFTS = [(a, b, c) for a in (-1, 0, 1) for b in (-1, 0, 1) for c in (-1, 0, 1)]


def lattice_part(
    ns,
    nn,
    pop_hbm,
    wall_hbm,
    w_lift,
    b_lift,
    w_mix,
    b_mix,
    w_head,
    b_head,
    anchors_hbm,
    spread_hbm,
    select_hbm,
    choose_hbm,
    inside_hbm,
    more_fetches,
    n_peers,
    meanwhile,
    fin,
    fin_sem,
    patches,
    targets,
    wets,
    wall,
    v_lift,
    v_blift,
    v_mix,
    v_bmix,
    v_head,
    v_bhead,
    anchors,
    spread,
    select,
    choose,
    inside,
    wb,
    small,
    early,
    late,
    windows,
    pack_l,
    pack_r,
    pack_u,
    pack_d,
    got_l,
    got_r,
    got_u,
    got_d,
    got_c,
    weights,
    cells,
    post,
    loads,
    halo_send,
    halo_recv,
    ag_send,
    ag_recv,
    fw_send,
    fw_recv,
):
    s = lax.axis_index("span")
    n = lax.axis_index("normal")
    chips = ns // 2
    chip = s // 2
    core = s % 2
    right, left = (s + 1) % ns, (s + ns - 1) % ns
    up, down = (n + 1) % nn, (n + nn - 1) % nn
    sibling = chip * 2 + (1 - core)

    def place(nn_, ss_):
        return {"normal": nn_, "span": ss_}

    fetches = [
        pltpu.make_async_copy(src, dst, loads.at[i])
        for i, (src, dst) in enumerate(
            (
                (pop_hbm, cells.at[0:19, :, 0:CZ, 0:CY]),
                (wall_hbm, wall),
                (w_lift, v_lift),
                (b_lift, v_blift),
                (w_mix, v_mix),
                (b_mix, v_bmix),
                (w_head, v_head),
                (b_head, v_bhead),
                (anchors_hbm, anchors),
                (spread_hbm, spread),
                (select_hbm, select),
                (choose_hbm, choose),
                (inside_hbm, inside),
                *more_fetches,
            )
        )
    ]
    fetches[0].start()
    fetches[1].start()

    z_peers = [((chip + k) % chips) * 2 + core for k in range(1, chips)]
    far_z = [((chip + k) % chips) * 2 + core for k in far_first(chips)]
    peers = [place(n, peer) for peer in far_z]
    peers += [place(other, s) for other in n_peers]
    peers += [
        place(up, right),
        place(up, left),
        place(down, right),
        place(down, left),
        place(n, right),
        place(n, left),
        place(n, sibling),
    ]
    barrier = pltpu.get_barrier_semaphore()
    for peer in peers:
        pl.semaphore_signal(barrier, inc=1, device_id=peer, device_id_type=MESH)
    for copy in fetches[2:]:
        copy.start()

    sub = lax.broadcasted_iota(jnp.int32, (8, 128), 0)
    low = sub < 4
    wb[...] = jnp.zeros((144, 128), F32)
    small[...] = jnp.zeros((16, 128), F32)
    fetches[0].wait()
    fetches[1].wait()
    cells[19, :, 0:CZ, 0:CY] = wall[...].astype(F32)

    def own_chunk(i, inner):
        x = i // 2
        part = pl.ds(pl.multiple_of((i % 2) * 8, 8), 8)
        states = [cells[q, x, part, 0:CY] for q in range(19)]
        wet = cells[19, x, part, 0:CY] < 0.5
        for q, value in enumerate(collide(states, wet)):
            post[q, x, part, 0:CY] = value
        return inner

    lax.fori_loop(0, 8, own_chunk, 0, unroll=4)

    def source(k):
        return post.at[k] if k < 19 else cells.at[19]

    for k in range(20):
        for j in range(2):
            t0 = source(k)[2 * j, 0:CZ, 0:CY]
            t1 = source(k)[2 * j + 1, 0:CZ, 0:CY]
            pack_u[k, j] = jnp.where(low, pltpu.roll(t1[8:16], 4, 0), t0[8:16])
            pack_d[k, j] = jnp.where(low, t0[0:8], pltpu.roll(t1[0:8], 4, 0))
    pl.semaphore_wait(barrier, len(peers))

    def halo(i, src, dst, peer):
        return pltpu.make_async_remote_copy(
            src_ref=src,
            dst_ref=dst,
            send_sem=halo_send.at[i],
            recv_sem=halo_recv.at[i],
            device_id=peer,
            device_id_type=MESH,
        )

    sends = [
        halo(0, pack_u, got_u, place(up, s)),
        halo(1, pack_d, got_d, place(down, s)),
    ]
    for copy in sends:
        copy.start()
    slot = lax.broadcasted_iota(jnp.int32, (64, 128), 1) // 4
    pl_val = jnp.ones((64, 128), F32)
    pr_val = jnp.ones((64, 128), F32)
    for k in range(20):
        f = source(k)[:, 0:CZ, 0:CY].reshape(64, 128)
        rolled = pltpu.roll(f, 4 * k, 1) if k else f
        pl_val = jnp.where(slot == k, rolled, pl_val)
        pr_val = jnp.where(slot == (k - 1) % 32, rolled, pr_val)
    pack_l[...] = pl_val.reshape(SX, CZ, CY)
    pack_r[...] = pr_val.reshape(SX, CZ, CY)

    top, bottom = pl.ds(8, 8), pl.ds(0, 8)
    more = [
        halo(2, pack_l, got_l, place(n, left)),
        halo(3, pack_r, got_r, place(n, right)),
        halo(4, pack_l.at[:, bottom, :], got_c.at[0], place(down, left)),
        halo(5, pack_l.at[:, top, :], got_c.at[1], place(up, left)),
        halo(6, pack_r.at[:, bottom, :], got_c.at[2], place(down, right)),
        halo(7, pack_r.at[:, top, :], got_c.at[3], place(up, right)),
    ]
    for copy in more:
        copy.start()
    sends += more

    for copy in fetches[2:8]:
        copy.wait()
    wb[0:64, 0:108] = v_lift[0].astype(F32)
    wb[64:128, 0:64] = v_mix[0].astype(F32)
    small[0:1, 0:64] = v_blift[...].astype(F32)
    small[1:2, 0:64] = v_bmix[...].astype(F32)
    small[2:3, 0:4] = v_bhead[...].astype(F32)
    small[4:8, 0:64] = v_head[0].astype(F32)
    row16 = lax.broadcasted_iota(jnp.int32, (16, 128), 0)
    lane16 = lax.broadcasted_iota(jnp.int32, (16, 128), 1)
    head_at = (row16 >= 4) & (row16 < 8)
    head_at = head_at & ((lane16 == row16 + 108) | (lane16 == row16 + 112))
    to_top = ((row16 == 0) & (lane16 == 108)) | head_at
    to_mix = (row16 == 1) & (lane16 == 64)
    to_head = (row16 == 2) & (lane16 == 64)
    rows = small[...].astype(BF16)

    def turned(mask):
        return dot(rows, mask.astype(F32).astype(BF16), TN)

    seat = lax.broadcasted_iota(jnp.int32, (16, 128), 1)
    first = row16 % 12
    held = (row16 < 4) | (row16 >= 12)
    picks = (held & (seat == first)).astype(F32).astype(BF16)
    seat4 = lax.broadcasted_iota(jnp.int32, (16, 16), 1)
    row4 = lax.broadcasted_iota(jnp.int32, (16, 16), 0)
    picks4 = (((row4 < 4) | (row4 >= 12)) & (seat4 == row4 % 12 + 4)).astype(F32).astype(BF16)
    wb[0:64] = wb[0:64] + turned(to_top)[0:64]
    wb[64:128] = wb[64:128] + turned(to_mix)[0:64]
    wb[128:144] = dot(picks4, rows) + dot(picks, turned(to_head).astype(BF16))
    mine = wb[...].astype(BF16)
    weights[s] = mine

    gathers = []
    for k, peer in enumerate(z_peers):
        gathers.append(
            pltpu.make_async_remote_copy(
                src_ref=weights.at[s],
                dst_ref=weights.at[s],
                send_sem=ag_send.at[k],
                recv_sem=ag_recv.at[k],
                device_id=place(n, peer),
                device_id_type=MESH,
            )
        )
    for copy in gathers:
        copy.start()

    def forward(i, owner):
        return pltpu.make_async_remote_copy(
            src_ref=weights.at[owner],
            dst_ref=weights.at[owner],
            send_sem=fw_send.at[i],
            recv_sem=fw_recv.at[i],
            device_id=place(n, sibling),
            device_id_type=MESH,
        )

    forwards = [forward(0, s)]
    forwards[0].start()

    fluid = (1 - wall[...]).astype(F32)
    before = features([cells[q, :, 0:CZ, 0:CY] for q in range(19)], fluid)
    for c in range(4):
        early[:, c] = before[c].astype(BF16)
    early[:, 4] = fluid.astype(BF16)
    for copy in fetches[8:]:
        copy.wait()

    ahead = lax.broadcasted_iota(jnp.int32, (128, 256), 0)
    ahead = ahead - lax.broadcasted_iota(jnp.int32, (128, 256), 1) % 16
    unit_row = (lax.broadcasted_iota(jnp.int32, (40, VOX), 0) == 0).astype(F32)

    def cut(field, count, crop, window):
        ox = anchors[0, 0, 0, crop]
        near = field[ox].reshape(count * CZ, 128)
        far = field[(ox + 1) % SX].reshape(count * CZ, 128)
        wide = dot(jnp.concatenate([near, far], axis=0), window)
        return (wide * spread[0 : count * CZ * 2]).astype(BF16)

    def early_pair(i, carry):
        parts = []
        for j in range(2):
            crop = 2 * i + j
            oy = anchors[0, 1, 0, crop] % CY
            window = (ahead == oy).astype(F32).astype(BF16)
            windows[crop] = window
            parts.append(cut(early, 5, crop, window))
        got = dot(select[...], jnp.concatenate(parts, axis=0))
        x8 = jnp.concatenate([got[0:8], got[8:16]], axis=1)
        wets[i] = jnp.concatenate([got[16:24], got[24:32]], axis=1)
        moved = []
        for dx, dz, dy in SHIFTS:
            shift = (-(dx * 256 + dz * 16 + dy)) % VOX
            moved.append(pltpu.roll(x8, shift, 1) if shift else x8)
        moved.append(unit_row)
        patches[i] = jnp.concatenate(moved, axis=0).astype(BF16) * inside[...]
        return carry

    lax.fori_loop(0, CROPS_DEV // 2, early_pair, 0)

    meanwhile()
    for copy in sends[2:]:
        copy.wait()

    low4 = jnp.broadcast_to(low[None], (SX, 8, 128))
    edge_l = jnp.concatenate([got_l[...], jnp.where(low4, got_c[0], got_c[1])], axis=1)
    edge_r = jnp.concatenate([got_r[...], jnp.where(low4, got_c[2], got_c[3])], axis=1)
    edge_l = edge_l.reshape(SX * EZ, 128)
    edge_r = edge_r.reshape(SX * EZ, 128)
    odd = (lax.broadcasted_iota(jnp.int32, (SX * EZ, 128), 1) // 4) % 2 == 1
    mixed = (jnp.where(odd, edge_r, edge_l), jnp.where(odd, edge_l, edge_r))
    for k in range(20):
        side = mixed[k % 2]
        if k:
            side = pltpu.roll(side, 128 - 4 * k, 1)
        source(k)[:, :, CY:EY] = side.reshape(SX, EZ, 128)
    for copy in sends[:2]:
        copy.wait()
    for k in range(20):
        for j in range(2):
            u, d = got_u[k, j], got_d[k, j]
            source(k)[2 * j, CZ:EZ, 0:CY] = jnp.where(low, d, u)
            source(k)[2 * j + 1, CZ:EZ, 0:CY] = pltpu.roll(jnp.where(low, u, d), 4, 0)

    def one_step(step, carry):
        def one_chunk(i, inner):
            x = i // 3
            part = pl.ds(pl.multiple_of((i % 3) * 8, 8), 8)
            states = [cells[q, x, part, :] for q in range(19)]
            wet = cells[19, x, part, :] < 0.5
            for q, value in enumerate(collide(states, wet)):
                post[q, x, part, :] = value
            return inner

        lax.fori_loop(0, 12, one_chunk, 0, unroll=6)
        move()
        return carry

    def move():
        def one_slab(x, inner):
            for q in range(19):
                cx, cy, cz = VELOCITY[q]
                slab = post[q, (x + SX - cx) % SX]
                if cz:
                    slab = pltpu.roll(slab, cz % EZ, 0)
                if cy:
                    slab = pltpu.roll(slab, cy % EY, 1)
                cells[q, x] = slab
            return inner

        lax.fori_loop(0, SX, one_slab, 0, unroll=4)

    move()
    one_step(1, 0)
    for k in range(1, chips):
        gathers[k - 1].wait()
        owner = ((chip + chips - k) % chips) * 2 + core
        copy = forward(k, owner)
        copy.start()
        forwards.append(copy)
    lax.fori_loop(2, STEPS, one_step, 0)

    store = pltpu.make_async_copy(cells.at[0:19, :, 0:CZ, 0:CY], fin, fin_sem)
    store.start()
    final = [cells[q, :, 0:CZ, 0:CY] for q in range(19)]
    after = features(final, fluid)
    for c in range(4):
        late[:, c] = (after[c] - before[c]).astype(BF16)

    cuts = [cut(late, 4, crop, windows[crop]) for crop in range(CROPS_DEV)]
    for i in range(CROPS_DEV // 2):
        got = dot(choose[...], jnp.concatenate(cuts[2 * i : 2 * i + 2], axis=0))
        targets[i] = jnp.concatenate([got[0:8], got[8:16]], axis=1)
    for copy in forwards:
        copy.wait()
    return store


def gelu_both(x):
    c1, c2 = 0.7978845608028654, 0.7978845608028654 * 0.044715
    sq = x * x
    half = 0.5 * jnp.tanh(x * (c1 + c2 * sq)) + 0.5
    value = x * half
    slope = half + value * (1.0 - half) * (2.0 * c1 + 6.0 * c2 * sq)
    return value, slope


def constants():
    row = np.arange(160)
    lane = np.arange(256)
    spread = (lane[None, :] // 16 == row[:, None] % 16).astype(np.float32)
    select = np.zeros((32, 320), np.float32)
    choose = np.zeros((16, 256), np.float32)
    for xi in range(2):
        for i in range(8):
            crop, channel = i // 4, i % 4
            start = crop * 160 + xi * 80 + channel * 16
            select[xi * 8 + i, start : start + 16] = 1.0
            start = crop * 160 + xi * 80 + 64
            select[16 + xi * 8 + i, start : start + 16] = 1.0
            start = crop * 128 + xi * 64 + channel * 16
            choose[xi * 8 + i, start : start + 16] = 1.0
    expand = np.zeros((2, 128, 256), np.float32)
    for pos in range(2):
        for k in range(27):
            for c in range(4):
                expand[pos, 4 * k + c, 8 * k + 4 * pos + c] = 1.0
        expand[pos, 108, 216] = 1.0
    voxel = np.arange(VOX)
    vx, vz, vy = voxel // 256, voxel // 16 % 16, voxel % 16
    inside = np.ones((256, VOX), np.float32)
    for k, (dx, dz, dy) in enumerate(SHIFTS):
        good = (
            (vx + dx >= 0)
            & (vx + dx < 2)
            & (vz + dz >= 0)
            & (vz + dz < 16)
            & (vy + dy >= 0)
            & (vy + dy < 16)
        )
        inside[8 * k : 8 * k + 8] = good[None]
    return (
        (
            jnp.asarray(spread),
            jnp.asarray(select, BF16),
            jnp.asarray(choose, BF16),
            jnp.asarray(inside, BF16),
        ),
        (
            jnp.asarray(expand, BF16),
            jnp.asarray(np.transpose(expand, (0, 2, 1)), BF16),
        ),
    )


def train_part(
    ns,
    nn,
    trainers,
    patches_ref,
    targets,
    wets,
    wall_w,
    expand,
    shrink,
    out,
    crops,
    index,
    grads,
    pair,
    held,
    sent,
    parts,
    zparts,
    mine,
    whole,
    pair_send,
    pair_recv,
    rs_send,
    rs_recv,
    z_send,
    z_recv,
    ag_send,
    ag_recv,
):
    s = lax.axis_index("span")
    n = lax.axis_index("normal")
    chips = ns // 2
    chip = s // 2
    core = s % 2
    sibling = chip * 2 + (1 - core)
    rows = 128 // nn
    n_peers = normal_peers(n, nn)
    z_peers = [(chip + k) % chips for k in far_first(chips)]

    def at_span(other):
        return {"span": other, "normal": n}

    def at_normal(other):
        return {"span": s, "normal": other}

    crops[CROPS_DEV] = jnp.zeros((128, 128), F32)
    unit = (lax.broadcasted_iota(jnp.int32, (64, VOX), 0) == 0).astype(F32).astype(BF16)
    lane64 = lax.broadcasted_iota(jnp.int32, (64, 128), 1)
    lane128 = lax.broadcasted_iota(jnp.int32, (128, 128), 1)

    def one_group(g, carry):
        wide = range(GROUP)
        both = range(2)
        pairs = [g * GROUP + p for p in wide]
        mats = [[wall_w[trainers[0, 0, 0, 2 * i + j]] for j in both] for i in pairs]
        patches = [patches_ref[i] for i in pairs]
        lift = [[dot(mats[p][j][0:64], expand[j]) for j in both] for p in wide]
        lift = [jnp.concatenate(lift[p], axis=0).astype(BF16) for p in wide]
        z1 = [dot(lift[p], patches[p]) for p in wide]
        h1, slope1 = [], []
        for p in wide:
            value, slope = gelu_both(z1[p])
            h1.append(value.astype(BF16))
            slope1.append(slope)
        own = [[h1[p][64 * j : 64 * j + 64] for j in both] for p in wide]
        ext1 = [[jnp.concatenate([own[p][j], unit], axis=0) for j in both] for p in wide]
        z2 = [[dot(mats[p][j][64:128], ext1[p][j]) for j in both] for p in wide]
        ext2 = [[None, None] for p in wide]
        slope2 = [[None, None] for p in wide]
        for p in wide:
            for j in both:
                value, slope2[p][j] = gelu_both(z2[p][j])
                h2 = (own[p][j].astype(F32) + value).astype(BF16)
                ext2[p][j] = jnp.concatenate([h2, unit], axis=0)
        pred = [
            [dot(mats[p][j][128:144], ext2[p][j])[8 * j : 8 * j + 8] for j in both] for p in wide
        ]
        errors = []
        for p in wide:
            missed = pred[p][0] + pred[p][1] - targets[pairs[p]]
            weighted = wets[pairs[p]] * missed
            loss8 = weighted * missed * (1.0 / (4.0 * VOX))
            dpred = weighted * (2.0 / (4.0 * VOX))
            tail = jnp.concatenate([dpred, loss8], axis=0).astype(BF16)
            errors.append(jnp.concatenate([jnp.zeros((112, VOX), BF16), tail], axis=0))
        head = [
            [jnp.where(keeps[j], mats[p][j][0:64].astype(F32), 0.0).astype(BF16) for j in both]
            for p in wide
        ]
        dh2 = [[dot(head[p][j], errors[p]) for j in both] for p in wide]
        dz2 = [[(dh2[p][j] * slope2[p][j]).astype(BF16) for j in both] for p in wide]
        back = [[dot(mats[p][j][64:128, 0:64], dz2[p][j], TN) for j in both] for p in wide]
        dh1 = [jnp.concatenate([dh2[p][j] + back[p][j] for j in both], axis=0) for p in wide]
        dz1 = [(dh1[p] * slope1[p]).astype(BF16) for p in wide]
        lifted = [dot(dz1[p], patches[p], NT).astype(BF16) for p in wide]
        mixed = [[dot(dz2[p][j], ext1[p][j], NT) for j in both] for p in wide]
        heads = [[dot(ext2[p][j], errors[p], NT) for j in both] for p in wide]
        less = [[dot(lifted[p][64 * j : 64 * j + 64], shrink[j]) for j in both] for p in wide]
        for p in wide:
            for j in both:
                mine_only = jnp.where(owned[j], heads[p][j], 0.0)
                upper = (less[p][j] + mine_only[0:64]).astype(BF16).astype(F32)
                lower = mixed[p][j] + mine_only[64:128]
                lower = jnp.where(lane64 < 64, lower.astype(BF16).astype(F32), lower)
                crops[2 * pairs[p] + j, 0:64] = upper
                crops[2 * pairs[p] + j, 64:128] = lower
        return carry

    keeps = [(lane64 >= 112 + 4 * j) & (lane64 < 116 + 4 * j) for j in range(2)]
    owned = [(lane128 // 4) % 2 == j for j in range(2)]
    lax.fori_loop(0, CROPS_DEV // 2 // GROUP, one_group, 0)

    def member(m):
        return crops[index[m, 0]] + crops[index[m, 1]]

    def theirs(z, carry):
        grads[z] = member(2 * z + 1 - core).astype(BF16)
        return carry

    lax.fori_loop(0, chips, theirs, 0)

    def remote(src, dst, send, recv, peer):
        copy = pltpu.make_async_remote_copy(
            src_ref=src,
            dst_ref=dst,
            send_sem=send,
            recv_sem=recv,
            device_id=peer,
            device_id_type=MESH,
        )
        copy.start()
        return copy

    first = remote(grads, pair, pair_send.at[0], pair_recv.at[0], at_span(sibling))

    def ours(z, carry):
        held[z] = member(2 * z + core)
        return carry

    lax.fori_loop(0, chips, ours, 0)
    first.wait()
    for z in range(0, chips, 2):
        two = [held[z + i] + pair[z + i].astype(F32) for i in range(2)]
        two = jnp.concatenate([v.reshape(nn, rows, 128) for v in two], axis=1)
        sent[:, z * rows : (z + 2) * rows, :] = two.astype(BF16)
    seconds = []
    for k, other in enumerate(n_peers):
        seconds.append(
            remote(sent.at[other], parts.at[k], rs_send.at[k], rs_recv.at[k], at_normal(other))
        )
    own = sent[n].astype(F32)
    for k in range(nn - 1):
        seconds[k].wait()
        own = own + parts[k].astype(F32)
    mine[...] = own.reshape(chips, rows, 128)
    thirds = []
    for k, other in enumerate(z_peers):
        thirds.append(
            remote(
                mine.at[other],
                zparts.at[k],
                z_send.at[k],
                z_recv.at[k],
                at_span(other * 2 + core),
            )
        )
    total = mine[chip]
    for k in range(chips - 1):
        thirds[k].wait()
        total = total + zparts[k]
    whole[n] = total * (1.0 / (CROPS_DEV * nn))
    fourths = []
    for k, other in enumerate(n_peers):
        fourths.append(
            remote(
                whole.at[n], whole.at[n], ag_send.at[k], ag_recv.at[k], at_normal(other)
            )
        )
    for copy in fourths:
        copy.wait()
    out[...] = whole[...]


def far_first(count):
    return sorted(range(1, count), key=lambda k: -min(k, count - k))


def normal_peers(n, nn):
    if nn != 16:
        return [(n + k) % nn for k in range(1, nn)]
    moves = [(i, j) for i in range(4) for j in range(4) if i or j]
    moves.sort(key=lambda m: -(min(m[0], 4 - m[0]) + min(m[1], 4 - m[1])))
    return [(n // 4 + i) % 4 * 4 + (n % 4 + j) % 4 for i, j in moves]


def fused_kernel(ns, nn, *refs):
    (
        pop,
        wall,
        w_lift,
        b_lift,
        w_mix,
        b_mix,
        w_head,
        b_head,
        anchors,
        trainers,
        spread,
        select,
        choose,
        inside,
        expand,
        shrink,
        fin,
        total,
    ) = refs[:18]
    fin_sem, v_trainers, v_expand, v_shrink, patches, targets, wets, weights = refs[18:26]
    lattice_refs, train_refs = refs[26:61], refs[61:]
    n = lax.axis_index("normal")
    n_peers = normal_peers(n, nn)
    def meanwhile():
        def remember(m, carry):
            last, before = jnp.int32(CROPS_DEV), jnp.int32(CROPS_DEV)
            for c in range(CROPS_DEV):
                match = v_trainers[0, 0, 0, c] == m
                before = jnp.where(match, last, before)
                last = jnp.where(match, c, last)
            train_refs[1][m, 0] = last
            train_refs[1][m, 1] = before
            return carry

        lax.fori_loop(0, ns, remember, 0)

    store = lattice_part(
        ns,
        nn,
        pop,
        wall,
        w_lift,
        b_lift,
        w_mix,
        b_mix,
        w_head,
        b_head,
        anchors,
        spread,
        select,
        choose,
        inside,
        ((trainers, v_trainers), (expand, v_expand), (shrink, v_shrink)),
        n_peers,
        meanwhile,
        fin,
        fin_sem,
        patches,
        targets,
        wets,
        *lattice_refs[:26],
        weights,
        *lattice_refs[26:],
    )
    train_part(
        ns,
        nn,
        v_trainers,
        patches,
        targets,
        wets,
        weights,
        v_expand,
        v_shrink,
        total,
        *train_refs,
    )
    store.wait()


def unpack_kernel(fin, total, *refs):
    outs, stages, stage, whole_v, sems = refs[:8], refs[8:15], refs[15], refs[16], refs[17]
    o_lift, o_blift, o_mix, o_bmix, o_head, o_bhead, o_loss = stages

    def hop(i, src, dst):
        copy = pltpu.make_async_copy(src, dst, sems.at[i])
        copy.start()
        return copy

    first = hop(0, total, whole_v)
    edges = (0, 5, 10, 15, 19)
    spans = [pl.ds(a, b - a) for a, b in zip(edges[:-1], edges[1:])]
    reads = [hop(1 + i, fin.at[span], stage.at[span]) for i, span in enumerate(spans)]
    first.wait()
    whole = whole_v[...]
    turned = whole.T
    o_lift[0] = whole[0:64, 0:108]
    o_mix[0] = whole[64:128, 0:64]
    o_blift[...] = turned[108:109, 0:64]
    o_bmix[...] = turned[64:65, 64:128]
    heads = turned[112:120, 0:64]
    o_head[0] = heads[0:4] + heads[4:8]
    line = whole[64:65]
    o_bhead[...] = line[:, 112:116] + line[:, 116:120]
    lane = lax.broadcasted_iota(jnp.int32, (1, 128), 1)
    o_loss[...] = jnp.sum(jnp.where(lane >= 120, line, 0.0), axis=1, keepdims=True)
    writes = [hop(9 + i, stages[i], outs[1 + i]) for i in range(7)]
    for i, span in enumerate(spans):
        reads[i].wait()
        writes.append(hop(5 + i, stage.at[span], outs[0].at[span]))
    for copy in writes:
        copy.wait()


def local(
    populations, wall_mask, crop_anchors, trainers, w_lift, b_lift, w_mix, b_mix, w_head, b_head
):
    ns, nn = lax.axis_size("span"), lax.axis_size("normal")
    chips = ns // 2
    pairs = CROPS_DEV // 2
    vmem = pl.BlockSpec(memory_space=pltpu.VMEM)
    hbm = pl.BlockSpec(memory_space=pltpu.HBM)
    dma = pltpu.SemaphoreType.DMA
    shape = jax.ShapeDtypeStruct
    cutting, weighing = constants()
    spread, select, choose, inside = cutting
    edge = pltpu.VMEM((SX, CZ, CY), F32)
    flat = pltpu.VMEM((20, 2, 8, 128), F32)
    rows = 128 // nn
    final, total = pl.pallas_call(
        functools.partial(fused_kernel, ns, nn),
        out_shape=(shape((19, SX, CZ, CY), F32), shape((nn, rows, 128), F32)),
        in_specs=[hbm] * 16,
        out_specs=(hbm, vmem),
        scratch_shapes=[
            dma,
            pltpu.SMEM((1, 1, 1, CROPS_DEV), jnp.int32),
            pltpu.VMEM((2, 128, 256), BF16),
            pltpu.VMEM((2, 256, 128), BF16),
            pltpu.VMEM((pairs, 256, VOX), BF16),
            pltpu.VMEM((pairs, 8, VOX), F32),
            pltpu.VMEM((pairs, 8, VOX), F32),
            pltpu.VMEM((ns, 144, 128), BF16),
            pltpu.VMEM((SX, CZ, CY), jnp.int32),
            pltpu.VMEM(w_lift.shape, BF16),
            pltpu.VMEM(b_lift.shape, BF16),
            pltpu.VMEM(w_mix.shape, BF16),
            pltpu.VMEM(b_mix.shape, BF16),
            pltpu.VMEM(w_head.shape, BF16),
            pltpu.VMEM(b_head.shape, BF16),
            pltpu.SMEM((1, 3, 1, CROPS_DEV), jnp.int32),
            pltpu.VMEM(spread.shape, F32),
            pltpu.VMEM(select.shape, BF16),
            pltpu.VMEM(choose.shape, BF16),
            pltpu.VMEM(inside.shape, BF16),
            pltpu.VMEM((144, 128), F32),
            pltpu.VMEM((16, 128), F32),
            pltpu.VMEM((SX, 5, CZ, CY), BF16),
            pltpu.VMEM((SX, 4, CZ, CY), BF16),
            pltpu.VMEM((CROPS_DEV, 128, 256), BF16),
            edge,
            edge,
            flat,
            flat,
            edge,
            edge,
            flat,
            flat,
            pltpu.VMEM((4, SX, 8, 128), F32),
            pltpu.VMEM((20, SX, EZ, EY), F32),
            pltpu.VMEM((19, SX, EZ, EY), F32),
            dma((16,)),
            dma((8,)),
            dma((8,)),
            dma((chips,)),
            dma((chips,)),
            dma((chips,)),
            dma((chips,)),
            pltpu.VMEM((CROPS_DEV + 1, 128, 128), F32),
            pltpu.SMEM((ns, 2), jnp.int32),
            pltpu.VMEM((chips, 128, 128), BF16),
            pltpu.VMEM((chips, 128, 128), BF16),
            pltpu.VMEM((chips, 128, 128), F32),
            pltpu.VMEM((nn, chips * rows, 128), BF16),
            pltpu.VMEM((nn - 1, chips * rows, 128), BF16),
            pltpu.VMEM((chips - 1, rows, 128), F32),
            pltpu.VMEM((chips, rows, 128), F32),
            pltpu.VMEM((nn, rows, 128), F32),
            dma((1,)),
            dma((1,)),
            dma((nn - 1,)),
            dma((nn - 1,)),
            dma((chips - 1,)),
            dma((chips - 1,)),
            dma((nn - 1,)),
            dma((nn - 1,)),
        ],
        compiler_params=pltpu.CompilerParams(
            collective_id=0, has_side_effects=True, vmem_limit_bytes=60 << 20
        ),
        name="channel",
    )(
        populations,
        wall_mask,
        w_lift,
        b_lift,
        w_mix,
        b_mix,
        w_head,
        b_head,
        jnp.transpose(crop_anchors, (0, 3, 1, 2)),
        jnp.swapaxes(trainers, 2, 3),
        spread,
        select,
        choose,
        inside,
        *weighing,
    )
    small = [
        shape(w_lift.shape, F32),
        shape(b_lift.shape, F32),
        shape(w_mix.shape, F32),
        shape(b_mix.shape, F32),
        shape(w_head.shape, F32),
        shape(b_head.shape, F32),
        shape((1, 1), F32),
    ]
    outs = pl.pallas_call(
        unpack_kernel,
        out_shape=[shape(populations.shape, F32)] + small,
        in_specs=[hbm, hbm],
        out_specs=[hbm] * 8,
        scratch_shapes=[pltpu.VMEM(leaf.shape, F32) for leaf in small]
        + [
            pltpu.VMEM(populations.shape, F32),
            pltpu.VMEM((128, 128), F32),
            dma((16,)),
        ],
        compiler_params=pltpu.CompilerParams(vmem_limit_bytes=60 << 20),
        name="unpack",
    )(final, total.reshape(128, 128))
    return tuple(outs[:7]) + (outs[7].reshape(1),)


def solution(mesh):
    return jax.shard_map(
        local,
        mesh=mesh,
        in_specs=(
            P(None, None, "normal", "span"),
            P(None, "normal", "span"),
            P("normal", "span", None, None),
            P("normal", "span", None, None),
            P("span", None, None),
            P("span", None),
            P("span", None, None),
            P("span", None),
            P("span", None, None),
            P("span", None),
        ),
        out_specs=(
            P(None, None, "normal", "span"),
            P("span", None, None),
            P("span", None),
            P("span", None, None),
            P("span", None),
            P("span", None, None),
            P("span", None),
            P("span"),
        ),
        check_vma=False,
    )
```

```python
import functools

import jax
import jax.numpy as jnp
import numpy as np
from jax import lax
from jax.experimental import pallas as pl
from jax.experimental.pallas import tpu as pltpu
from jax.sharding import PartitionSpec as P

STEPS = 4
CROPS_DEV = 12
GROUP = 6
SX, CZ, CY = 4, 16, 128
EZ, EY = 24, 256
HID = 64
VOX = 512

VELOCITY = (
    (0, 0, 0),
    (1, 0, 0),
    (-1, 0, 0),
    (0, 1, 0),
    (0, -1, 0),
    (0, 0, 1),
    (0, 0, -1),
    (1, 1, 0),
    (-1, -1, 0),
    (1, -1, 0),
    (-1, 1, 0),
    (1, 0, 1),
    (-1, 0, -1),
    (1, 0, -1),
    (-1, 0, 1),
    (0, 1, 1),
    (0, -1, -1),
    (0, 1, -1),
    (0, -1, 1),
)
WEIGHTS = (1.0 / 3.0,) + (1.0 / 18.0,) * 6 + (1.0 / 36.0,) * 12
OPPOSITE = (0, 2, 1, 4, 3, 6, 5, 8, 7, 10, 9, 12, 11, 14, 13, 16, 15, 18, 17)
OMEGA = 1.25
SCALE_DENSITY = 50.0
SCALE_FLOW = 30.0
F32 = jnp.float32
BF16 = jnp.bfloat16
MESH = pl.DeviceIdType.MESH


def signed_sum(entries, factors):
    running = None
    for entry, factor in zip(entries, factors):
        if factor == 0:
            continue
        if running is None:
            running = entry if factor > 0 else -entry
        else:
            running = running + entry if factor > 0 else running - entry
    return running


def moments(states):
    density = states[0]
    for number in range(1, 19):
        density = density + states[number]
    inverse = 1.0 / density
    flows = []
    for axis_id in range(3):
        summed = signed_sum(states, [VELOCITY[number][axis_id] for number in range(19)])
        flows.append(summed * inverse)
    return (density, flows[0], flows[1], flows[2])


def collide(states, wet_cells):
    density, flow_x, flow_y, flow_z = moments(states)
    flows = (flow_x, flow_y, flow_z)
    speed_sq = flow_x * flow_x + flow_y * flow_y + flow_z * flow_z
    base = 1.0 - 1.5 * speed_sq
    result = [None] * 19
    kept = 1.0 - OMEGA
    scaled = {w: (OMEGA * w) * density for w in set(WEIGHTS)}
    relaxed = kept * states[0] + scaled[WEIGHTS[0]] * base
    result[0] = jnp.where(wet_cells, relaxed, states[0])
    for number in range(1, 19, 2):
        other = OPPOSITE[number]
        along = signed_sum(flows, VELOCITY[number])
        weight = scaled[WEIGHTS[number]]
        even = weight * (base + (4.5 * along) * along)
        odd = weight * (3.0 * along)
        forth = kept * states[number] + (even + odd)
        back = kept * states[other] + (even - odd)
        result[number] = jnp.where(wet_cells, forth, states[other])
        result[other] = jnp.where(wet_cells, back, states[number])
    return result


def features(states, fluid):
    density, flow_x, flow_y, flow_z = moments(states)
    return [
        (density - 1.0) * SCALE_DENSITY * fluid,
        flow_x * SCALE_FLOW * fluid,
        flow_y * SCALE_FLOW * fluid,
        flow_z * SCALE_FLOW * fluid,
    ]


NT = (((1,), (1,)), ((), ()))
TN = (((0,), (0,)), ((), ()))


def dot(a, b, dims=(((1,), (0,)), ((), ()))):
    return lax.dot_general(a, b, dims, preferred_element_type=F32)


SHIFTS = [(a, b, c) for a in (-1, 0, 1) for b in (-1, 0, 1) for c in (-1, 0, 1)]


def lattice_part(
    ns,
    nn,
    pop_hbm,
    wall_hbm,
    w_lift,
    b_lift,
    w_mix,
    b_mix,
    w_head,
    b_head,
    anchors_hbm,
    spread_hbm,
    select_hbm,
    choose_hbm,
    inside_hbm,
    more_fetches,
    n_peers,
    meanwhile,
    fin,
    fin_sem,
    patches,
    targets,
    wets,
    wall,
    v_lift,
    v_blift,
    v_mix,
    v_bmix,
    v_head,
    v_bhead,
    anchors,
    spread,
    select,
    choose,
    inside,
    wb,
    small,
    early,
    late,
    windows,
    pack_l,
    pack_r,
    pack_u,
    pack_d,
    got_l,
    got_r,
    got_u,
    got_d,
    got_c,
    weights,
    cells,
    post,
    loads,
    halo_send,
    halo_recv,
    ag_send,
    ag_recv,
    fw_send,
    fw_recv,
):
    s = lax.axis_index("span")
    n = lax.axis_index("normal")
    chips = ns // 2
    chip = s // 2
    core = s % 2
    right, left = (s + 1) % ns, (s + ns - 1) % ns
    up, down = (n + 1) % nn, (n + nn - 1) % nn
    sibling = chip * 2 + (1 - core)

    def place(nn_, ss_):
        return {"normal": nn_, "span": ss_}

    fetches = [
        pltpu.make_async_copy(src, dst, loads.at[i])
        for i, (src, dst) in enumerate(
            (
                (pop_hbm, cells.at[0:19, :, 0:CZ, 0:CY]),
                (wall_hbm, wall),
                (w_lift, v_lift),
                (b_lift, v_blift),
                (w_mix, v_mix),
                (b_mix, v_bmix),
                (w_head, v_head),
                (b_head, v_bhead),
                (anchors_hbm, anchors),
                (spread_hbm, spread),
                (select_hbm, select),
                (choose_hbm, choose),
                (inside_hbm, inside),
                *more_fetches,
            )
        )
    ]
    fetches[0].start()
    fetches[1].start()

    z_peers = [((chip + k) % chips) * 2 + core for k in range(1, chips)]
    far_z = [((chip + k) % chips) * 2 + core for k in far_first(chips)]
    peers = [place(n, peer) for peer in far_z]
    peers += [place(other, s) for other in n_peers]
    peers += [
        place(up, right),
        place(up, left),
        place(down, right),
        place(down, left),
        place(n, right),
        place(n, left),
        place(n, sibling),
    ]
    barrier = pltpu.get_barrier_semaphore()
    for peer in peers:
        pl.semaphore_signal(barrier, inc=1, device_id=peer, device_id_type=MESH)
    for copy in fetches[2:]:
        copy.start()

    sub = lax.broadcasted_iota(jnp.int32, (8, 128), 0)
    low = sub < 4
    wb[...] = jnp.zeros((144, 128), F32)
    small[...] = jnp.zeros((16, 128), F32)
    fetches[0].wait()
    fetches[1].wait()
    cells[19, :, 0:CZ, 0:CY] = wall[...].astype(F32)

    def own_chunk(i, inner):
        x = i // 2
        part = pl.ds(pl.multiple_of((i % 2) * 8, 8), 8)
        states = [cells[q, x, part, 0:CY] for q in range(19)]
        wet = cells[19, x, part, 0:CY] < 0.5
        for q, value in enumerate(collide(states, wet)):
            post[q, x, part, 0:CY] = value
        return inner

    lax.fori_loop(0, 8, own_chunk, 0, unroll=4)

    def source(k):
        return post.at[k] if k < 19 else cells.at[19]

    for k in range(20):
        for j in range(2):
            t0 = source(k)[2 * j, 0:CZ, 0:CY]
            t1 = source(k)[2 * j + 1, 0:CZ, 0:CY]
            pack_u[k, j] = jnp.where(low, pltpu.roll(t1[8:16], 4, 0), t0[8:16])
            pack_d[k, j] = jnp.where(low, t0[0:8], pltpu.roll(t1[0:8], 4, 0))
    pl.semaphore_wait(barrier, len(peers))

    def halo(i, src, dst, peer):
        return pltpu.make_async_remote_copy(
            src_ref=src,
            dst_ref=dst,
            send_sem=halo_send.at[i],
            recv_sem=halo_recv.at[i],
            device_id=peer,
            device_id_type=MESH,
        )

    sends = [
        halo(0, pack_u, got_u, place(up, s)),
        halo(1, pack_d, got_d, place(down, s)),
    ]
    for copy in sends:
        copy.start()
    slot = lax.broadcasted_iota(jnp.int32, (64, 128), 1) // 4
    pl_val = jnp.ones((64, 128), F32)
    pr_val = jnp.ones((64, 128), F32)
    for k in range(20):
        f = source(k)[:, 0:CZ, 0:CY].reshape(64, 128)
        rolled = pltpu.roll(f, 4 * k, 1) if k else f
        pl_val = jnp.where(slot == k, rolled, pl_val)
        pr_val = jnp.where(slot == (k - 1) % 32, rolled, pr_val)
    pack_l[...] = pl_val.reshape(SX, CZ, CY)
    pack_r[...] = pr_val.reshape(SX, CZ, CY)

    top, bottom = pl.ds(8, 8), pl.ds(0, 8)
    more = [
        halo(2, pack_l, got_l, place(n, left)),
        halo(3, pack_r, got_r, place(n, right)),
        halo(4, pack_l.at[:, bottom, :], got_c.at[0], place(down, left)),
        halo(5, pack_l.at[:, top, :], got_c.at[1], place(up, left)),
        halo(6, pack_r.at[:, bottom, :], got_c.at[2], place(down, right)),
        halo(7, pack_r.at[:, top, :], got_c.at[3], place(up, right)),
    ]
    for copy in more:
        copy.start()
    sends += more

    for copy in fetches[2:8]:
        copy.wait()
    wb[0:64, 0:108] = v_lift[0].astype(F32)
    wb[64:128, 0:64] = v_mix[0].astype(F32)
    small[0:1, 0:64] = v_blift[...].astype(F32)
    small[1:2, 0:64] = v_bmix[...].astype(F32)
    small[2:3, 0:4] = v_bhead[...].astype(F32)
    small[4:8, 0:64] = v_head[0].astype(F32)
    row16 = lax.broadcasted_iota(jnp.int32, (16, 128), 0)
    lane16 = lax.broadcasted_iota(jnp.int32, (16, 128), 1)
    head_at = (row16 >= 4) & (row16 < 8)
    head_at = head_at & ((lane16 == row16 + 108) | (lane16 == row16 + 112))
    to_top = ((row16 == 0) & (lane16 == 108)) | head_at
    to_mix = (row16 == 1) & (lane16 == 64)
    to_head = (row16 == 2) & (lane16 == 64)
    rows = small[...].astype(BF16)

    def turned(mask):
        return dot(rows, mask.astype(F32).astype(BF16), TN)

    seat = lax.broadcasted_iota(jnp.int32, (16, 128), 1)
    first = row16 % 12
    held = (row16 < 4) | (row16 >= 12)
    picks = (held & (seat == first)).astype(F32).astype(BF16)
    seat4 = lax.broadcasted_iota(jnp.int32, (16, 16), 1)
    row4 = lax.broadcasted_iota(jnp.int32, (16, 16), 0)
    picks4 = (((row4 < 4) | (row4 >= 12)) & (seat4 == row4 % 12 + 4)).astype(F32).astype(BF16)
    wb[0:64] = wb[0:64] + turned(to_top)[0:64]
    wb[64:128] = wb[64:128] + turned(to_mix)[0:64]
    wb[128:144] = dot(picks4, rows) + dot(picks, turned(to_head).astype(BF16))
    mine = wb[...].astype(BF16)
    weights[s] = mine

    gathers = []
    for k, peer in enumerate(z_peers):
        gathers.append(
            pltpu.make_async_remote_copy(
                src_ref=weights.at[s],
                dst_ref=weights.at[s],
                send_sem=ag_send.at[k],
                recv_sem=ag_recv.at[k],
                device_id=place(n, peer),
                device_id_type=MESH,
            )
        )
    for copy in gathers:
        copy.start()

    def forward(i, owner):
        return pltpu.make_async_remote_copy(
            src_ref=weights.at[owner],
            dst_ref=weights.at[owner],
            send_sem=fw_send.at[i],
            recv_sem=fw_recv.at[i],
            device_id=place(n, sibling),
            device_id_type=MESH,
        )

    forwards = [forward(0, s)]
    forwards[0].start()

    fluid = (1 - wall[...]).astype(F32)
    before = features([cells[q, :, 0:CZ, 0:CY] for q in range(19)], fluid)
    for c in range(4):
        early[:, c] = before[c].astype(BF16)
    early[:, 4] = fluid.astype(BF16)
    for copy in fetches[8:]:
        copy.wait()

    ahead = lax.broadcasted_iota(jnp.int32, (128, 256), 0)
    ahead = ahead - lax.broadcasted_iota(jnp.int32, (128, 256), 1) % 16
    unit_row = (lax.broadcasted_iota(jnp.int32, (40, VOX), 0) == 0).astype(F32)

    def cut(field, count, crop, window):
        ox = anchors[0, 0, 0, crop]
        near = field[ox].reshape(count * CZ, 128)
        far = field[(ox + 1) % SX].reshape(count * CZ, 128)
        wide = dot(jnp.concatenate([near, far], axis=0), window)
        return (wide * spread[0 : count * CZ * 2]).astype(BF16)

    def early_pair(i, carry):
        parts = []
        for j in range(2):
            crop = 2 * i + j
            oy = anchors[0, 1, 0, crop] % CY
            window = (ahead == oy).astype(F32).astype(BF16)
            windows[crop] = window
            parts.append(cut(early, 5, crop, window))
        got = dot(select[...], jnp.concatenate(parts, axis=0))
        x8 = jnp.concatenate([got[0:8], got[8:16]], axis=1)
        wets[i] = jnp.concatenate([got[16:24], got[24:32]], axis=1)
        moved = []
        for dx, dz, dy in SHIFTS:
            shift = (-(dx * 256 + dz * 16 + dy)) % VOX
            moved.append(pltpu.roll(x8, shift, 1) if shift else x8)
        moved.append(unit_row)
        patches[i] = jnp.concatenate(moved, axis=0).astype(BF16) * inside[...]
        return carry

    lax.fori_loop(0, CROPS_DEV // 2, early_pair, 0)

    meanwhile()
    for copy in sends[2:]:
        copy.wait()

    low4 = jnp.broadcast_to(low[None], (SX, 8, 128))
    edge_l = jnp.concatenate([got_l[...], jnp.where(low4, got_c[0], got_c[1])], axis=1)
    edge_r = jnp.concatenate([got_r[...], jnp.where(low4, got_c[2], got_c[3])], axis=1)
    edge_l = edge_l.reshape(SX * EZ, 128)
    edge_r = edge_r.reshape(SX * EZ, 128)
    odd = (lax.broadcasted_iota(jnp.int32, (SX * EZ, 128), 1) // 4) % 2 == 1
    mixed = (jnp.where(odd, edge_r, edge_l), jnp.where(odd, edge_l, edge_r))
    for k in range(20):
        side = mixed[k % 2]
        if k:
            side = pltpu.roll(side, 128 - 4 * k, 1)
        source(k)[:, :, CY:EY] = side.reshape(SX, EZ, 128)
    for copy in sends[:2]:
        copy.wait()
    for k in range(20):
        for j in range(2):
            u, d = got_u[k, j], got_d[k, j]
            source(k)[2 * j, CZ:EZ, 0:CY] = jnp.where(low, d, u)
            source(k)[2 * j + 1, CZ:EZ, 0:CY] = pltpu.roll(jnp.where(low, u, d), 4, 0)

    def one_step(step, carry):
        def one_chunk(i, inner):
            x = i // 3
            part = pl.ds(pl.multiple_of((i % 3) * 8, 8), 8)
            states = [cells[q, x, part, :] for q in range(19)]
            wet = cells[19, x, part, :] < 0.5
            for q, value in enumerate(collide(states, wet)):
                post[q, x, part, :] = value
            return inner

        lax.fori_loop(0, 12, one_chunk, 0, unroll=6)
        move()
        return carry

    def move():
        def one_slab(x, inner):
            for q in range(19):
                cx, cy, cz = VELOCITY[q]
                slab = post[q, (x + SX - cx) % SX]
                if cz:
                    slab = pltpu.roll(slab, cz % EZ, 0)
                if cy:
                    slab = pltpu.roll(slab, cy % EY, 1)
                cells[q, x] = slab
            return inner

        lax.fori_loop(0, SX, one_slab, 0, unroll=4)

    move()
    one_step(1, 0)
    one_step(2, 0)
    for k in range(1, chips):
        gathers[k - 1].wait()
        owner = ((chip + chips - k) % chips) * 2 + core
        copy = forward(k, owner)
        copy.start()
        forwards.append(copy)
    one_step(3, 0)

    store = pltpu.make_async_copy(cells.at[0:19, :, 0:CZ, 0:CY], fin, fin_sem)
    store.start()
    final = [cells[q, :, 0:CZ, 0:CY] for q in range(19)]
    after = features(final, fluid)
    for c in range(4):
        late[:, c] = (after[c] - before[c]).astype(BF16)

    cuts = [cut(late, 4, crop, windows[crop]) for crop in range(CROPS_DEV)]
    for i in range(CROPS_DEV // 2):
        got = dot(choose[...], jnp.concatenate(cuts[2 * i : 2 * i + 2], axis=0))
        targets[i] = jnp.concatenate([got[0:8], got[8:16]], axis=1)
    for copy in forwards:
        copy.wait()
    return store


def gelu_both(x):
    c1, c2 = 0.7978845608028654, 0.7978845608028654 * 0.044715
    sq = x * x
    half = 0.5 * jnp.tanh(x * (c1 + c2 * sq)) + 0.5
    value = x * half
    slope = half + value * (1.0 - half) * (2.0 * c1 + 6.0 * c2 * sq)
    return value, slope


def constants():
    row = np.arange(160)
    lane = np.arange(256)
    spread = (lane[None, :] // 16 == row[:, None] % 16).astype(np.float32)
    select = np.zeros((32, 320), np.float32)
    choose = np.zeros((16, 256), np.float32)
    for xi in range(2):
        for i in range(8):
            crop, channel = i // 4, i % 4
            start = crop * 160 + xi * 80 + channel * 16
            select[xi * 8 + i, start : start + 16] = 1.0
            start = crop * 160 + xi * 80 + 64
            select[16 + xi * 8 + i, start : start + 16] = 1.0
            start = crop * 128 + xi * 64 + channel * 16
            choose[xi * 8 + i, start : start + 16] = 1.0
    expand = np.zeros((2, 128, 256), np.float32)
    for pos in range(2):
        for k in range(27):
            for c in range(4):
                expand[pos, 4 * k + c, 8 * k + 4 * pos + c] = 1.0
        expand[pos, 108, 216] = 1.0
    voxel = np.arange(VOX)
    vx, vz, vy = voxel // 256, voxel // 16 % 16, voxel % 16
    inside = np.ones((256, VOX), np.float32)
    for k, (dx, dz, dy) in enumerate(SHIFTS):
        good = (
            (vx + dx >= 0)
            & (vx + dx < 2)
            & (vz + dz >= 0)
            & (vz + dz < 16)
            & (vy + dy >= 0)
            & (vy + dy < 16)
        )
        inside[8 * k : 8 * k + 8] = good[None]
    return (
        (
            jnp.asarray(spread),
            jnp.asarray(select, BF16),
            jnp.asarray(choose, BF16),
            jnp.asarray(inside, BF16),
        ),
        (
            jnp.asarray(expand, BF16),
            jnp.asarray(np.transpose(expand, (0, 2, 1)), BF16),
        ),
    )


def train_part(
    ns,
    nn,
    trainers,
    patches_ref,
    targets,
    wets,
    wall_w,
    expand,
    shrink,
    out,
    crops,
    index,
    grads,
    pair,
    held,
    sent,
    parts,
    zparts,
    mine,
    whole,
    pair_send,
    pair_recv,
    rs_send,
    rs_recv,
    z_send,
    z_recv,
    ag_send,
    ag_recv,
):
    s = lax.axis_index("span")
    n = lax.axis_index("normal")
    chips = ns // 2
    chip = s // 2
    core = s % 2
    sibling = chip * 2 + (1 - core)
    rows = 128 // nn
    n_peers = normal_peers(n, nn)
    z_peers = [(chip + k) % chips for k in far_first(chips)]

    def at_span(other):
        return {"span": other, "normal": n}

    def at_normal(other):
        return {"span": s, "normal": other}

    crops[CROPS_DEV] = jnp.zeros((128, 128), F32)
    unit = (lax.broadcasted_iota(jnp.int32, (64, VOX), 0) == 0).astype(F32).astype(BF16)
    lane64 = lax.broadcasted_iota(jnp.int32, (64, 128), 1)
    lane128 = lax.broadcasted_iota(jnp.int32, (128, 128), 1)

    def one_group(g, carry):
        wide = range(GROUP)
        both = range(2)
        pairs = [g * GROUP + p for p in wide]
        mats = [[wall_w[trainers[0, 0, 0, 2 * i + j]] for j in both] for i in pairs]
        patches = [patches_ref[i] for i in pairs]
        lift = [[dot(mats[p][j][0:64], expand[j]) for j in both] for p in wide]
        lift = [jnp.concatenate(lift[p], axis=0).astype(BF16) for p in wide]
        z1 = [dot(lift[p], patches[p]) for p in wide]
        h1, slope1 = [], []
        for p in wide:
            value, slope = gelu_both(z1[p])
            h1.append(value.astype(BF16))
            slope1.append(slope)
        own = [[h1[p][64 * j : 64 * j + 64] for j in both] for p in wide]
        ext1 = [[jnp.concatenate([own[p][j], unit], axis=0) for j in both] for p in wide]
        z2 = [[dot(mats[p][j][64:128], ext1[p][j]) for j in both] for p in wide]
        ext2 = [[None, None] for p in wide]
        slope2 = [[None, None] for p in wide]
        for p in wide:
            for j in both:
                value, slope2[p][j] = gelu_both(z2[p][j])
                h2 = (own[p][j].astype(F32) + value).astype(BF16)
                ext2[p][j] = jnp.concatenate([h2, unit], axis=0)
        pred = [
            [dot(mats[p][j][128:144], ext2[p][j])[8 * j : 8 * j + 8] for j in both] for p in wide
        ]
        errors = []
        for p in wide:
            missed = pred[p][0] + pred[p][1] - targets[pairs[p]]
            weighted = wets[pairs[p]] * missed
            loss8 = weighted * missed * (1.0 / (4.0 * VOX))
            dpred = weighted * (2.0 / (4.0 * VOX))
            tail = jnp.concatenate([dpred, loss8], axis=0).astype(BF16)
            errors.append(jnp.concatenate([jnp.zeros((112, VOX), BF16), tail], axis=0))
        head = [
            [jnp.where(keeps[j], mats[p][j][0:64].astype(F32), 0.0).astype(BF16) for j in both]
            for p in wide
        ]
        dh2 = [[dot(head[p][j], errors[p]) for j in both] for p in wide]
        dz2 = [[(dh2[p][j] * slope2[p][j]).astype(BF16) for j in both] for p in wide]
        back = [[dot(mats[p][j][64:128, 0:64], dz2[p][j], TN) for j in both] for p in wide]
        dh1 = [jnp.concatenate([dh2[p][j] + back[p][j] for j in both], axis=0) for p in wide]
        dz1 = [(dh1[p] * slope1[p]).astype(BF16) for p in wide]
        lifted = [dot(dz1[p], patches[p], NT).astype(BF16) for p in wide]
        mixed = [[dot(dz2[p][j], ext1[p][j], NT) for j in both] for p in wide]
        heads = [[dot(ext2[p][j], errors[p], NT) for j in both] for p in wide]
        less = [[dot(lifted[p][64 * j : 64 * j + 64], shrink[j]) for j in both] for p in wide]
        for p in wide:
            for j in both:
                mine_only = jnp.where(owned[j], heads[p][j], 0.0)
                upper = (less[p][j] + mine_only[0:64]).astype(BF16).astype(F32)
                lower = mixed[p][j] + mine_only[64:128]
                lower = jnp.where(lane64 < 64, lower.astype(BF16).astype(F32), lower)
                crops[2 * pairs[p] + j, 0:64] = upper
                crops[2 * pairs[p] + j, 64:128] = lower
        return carry

    keeps = [(lane64 >= 112 + 4 * j) & (lane64 < 116 + 4 * j) for j in range(2)]
    owned = [(lane128 // 4) % 2 == j for j in range(2)]
    lax.fori_loop(0, CROPS_DEV // 2 // GROUP, one_group, 0)

    def member(m):
        return crops[index[m, 0]] + crops[index[m, 1]]

    def theirs(z, carry):
        grads[z] = member(2 * z + 1 - core).astype(BF16)
        return carry

    lax.fori_loop(0, chips, theirs, 0, unroll=chips)

    def remote(src, dst, send, recv, peer):
        copy = pltpu.make_async_remote_copy(
            src_ref=src,
            dst_ref=dst,
            send_sem=send,
            recv_sem=recv,
            device_id=peer,
            device_id_type=MESH,
        )
        copy.start()
        return copy

    first = remote(grads, pair, pair_send.at[0], pair_recv.at[0], at_span(sibling))

    def ours(z, carry):
        held[z] = member(2 * z + core)
        return carry

    lax.fori_loop(0, chips, ours, 0, unroll=chips)
    first.wait()
    for z in range(0, chips, 2):
        two = [held[z + i] + pair[z + i].astype(F32) for i in range(2)]
        two = jnp.concatenate([v.reshape(nn, rows, 128) for v in two], axis=1)
        sent[:, z * rows : (z + 2) * rows, :] = two.astype(BF16)
    seconds = []
    for k, other in enumerate(n_peers):
        seconds.append(
            remote(sent.at[other], parts.at[k], rs_send.at[k], rs_recv.at[k], at_normal(other))
        )
    own = sent[n].astype(F32)
    for k in range(nn - 1):
        seconds[k].wait()
        own = own + parts[k].astype(F32)
    mine[...] = own.reshape(chips, rows, 128)
    thirds = []
    for k, other in enumerate(z_peers):
        thirds.append(
            remote(
                mine.at[other],
                zparts.at[k],
                z_send.at[k],
                z_recv.at[k],
                at_span(other * 2 + core),
            )
        )
    total = mine[chip]
    for k in range(chips - 1):
        thirds[k].wait()
        total = total + zparts[k]
    whole[n] = total * (1.0 / (CROPS_DEV * nn))
    fourths = []
    for k, other in enumerate(n_peers):
        fourths.append(
            remote(
                whole.at[n], whole.at[n], ag_send.at[k], ag_recv.at[k], at_normal(other)
            )
        )
    for copy in fourths:
        copy.wait()
    out[...] = whole[...]


def far_first(count):
    return sorted(range(1, count), key=lambda k: -min(k, count - k))


def normal_peers(n, nn):
    if nn != 16:
        return [(n + k) % nn for k in range(1, nn)]
    moves = [(i, j) for i in range(4) for j in range(4) if i or j]
    moves.sort(key=lambda m: -(min(m[0], 4 - m[0]) + min(m[1], 4 - m[1])))
    return [(n // 4 + i) % 4 * 4 + (n % 4 + j) % 4 for i, j in moves]


def fused_kernel(ns, nn, *refs):
    (
        pop,
        wall,
        w_lift,
        b_lift,
        w_mix,
        b_mix,
        w_head,
        b_head,
        anchors,
        trainers,
        spread,
        select,
        choose,
        inside,
        expand,
        shrink,
        fin,
        total,
    ) = refs[:18]
    fin_sem, v_trainers, v_expand, v_shrink, patches, targets, wets, weights = refs[18:26]
    lattice_refs, train_refs = refs[26:61], refs[61:]
    n = lax.axis_index("normal")
    n_peers = normal_peers(n, nn)
    def meanwhile():
        def remember(m, carry):
            last, before = jnp.int32(CROPS_DEV), jnp.int32(CROPS_DEV)
            for c in range(CROPS_DEV):
                match = v_trainers[0, 0, 0, c] == m
                before = jnp.where(match, last, before)
                last = jnp.where(match, c, last)
            train_refs[1][m, 0] = last
            train_refs[1][m, 1] = before
            return carry

        lax.fori_loop(0, ns, remember, 0)

    store = lattice_part(
        ns,
        nn,
        pop,
        wall,
        w_lift,
        b_lift,
        w_mix,
        b_mix,
        w_head,
        b_head,
        anchors,
        spread,
        select,
        choose,
        inside,
        ((trainers, v_trainers), (expand, v_expand), (shrink, v_shrink)),
        n_peers,
        meanwhile,
        fin,
        fin_sem,
        patches,
        targets,
        wets,
        *lattice_refs[:26],
        weights,
        *lattice_refs[26:],
    )
    train_part(
        ns,
        nn,
        v_trainers,
        patches,
        targets,
        wets,
        weights,
        v_expand,
        v_shrink,
        total,
        *train_refs,
    )
    store.wait()


def unpack_kernel(fin, total, *refs):
    outs, stages, sems = refs[:8], refs[8:15], refs[15]
    o_lift, o_blift, o_mix, o_bmix, o_head, o_bhead, o_loss = stages

    def hop(i, src, dst):
        copy = pltpu.make_async_copy(src, dst, sems.at[i])
        copy.start()
        return copy

    writes = [hop(0, fin, outs[0])]
    whole = total[...].reshape(128, 128)
    turned = whole.T
    o_lift[0] = whole[0:64, 0:108]
    o_mix[0] = whole[64:128, 0:64]
    o_blift[...] = turned[108:109, 0:64]
    o_bmix[...] = turned[64:65, 64:128]
    heads = turned[112:120, 0:64]
    o_head[0] = heads[0:4] + heads[4:8]
    line = whole[64:65]
    o_bhead[...] = line[:, 112:116] + line[:, 116:120]
    lane = lax.broadcasted_iota(jnp.int32, (1, 128), 1)
    o_loss[...] = jnp.sum(jnp.where(lane >= 120, line, 0.0), axis=1, keepdims=True)
    writes += [hop(1 + i, stages[i], outs[1 + i]) for i in range(7)]
    for copy in writes:
        copy.wait()


def local(
    populations, wall_mask, crop_anchors, trainers, w_lift, b_lift, w_mix, b_mix, w_head, b_head
):
    ns, nn = lax.axis_size("span"), lax.axis_size("normal")
    chips = ns // 2
    pairs = CROPS_DEV // 2
    vmem = pl.BlockSpec(memory_space=pltpu.VMEM)
    hbm = pl.BlockSpec(memory_space=pltpu.HBM)
    dma = pltpu.SemaphoreType.DMA
    shape = jax.ShapeDtypeStruct
    cutting, weighing = constants()
    spread, select, choose, inside = cutting
    edge = pltpu.VMEM((SX, CZ, CY), F32)
    flat = pltpu.VMEM((20, 2, 8, 128), F32)
    rows = 128 // nn
    final, total = pl.pallas_call(
        functools.partial(fused_kernel, ns, nn),
        out_shape=(pltpu.VMEM((19, SX, CZ, CY), F32), pltpu.VMEM((nn, rows, 128), F32)),
        in_specs=[hbm] * 16,
        out_specs=(vmem, vmem),
        scratch_shapes=[
            dma,
            pltpu.SMEM((1, 1, 1, CROPS_DEV), jnp.int32),
            pltpu.VMEM((2, 128, 256), BF16),
            pltpu.VMEM((2, 256, 128), BF16),
            pltpu.VMEM((pairs, 256, VOX), BF16),
            pltpu.VMEM((pairs, 8, VOX), F32),
            pltpu.VMEM((pairs, 8, VOX), F32),
            pltpu.VMEM((ns, 144, 128), BF16),
            pltpu.VMEM((SX, CZ, CY), jnp.int32),
            pltpu.VMEM(w_lift.shape, BF16),
            pltpu.VMEM(b_lift.shape, BF16),
            pltpu.VMEM(w_mix.shape, BF16),
            pltpu.VMEM(b_mix.shape, BF16),
            pltpu.VMEM(w_head.shape, BF16),
            pltpu.VMEM(b_head.shape, BF16),
            pltpu.SMEM((1, 3, 1, CROPS_DEV), jnp.int32),
            pltpu.VMEM(spread.shape, F32),
            pltpu.VMEM(select.shape, BF16),
            pltpu.VMEM(choose.shape, BF16),
            pltpu.VMEM(inside.shape, BF16),
            pltpu.VMEM((144, 128), F32),
            pltpu.VMEM((16, 128), F32),
            pltpu.VMEM((SX, 5, CZ, CY), BF16),
            pltpu.VMEM((SX, 4, CZ, CY), BF16),
            pltpu.VMEM((CROPS_DEV, 128, 256), BF16),
            edge,
            edge,
            flat,
            flat,
            edge,
            edge,
            flat,
            flat,
            pltpu.VMEM((4, SX, 8, 128), F32),
            pltpu.VMEM((20, SX, EZ, EY), F32),
            pltpu.VMEM((19, SX, EZ, EY), F32),
            dma((16,)),
            dma((8,)),
            dma((8,)),
            dma((chips,)),
            dma((chips,)),
            dma((chips,)),
            dma((chips,)),
            pltpu.VMEM((CROPS_DEV + 1, 128, 128), F32),
            pltpu.SMEM((ns, 2), jnp.int32),
            pltpu.VMEM((chips, 128, 128), BF16),
            pltpu.VMEM((chips, 128, 128), BF16),
            pltpu.VMEM((chips, 128, 128), F32),
            pltpu.VMEM((nn, chips * rows, 128), BF16),
            pltpu.VMEM((nn - 1, chips * rows, 128), BF16),
            pltpu.VMEM((chips - 1, rows, 128), F32),
            pltpu.VMEM((chips, rows, 128), F32),
            pltpu.VMEM((nn, rows, 128), F32),
            dma((1,)),
            dma((1,)),
            dma((nn - 1,)),
            dma((nn - 1,)),
            dma((chips - 1,)),
            dma((chips - 1,)),
            dma((nn - 1,)),
            dma((nn - 1,)),
        ],
        compiler_params=pltpu.CompilerParams(
            collective_id=0, has_side_effects=True, vmem_limit_bytes=60 << 20
        ),
        name="channel",
    )(
        populations,
        wall_mask,
        w_lift,
        b_lift,
        w_mix,
        b_mix,
        w_head,
        b_head,
        jnp.transpose(crop_anchors, (0, 3, 1, 2)),
        jnp.swapaxes(trainers, 2, 3),
        spread,
        select,
        choose,
        inside,
        *weighing,
    )
    small = [
        shape(w_lift.shape, F32),
        shape(b_lift.shape, F32),
        shape(w_mix.shape, F32),
        shape(b_mix.shape, F32),
        shape(w_head.shape, F32),
        shape(b_head.shape, F32),
        shape((1, 1), F32),
    ]
    outs = pl.pallas_call(
        unpack_kernel,
        out_shape=[shape(populations.shape, F32)] + small,
        in_specs=[vmem, vmem],
        out_specs=[hbm] * 8,
        scratch_shapes=[pltpu.VMEM(leaf.shape, F32) for leaf in small] + [dma((8,))],
        compiler_params=pltpu.CompilerParams(vmem_limit_bytes=4 << 20),
        name="unpack",
    )(final, total)
    return tuple(outs[:7]) + (outs[7].reshape(1),)


def solution(mesh):
    return jax.shard_map(
        local,
        mesh=mesh,
        in_specs=(
            P(None, None, "normal", "span"),
            P(None, "normal", "span"),
            P("normal", "span", None, None),
            P("normal", "span", None, None),
            P("span", None, None),
            P("span", None),
            P("span", None, None),
            P("span", None),
            P("span", None, None),
            P("span", None),
        ),
        out_specs=(
            P(None, None, "normal", "span"),
            P("span", None, None),
            P("span", None),
            P("span", None, None),
            P("span", None),
            P("span", None, None),
            P("span", None),
            P("span"),
        ),
        check_vma=False,
    )
```

```python
import functools

import jax
import jax.numpy as jnp
import numpy as np
from jax import lax
from jax.experimental import pallas as pl
from jax.experimental.pallas import tpu as pltpu
from jax.sharding import PartitionSpec as P

STEPS = 4
CROPS_DEV = 12
GROUP = 6
SX, CZ, CY = 4, 16, 128
EZ, EY = 24, 256
HID = 64
VOX = 512

VELOCITY = (
    (0, 0, 0),
    (1, 0, 0),
    (-1, 0, 0),
    (0, 1, 0),
    (0, -1, 0),
    (0, 0, 1),
    (0, 0, -1),
    (1, 1, 0),
    (-1, -1, 0),
    (1, -1, 0),
    (-1, 1, 0),
    (1, 0, 1),
    (-1, 0, -1),
    (1, 0, -1),
    (-1, 0, 1),
    (0, 1, 1),
    (0, -1, -1),
    (0, 1, -1),
    (0, -1, 1),
)
WEIGHTS = (1.0 / 3.0,) + (1.0 / 18.0,) * 6 + (1.0 / 36.0,) * 12
OPPOSITE = (0, 2, 1, 4, 3, 6, 5, 8, 7, 10, 9, 12, 11, 14, 13, 16, 15, 18, 17)
OMEGA = 1.25
SCALE_DENSITY = 50.0
SCALE_FLOW = 30.0
F32 = jnp.float32
BF16 = jnp.bfloat16
MESH = pl.DeviceIdType.MESH


def signed_sum(entries, factors):
    running = None
    for entry, factor in zip(entries, factors):
        if factor == 0:
            continue
        if running is None:
            running = entry if factor > 0 else -entry
        else:
            running = running + entry if factor > 0 else running - entry
    return running


def moments(states):
    density = states[0]
    for number in range(1, 19):
        density = density + states[number]
    inverse = 1.0 / density
    flows = []
    for axis_id in range(3):
        summed = signed_sum(states, [VELOCITY[number][axis_id] for number in range(19)])
        flows.append(summed * inverse)
    return (density, flows[0], flows[1], flows[2])


def collide(states, wet_cells):
    density, flow_x, flow_y, flow_z = moments(states)
    flows = (flow_x, flow_y, flow_z)
    speed_sq = flow_x * flow_x + flow_y * flow_y + flow_z * flow_z
    base = 1.0 - 1.5 * speed_sq
    result = [None] * 19
    kept = 1.0 - OMEGA
    scaled = {w: (OMEGA * w) * density for w in set(WEIGHTS)}
    relaxed = kept * states[0] + scaled[WEIGHTS[0]] * base
    result[0] = jnp.where(wet_cells, relaxed, states[0])
    for number in range(1, 19, 2):
        other = OPPOSITE[number]
        along = signed_sum(flows, VELOCITY[number])
        weight = scaled[WEIGHTS[number]]
        even = weight * (base + (4.5 * along) * along)
        odd = weight * (3.0 * along)
        forth = kept * states[number] + (even + odd)
        back = kept * states[other] + (even - odd)
        result[number] = jnp.where(wet_cells, forth, states[other])
        result[other] = jnp.where(wet_cells, back, states[number])
    return result


def features(states, fluid):
    density, flow_x, flow_y, flow_z = moments(states)
    return [
        (density - 1.0) * SCALE_DENSITY * fluid,
        flow_x * SCALE_FLOW * fluid,
        flow_y * SCALE_FLOW * fluid,
        flow_z * SCALE_FLOW * fluid,
    ]


NT = (((1,), (1,)), ((), ()))
TN = (((0,), (0,)), ((), ()))


def dot(a, b, dims=(((1,), (0,)), ((), ()))):
    return lax.dot_general(a, b, dims, preferred_element_type=F32)


SHIFTS = [(a, b, c) for a in (-1, 0, 1) for b in (-1, 0, 1) for c in (-1, 0, 1)]


def lattice_part(
    ns,
    nn,
    pop_hbm,
    wall_hbm,
    w_lift,
    b_lift,
    w_mix,
    b_mix,
    w_head,
    b_head,
    anchors_hbm,
    spread_hbm,
    select_hbm,
    choose_hbm,
    inside_hbm,
    more_fetches,
    n_peers,
    meanwhile,
    fin,
    fin_sem,
    patches,
    targets,
    wets,
    wall,
    v_lift,
    v_blift,
    v_mix,
    v_bmix,
    v_head,
    v_bhead,
    anchors,
    spread,
    select,
    choose,
    inside,
    wb,
    small,
    early,
    late,
    windows,
    pack_l,
    pack_r,
    pack_u,
    pack_d,
    got_l,
    got_r,
    got_u,
    got_d,
    got_c,
    weights,
    cells,
    post,
    loads,
    halo_send,
    halo_recv,
    ag_send,
    ag_recv,
    fw_send,
    fw_recv,
):
    s = lax.axis_index("span")
    n = lax.axis_index("normal")
    chips = ns // 2
    chip = s // 2
    core = s % 2
    right, left = (s + 1) % ns, (s + ns - 1) % ns
    up, down = (n + 1) % nn, (n + nn - 1) % nn
    sibling = chip * 2 + (1 - core)

    def place(nn_, ss_):
        return {"normal": nn_, "span": ss_}

    fetches = [
        pltpu.make_async_copy(src, dst, loads.at[i])
        for i, (src, dst) in enumerate(
            (
                (pop_hbm, cells.at[0:19, :, 0:CZ, 0:CY]),
                (wall_hbm, wall),
                (w_lift, v_lift),
                (b_lift, v_blift),
                (w_mix, v_mix),
                (b_mix, v_bmix),
                (w_head, v_head),
                (b_head, v_bhead),
                (anchors_hbm, anchors),
                (spread_hbm, spread),
                (select_hbm, select),
                (choose_hbm, choose),
                (inside_hbm, inside),
                *more_fetches,
            )
        )
    ]
    z_peers = [((chip + k) % chips) * 2 + core for k in range(1, chips)]
    far_z = [((chip + k) % chips) * 2 + core for k in far_first(chips)]
    peers = [place(n, peer) for peer in far_z]
    peers += [place(other, s) for other in n_peers]
    peers += [
        place(up, right),
        place(up, left),
        place(down, right),
        place(down, left),
        place(n, right),
        place(n, left),
        place(n, sibling),
    ]
    barrier = pltpu.get_barrier_semaphore()
    for peer in peers:
        pl.semaphore_signal(barrier, inc=1, device_id=peer, device_id_type=MESH)
    for copy in fetches:
        copy.start()

    sub = lax.broadcasted_iota(jnp.int32, (8, 128), 0)
    low = sub < 4
    wb[...] = jnp.zeros((144, 128), F32)
    small[...] = jnp.zeros((16, 128), F32)
    fetches[0].wait()
    fetches[1].wait()
    cells[19, :, 0:CZ, 0:CY] = wall[...].astype(F32)

    def own_chunk(i, inner):
        x = i // 2
        part = pl.ds(pl.multiple_of((i % 2) * 8, 8), 8)
        states = [cells[q, x, part, 0:CY] for q in range(19)]
        wet = cells[19, x, part, 0:CY] < 0.5
        for q, value in enumerate(collide(states, wet)):
            post[q, x, part, 0:CY] = value
        return inner

    lax.fori_loop(0, 8, own_chunk, 0, unroll=4)

    def source(k):
        return post.at[k] if k < 19 else cells.at[19]

    for k in range(20):
        for j in range(2):
            t0 = source(k)[2 * j, 0:CZ, 0:CY]
            t1 = source(k)[2 * j + 1, 0:CZ, 0:CY]
            pack_u[k, j] = jnp.where(low, pltpu.roll(t1[8:16], 4, 0), t0[8:16])
            pack_d[k, j] = jnp.where(low, t0[0:8], pltpu.roll(t1[0:8], 4, 0))
    pl.semaphore_wait(barrier, len(peers))

    def halo(i, src, dst, peer):
        return pltpu.make_async_remote_copy(
            src_ref=src,
            dst_ref=dst,
            send_sem=halo_send.at[i],
            recv_sem=halo_recv.at[i],
            device_id=peer,
            device_id_type=MESH,
        )

    sends = [
        halo(0, pack_u, got_u, place(up, s)),
        halo(1, pack_d, got_d, place(down, s)),
    ]
    for copy in sends:
        copy.start()
    slot = lax.broadcasted_iota(jnp.int32, (64, 128), 1) // 4
    pl_val = jnp.ones((64, 128), F32)
    pr_val = jnp.ones((64, 128), F32)
    for k in range(20):
        f = source(k)[:, 0:CZ, 0:CY].reshape(64, 128)
        rolled = pltpu.roll(f, 4 * k, 1) if k else f
        pl_val = jnp.where(slot == k, rolled, pl_val)
        pr_val = jnp.where(slot == (k - 1) % 32, rolled, pr_val)
    pack_l[...] = pl_val.reshape(SX, CZ, CY)
    pack_r[...] = pr_val.reshape(SX, CZ, CY)

    top, bottom = pl.ds(8, 8), pl.ds(0, 8)
    more = [
        halo(2, pack_l, got_l, place(n, left)),
        halo(3, pack_r, got_r, place(n, right)),
        halo(4, pack_l.at[:, bottom, :], got_c.at[0], place(down, left)),
        halo(5, pack_l.at[:, top, :], got_c.at[1], place(up, left)),
        halo(6, pack_r.at[:, bottom, :], got_c.at[2], place(down, right)),
        halo(7, pack_r.at[:, top, :], got_c.at[3], place(up, right)),
    ]
    for copy in more:
        copy.start()
    sends += more

    for copy in fetches[2:8]:
        copy.wait()
    wb[0:64, 0:108] = v_lift[0].astype(F32)
    wb[64:128, 0:64] = v_mix[0].astype(F32)
    small[0:1, 0:64] = v_blift[...].astype(F32)
    small[1:2, 0:64] = v_bmix[...].astype(F32)
    small[2:3, 0:4] = v_bhead[...].astype(F32)
    small[4:8, 0:64] = v_head[0].astype(F32)
    row16 = lax.broadcasted_iota(jnp.int32, (16, 128), 0)
    lane16 = lax.broadcasted_iota(jnp.int32, (16, 128), 1)
    head_at = (row16 >= 4) & (row16 < 8)
    head_at = head_at & ((lane16 == row16 + 108) | (lane16 == row16 + 112))
    to_top = ((row16 == 0) & (lane16 == 108)) | head_at
    to_mix = (row16 == 1) & (lane16 == 64)
    to_head = (row16 == 2) & (lane16 == 64)
    rows = small[...].astype(BF16)

    def turned(mask):
        return dot(rows, mask.astype(F32).astype(BF16), TN)

    seat = lax.broadcasted_iota(jnp.int32, (16, 128), 1)
    first = row16 % 12
    held = (row16 < 4) | (row16 >= 12)
    picks = (held & (seat == first)).astype(F32).astype(BF16)
    seat4 = lax.broadcasted_iota(jnp.int32, (16, 16), 1)
    row4 = lax.broadcasted_iota(jnp.int32, (16, 16), 0)
    picks4 = (((row4 < 4) | (row4 >= 12)) & (seat4 == row4 % 12 + 4)).astype(F32).astype(BF16)
    wb[0:64] = wb[0:64] + turned(to_top)[0:64]
    wb[64:128] = wb[64:128] + turned(to_mix)[0:64]
    wb[128:144] = dot(picks4, rows) + dot(picks, turned(to_head).astype(BF16))
    mine = wb[...].astype(BF16)
    weights[s] = mine

    gathers = []
    for k, peer in enumerate(z_peers):
        gathers.append(
            pltpu.make_async_remote_copy(
                src_ref=weights.at[s],
                dst_ref=weights.at[s],
                send_sem=ag_send.at[k],
                recv_sem=ag_recv.at[k],
                device_id=place(n, peer),
                device_id_type=MESH,
            )
        )
    for copy in gathers:
        copy.start()

    def forward(i, owner):
        return pltpu.make_async_remote_copy(
            src_ref=weights.at[owner],
            dst_ref=weights.at[owner],
            send_sem=fw_send.at[i],
            recv_sem=fw_recv.at[i],
            device_id=place(n, sibling),
            device_id_type=MESH,
        )

    forwards = [forward(0, s)]
    forwards[0].start()

    fluid = (1 - wall[...]).astype(F32)
    before = features([cells[q, :, 0:CZ, 0:CY] for q in range(19)], fluid)
    for c in range(4):
        early[:, c] = before[c].astype(BF16)
    early[:, 4] = fluid.astype(BF16)
    for copy in fetches[8:]:
        copy.wait()

    ahead = lax.broadcasted_iota(jnp.int32, (128, 256), 0)
    ahead = ahead - lax.broadcasted_iota(jnp.int32, (128, 256), 1) % 16
    unit_row = (lax.broadcasted_iota(jnp.int32, (40, VOX), 0) == 0).astype(F32)

    def cut(field, count, crop, window):
        ox = anchors[0, 0, 0, crop]
        near = field[ox].reshape(count * CZ, 128)
        far = field[(ox + 1) % SX].reshape(count * CZ, 128)
        wide = dot(jnp.concatenate([near, far], axis=0), window)
        return (wide * spread[0 : count * CZ * 2]).astype(BF16)

    def early_pair(i, carry):
        parts = []
        for j in range(2):
            crop = 2 * i + j
            oy = anchors[0, 1, 0, crop] % CY
            window = (ahead == oy).astype(F32).astype(BF16)
            windows[crop] = window
            parts.append(cut(early, 5, crop, window))
        got = dot(select[...], jnp.concatenate(parts, axis=0))
        x8 = jnp.concatenate([got[0:8], got[8:16]], axis=1)
        wets[i] = jnp.concatenate([got[16:24], got[24:32]], axis=1)
        moved = []
        for dx, dz, dy in SHIFTS:
            shift = (-(dx * 256 + dz * 16 + dy)) % VOX
            moved.append(pltpu.roll(x8, shift, 1) if shift else x8)
        moved.append(unit_row)
        patches[i] = jnp.concatenate(moved, axis=0).astype(BF16) * inside[...]
        return carry

    lax.fori_loop(0, CROPS_DEV // 2, early_pair, 0)

    meanwhile()
    for copy in sends[2:]:
        copy.wait()

    low4 = jnp.broadcast_to(low[None], (SX, 8, 128))
    edge_l = jnp.concatenate([got_l[...], jnp.where(low4, got_c[0], got_c[1])], axis=1)
    edge_r = jnp.concatenate([got_r[...], jnp.where(low4, got_c[2], got_c[3])], axis=1)
    edge_l = edge_l.reshape(SX * EZ, 128)
    edge_r = edge_r.reshape(SX * EZ, 128)
    odd = (lax.broadcasted_iota(jnp.int32, (SX * EZ, 128), 1) // 4) % 2 == 1
    mixed = (jnp.where(odd, edge_r, edge_l), jnp.where(odd, edge_l, edge_r))
    for k in range(20):
        side = mixed[k % 2]
        if k:
            side = pltpu.roll(side, 128 - 4 * k, 1)
        source(k)[:, :, CY:EY] = side.reshape(SX, EZ, 128)
    for copy in sends[:2]:
        copy.wait()
    for k in range(20):
        for j in range(2):
            u, d = got_u[k, j], got_d[k, j]
            source(k)[2 * j, CZ:EZ, 0:CY] = jnp.where(low, d, u)
            source(k)[2 * j + 1, CZ:EZ, 0:CY] = pltpu.roll(jnp.where(low, u, d), 4, 0)

    def one_step(step, carry, last=False):
        def one_chunk(i, inner):
            x = i // 3
            part = pl.ds(pl.multiple_of((i % 3) * 8, 8), 8)
            states = [cells[q, x, part, :] for q in range(19)]
            wet = cells[19, x, part, :] < 0.5
            for q, value in enumerate(collide(states, wet)):
                post[q, x, part, :] = value
            return inner

        lax.fori_loop(0, 12, one_chunk, 0, unroll=6)
        move(last)
        return carry

    def move(last=False):
        def one_slab(x, inner):
            for q in range(19):
                cx, cy, cz = VELOCITY[q]
                slab = post[q, (x + SX - cx) % SX]
                if cz:
                    slab = pltpu.roll(slab, cz % EZ, 0)
                if cy:
                    slab = pltpu.roll(slab, cy % EY, 1)
                if last:
                    fin[q, x] = slab[0:CZ, 0:CY]
                else:
                    cells[q, x] = slab
            return inner

        lax.fori_loop(0, SX, one_slab, 0, unroll=4)

    move()
    one_step(1, 0)
    one_step(2, 0)
    for k in range(1, chips):
        gathers[k - 1].wait()
        owner = ((chip + chips - k) % chips) * 2 + core
        copy = forward(k, owner)
        copy.start()
        forwards.append(copy)
    one_step(3, 0, True)

    final = [fin[q] for q in range(19)]
    after = features(final, fluid)
    for c in range(4):
        late[:, c] = (after[c] - before[c]).astype(BF16)

    cuts = [cut(late, 4, crop, windows[crop]) for crop in range(CROPS_DEV)]
    for i in range(CROPS_DEV // 2):
        got = dot(choose[...], jnp.concatenate(cuts[2 * i : 2 * i + 2], axis=0))
        targets[i] = jnp.concatenate([got[0:8], got[8:16]], axis=1)
    for copy in forwards:
        copy.wait()


def gelu_both(x):
    c1, c2 = 0.7978845608028654, 0.7978845608028654 * 0.044715
    sq = x * x
    half = 0.5 * jnp.tanh(x * (c1 + c2 * sq)) + 0.5
    value = x * half
    slope = half + value * (1.0 - half) * (2.0 * c1 + 6.0 * c2 * sq)
    return value, slope


def constants():
    row = np.arange(160)
    lane = np.arange(256)
    spread = (lane[None, :] // 16 == row[:, None] % 16).astype(np.float32)
    select = np.zeros((32, 320), np.float32)
    choose = np.zeros((16, 256), np.float32)
    for xi in range(2):
        for i in range(8):
            crop, channel = i // 4, i % 4
            start = crop * 160 + xi * 80 + channel * 16
            select[xi * 8 + i, start : start + 16] = 1.0
            start = crop * 160 + xi * 80 + 64
            select[16 + xi * 8 + i, start : start + 16] = 1.0
            start = crop * 128 + xi * 64 + channel * 16
            choose[xi * 8 + i, start : start + 16] = 1.0
    expand = np.zeros((2, 128, 256), np.float32)
    for pos in range(2):
        for k in range(27):
            for c in range(4):
                expand[pos, 4 * k + c, 8 * k + 4 * pos + c] = 1.0
        expand[pos, 108, 216] = 1.0
    voxel = np.arange(VOX)
    vx, vz, vy = voxel // 256, voxel // 16 % 16, voxel % 16
    inside = np.ones((256, VOX), np.float32)
    for k, (dx, dz, dy) in enumerate(SHIFTS):
        good = (
            (vx + dx >= 0)
            & (vx + dx < 2)
            & (vz + dz >= 0)
            & (vz + dz < 16)
            & (vy + dy >= 0)
            & (vy + dy < 16)
        )
        inside[8 * k : 8 * k + 8] = good[None]
    return (
        (
            jnp.asarray(spread),
            jnp.asarray(select, BF16),
            jnp.asarray(choose, BF16),
            jnp.asarray(inside, BF16),
        ),
        (
            jnp.asarray(expand, BF16),
            jnp.asarray(np.transpose(expand, (0, 2, 1)), BF16),
        ),
    )


def train_part(
    ns,
    nn,
    trainers,
    patches_ref,
    targets,
    wets,
    wall_w,
    expand,
    shrink,
    out,
    crops,
    index,
    grads,
    pair,
    held,
    sent,
    parts,
    zparts,
    mine,
    whole,
    pair_send,
    pair_recv,
    rs_send,
    rs_recv,
    z_send,
    z_recv,
    ag_send,
    ag_recv,
):
    s = lax.axis_index("span")
    n = lax.axis_index("normal")
    chips = ns // 2
    chip = s // 2
    core = s % 2
    sibling = chip * 2 + (1 - core)
    rows = 128 // nn
    n_peers = normal_peers(n, nn)
    z_peers = [(chip + k) % chips for k in far_first(chips)]

    def at_span(other):
        return {"span": other, "normal": n}

    def at_normal(other):
        return {"span": s, "normal": other}

    crops[CROPS_DEV] = jnp.zeros((128, 128), F32)
    unit = (lax.broadcasted_iota(jnp.int32, (64, VOX), 0) == 0).astype(F32).astype(BF16)
    lane64 = lax.broadcasted_iota(jnp.int32, (64, 128), 1)
    lane128 = lax.broadcasted_iota(jnp.int32, (128, 128), 1)

    def one_group(g, carry):
        wide = range(GROUP)
        both = range(2)
        pairs = [g * GROUP + p for p in wide]
        mats = [[wall_w[trainers[0, 0, 0, 2 * i + j]] for j in both] for i in pairs]
        patches = [patches_ref[i] for i in pairs]
        lift = [[dot(mats[p][j][0:64], expand[j]) for j in both] for p in wide]
        lift = [jnp.concatenate(lift[p], axis=0).astype(BF16) for p in wide]
        z1 = [dot(lift[p], patches[p]) for p in wide]
        h1, slope1 = [], []
        for p in wide:
            value, slope = gelu_both(z1[p])
            h1.append(value.astype(BF16))
            slope1.append(slope)
        own = [[h1[p][64 * j : 64 * j + 64] for j in both] for p in wide]
        ext1 = [[jnp.concatenate([own[p][j], unit], axis=0) for j in both] for p in wide]
        z2 = [[dot(mats[p][j][64:128], ext1[p][j]) for j in both] for p in wide]
        ext2 = [[None, None] for p in wide]
        slope2 = [[None, None] for p in wide]
        for p in wide:
            for j in both:
                value, slope2[p][j] = gelu_both(z2[p][j])
                h2 = (own[p][j].astype(F32) + value).astype(BF16)
                ext2[p][j] = jnp.concatenate([h2, unit], axis=0)
        pred = [
            [dot(mats[p][j][128:144], ext2[p][j])[8 * j : 8 * j + 8] for j in both] for p in wide
        ]
        errors = []
        for p in wide:
            missed = pred[p][0] + pred[p][1] - targets[pairs[p]]
            weighted = wets[pairs[p]] * missed
            loss8 = weighted * missed * (1.0 / (4.0 * VOX))
            dpred = weighted * (2.0 / (4.0 * VOX))
            tail = jnp.concatenate([dpred, loss8], axis=0).astype(BF16)
            errors.append(jnp.concatenate([jnp.zeros((112, VOX), BF16), tail], axis=0))
        head = [
            [jnp.where(keeps[j], mats[p][j][0:64].astype(F32), 0.0).astype(BF16) for j in both]
            for p in wide
        ]
        dh2 = [[dot(head[p][j], errors[p]) for j in both] for p in wide]
        dz2 = [[(dh2[p][j] * slope2[p][j]).astype(BF16) for j in both] for p in wide]
        back = [[dot(mats[p][j][64:128, 0:64], dz2[p][j], TN) for j in both] for p in wide]
        dh1 = [jnp.concatenate([dh2[p][j] + back[p][j] for j in both], axis=0) for p in wide]
        dz1 = [(dh1[p] * slope1[p]).astype(BF16) for p in wide]
        lifted = [dot(dz1[p], patches[p], NT).astype(BF16) for p in wide]
        mixed = [[dot(dz2[p][j], ext1[p][j], NT) for j in both] for p in wide]
        heads = [[dot(ext2[p][j], errors[p], NT) for j in both] for p in wide]
        less = [[dot(lifted[p][64 * j : 64 * j + 64], shrink[j]) for j in both] for p in wide]
        for p in wide:
            for j in both:
                mine_only = jnp.where(owned[j], heads[p][j], 0.0)
                upper = (less[p][j] + mine_only[0:64]).astype(BF16).astype(F32)
                lower = mixed[p][j] + mine_only[64:128]
                lower = jnp.where(lane64 < 64, lower.astype(BF16).astype(F32), lower)
                crops[2 * pairs[p] + j, 0:64] = upper
                crops[2 * pairs[p] + j, 64:128] = lower
        return carry

    keeps = [(lane64 >= 112 + 4 * j) & (lane64 < 116 + 4 * j) for j in range(2)]
    owned = [(lane128 // 4) % 2 == j for j in range(2)]
    lax.fori_loop(0, CROPS_DEV // 2 // GROUP, one_group, 0)

    def member(m):
        return crops[index[m, 0]] + crops[index[m, 1]]

    def theirs(z, carry):
        grads[z] = member(2 * z + 1 - core).astype(BF16)
        return carry

    lax.fori_loop(0, chips, theirs, 0, unroll=chips)

    def remote(src, dst, send, recv, peer):
        copy = pltpu.make_async_remote_copy(
            src_ref=src,
            dst_ref=dst,
            send_sem=send,
            recv_sem=recv,
            device_id=peer,
            device_id_type=MESH,
        )
        copy.start()
        return copy

    first = remote(grads, pair, pair_send.at[0], pair_recv.at[0], at_span(sibling))

    def ours(z, carry):
        held[z] = member(2 * z + core)
        return carry

    lax.fori_loop(0, chips, ours, 0, unroll=chips)
    first.wait()
    for z in range(0, chips, 2):
        two = [held[z + i] + pair[z + i].astype(F32) for i in range(2)]
        two = jnp.concatenate([v.reshape(nn, rows, 128) for v in two], axis=1)
        sent[:, z * rows : (z + 2) * rows, :] = two.astype(BF16)
    seconds = []
    for k, other in enumerate(n_peers):
        seconds.append(
            remote(sent.at[other], parts.at[k], rs_send.at[k], rs_recv.at[k], at_normal(other))
        )
    own = sent[n].astype(F32)
    for k in range(nn - 1):
        seconds[k].wait()
        own = own + parts[k].astype(F32)
    mine[...] = own.reshape(chips, rows, 128)
    thirds = []
    for k, other in enumerate(z_peers):
        thirds.append(
            remote(
                mine.at[other],
                zparts.at[k],
                z_send.at[k],
                z_recv.at[k],
                at_span(other * 2 + core),
            )
        )
    total = mine[chip]
    for k in range(chips - 1):
        thirds[k].wait()
        total = total + zparts[k]
    whole[n] = total * (1.0 / (CROPS_DEV * nn))
    fourths = []
    for k, other in enumerate(n_peers):
        fourths.append(
            remote(
                whole.at[n], whole.at[n], ag_send.at[k], ag_recv.at[k], at_normal(other)
            )
        )
    for copy in fourths:
        copy.wait()
    out[...] = whole[...]


def far_first(count):
    return sorted(range(1, count), key=lambda k: -min(k, count - k))


def normal_peers(n, nn):
    if nn != 16:
        return [(n + k) % nn for k in range(1, nn)]
    moves = [(i, j) for i in range(4) for j in range(4) if i or j]
    moves.sort(key=lambda m: -(min(m[0], 4 - m[0]) + min(m[1], 4 - m[1])))
    return [(n // 4 + i) % 4 * 4 + (n % 4 + j) % 4 for i, j in moves]


def fused_kernel(ns, nn, *refs):
    (
        pop,
        wall,
        w_lift,
        b_lift,
        w_mix,
        b_mix,
        w_head,
        b_head,
        anchors,
        trainers,
        spread,
        select,
        choose,
        inside,
        expand,
        shrink,
        fin,
        total,
    ) = refs[:18]
    fin_sem, v_trainers, v_expand, v_shrink, patches, targets, wets, weights = refs[18:26]
    lattice_refs, train_refs = refs[26:61], refs[61:]
    n = lax.axis_index("normal")
    n_peers = normal_peers(n, nn)
    def meanwhile():
        def remember(m, carry):
            last, before = jnp.int32(CROPS_DEV), jnp.int32(CROPS_DEV)
            for c in range(CROPS_DEV):
                match = v_trainers[0, 0, 0, c] == m
                before = jnp.where(match, last, before)
                last = jnp.where(match, c, last)
            train_refs[1][m, 0] = last
            train_refs[1][m, 1] = before
            return carry

        lax.fori_loop(0, ns, remember, 0)

    lattice_part(
        ns,
        nn,
        pop,
        wall,
        w_lift,
        b_lift,
        w_mix,
        b_mix,
        w_head,
        b_head,
        anchors,
        spread,
        select,
        choose,
        inside,
        ((trainers, v_trainers), (expand, v_expand), (shrink, v_shrink)),
        n_peers,
        meanwhile,
        fin,
        fin_sem,
        patches,
        targets,
        wets,
        *lattice_refs[:26],
        weights,
        *lattice_refs[26:],
    )
    train_part(
        ns,
        nn,
        v_trainers,
        patches,
        targets,
        wets,
        weights,
        v_expand,
        v_shrink,
        total,
        *train_refs,
    )


def unpack_kernel(fin, total, *refs):
    outs, stages, sems = refs[:8], refs[8:15], refs[15]
    o_lift, o_blift, o_mix, o_bmix, o_head, o_bhead, o_loss = stages

    def hop(i, src, dst):
        copy = pltpu.make_async_copy(src, dst, sems.at[i])
        copy.start()
        return copy

    writes = [hop(0, fin, outs[0])]
    whole = total[...].reshape(128, 128)
    turned = whole.T
    o_lift[0] = whole[0:64, 0:108]
    o_mix[0] = whole[64:128, 0:64]
    o_blift[...] = turned[108:109, 0:64]
    o_bmix[...] = turned[64:65, 64:128]
    heads = turned[112:120, 0:64]
    o_head[0] = heads[0:4] + heads[4:8]
    line = whole[64:65]
    o_bhead[...] = line[:, 112:116] + line[:, 116:120]
    lane = lax.broadcasted_iota(jnp.int32, (1, 128), 1)
    o_loss[...] = jnp.sum(jnp.where(lane >= 120, line, 0.0), axis=1, keepdims=True)
    writes += [hop(1 + i, stages[i], outs[1 + i]) for i in range(7)]
    for copy in writes:
        copy.wait()


def local(
    populations, wall_mask, crop_anchors, trainers, w_lift, b_lift, w_mix, b_mix, w_head, b_head
):
    ns, nn = lax.axis_size("span"), lax.axis_size("normal")
    chips = ns // 2
    pairs = CROPS_DEV // 2
    vmem = pl.BlockSpec(memory_space=pltpu.VMEM)
    hbm = pl.BlockSpec(memory_space=pltpu.HBM)
    dma = pltpu.SemaphoreType.DMA
    shape = jax.ShapeDtypeStruct
    cutting, weighing = constants()
    spread, select, choose, inside = cutting
    edge = pltpu.VMEM((SX, CZ, CY), F32)
    flat = pltpu.VMEM((20, 2, 8, 128), F32)
    rows = 128 // nn
    final, total = pl.pallas_call(
        functools.partial(fused_kernel, ns, nn),
        out_shape=(pltpu.VMEM((19, SX, CZ, CY), F32), pltpu.VMEM((nn, rows, 128), F32)),
        in_specs=[hbm] * 16,
        out_specs=(vmem, vmem),
        scratch_shapes=[
            dma,
            pltpu.SMEM((1, 1, 1, CROPS_DEV), jnp.int32),
            pltpu.VMEM((2, 128, 256), BF16),
            pltpu.VMEM((2, 256, 128), BF16),
            pltpu.VMEM((pairs, 256, VOX), BF16),
            pltpu.VMEM((pairs, 8, VOX), F32),
            pltpu.VMEM((pairs, 8, VOX), F32),
            pltpu.VMEM((ns, 144, 128), BF16),
            pltpu.VMEM((SX, CZ, CY), jnp.int32),
            pltpu.VMEM(w_lift.shape, BF16),
            pltpu.VMEM(b_lift.shape, BF16),
            pltpu.VMEM(w_mix.shape, BF16),
            pltpu.VMEM(b_mix.shape, BF16),
            pltpu.VMEM(w_head.shape, BF16),
            pltpu.VMEM(b_head.shape, BF16),
            pltpu.SMEM((1, 3, 1, CROPS_DEV), jnp.int32),
            pltpu.VMEM(spread.shape, F32),
            pltpu.VMEM(select.shape, BF16),
            pltpu.VMEM(choose.shape, BF16),
            pltpu.VMEM(inside.shape, BF16),
            pltpu.VMEM((144, 128), F32),
            pltpu.VMEM((16, 128), F32),
            pltpu.VMEM((SX, 5, CZ, CY), BF16),
            pltpu.VMEM((SX, 4, CZ, CY), BF16),
            pltpu.VMEM((CROPS_DEV, 128, 256), BF16),
            edge,
            edge,
            flat,
            flat,
            edge,
            edge,
            flat,
            flat,
            pltpu.VMEM((4, SX, 8, 128), F32),
            pltpu.VMEM((20, SX, EZ, EY), F32),
            pltpu.VMEM((19, SX, EZ, EY), F32),
            dma((16,)),
            dma((8,)),
            dma((8,)),
            dma((chips,)),
            dma((chips,)),
            dma((chips,)),
            dma((chips,)),
            pltpu.VMEM((CROPS_DEV + 1, 128, 128), F32),
            pltpu.SMEM((ns, 2), jnp.int32),
            pltpu.VMEM((chips, 128, 128), BF16),
            pltpu.VMEM((chips, 128, 128), BF16),
            pltpu.VMEM((chips, 128, 128), F32),
            pltpu.VMEM((nn, chips * rows, 128), BF16),
            pltpu.VMEM((nn - 1, chips * rows, 128), BF16),
            pltpu.VMEM((chips - 1, rows, 128), F32),
            pltpu.VMEM((chips, rows, 128), F32),
            pltpu.VMEM((nn, rows, 128), F32),
            dma((1,)),
            dma((1,)),
            dma((nn - 1,)),
            dma((nn - 1,)),
            dma((chips - 1,)),
            dma((chips - 1,)),
            dma((nn - 1,)),
            dma((nn - 1,)),
        ],
        compiler_params=pltpu.CompilerParams(
            collective_id=0, has_side_effects=True, vmem_limit_bytes=60 << 20
        ),
        name="channel",
    )(
        populations,
        wall_mask,
        w_lift,
        b_lift,
        w_mix,
        b_mix,
        w_head,
        b_head,
        jnp.transpose(crop_anchors, (0, 3, 1, 2)),
        jnp.swapaxes(trainers, 2, 3),
        spread,
        select,
        choose,
        inside,
        *weighing,
    )
    small = [
        shape(w_lift.shape, F32),
        shape(b_lift.shape, F32),
        shape(w_mix.shape, F32),
        shape(b_mix.shape, F32),
        shape(w_head.shape, F32),
        shape(b_head.shape, F32),
        shape((1, 1), F32),
    ]
    outs = pl.pallas_call(
        unpack_kernel,
        out_shape=[shape(populations.shape, F32)] + small,
        in_specs=[vmem, vmem],
        out_specs=[hbm] * 8,
        scratch_shapes=[pltpu.VMEM(leaf.shape, F32) for leaf in small] + [dma((8,))],
        compiler_params=pltpu.CompilerParams(vmem_limit_bytes=4 << 20),
        name="unpack",
    )(final, total)
    return tuple(outs[:7]) + (outs[7].reshape(1),)


def solution(mesh):
    return jax.shard_map(
        local,
        mesh=mesh,
        in_specs=(
            P(None, None, "normal", "span"),
            P(None, "normal", "span"),
            P("normal", "span", None, None),
            P("normal", "span", None, None),
            P("span", None, None),
            P("span", None),
            P("span", None, None),
            P("span", None),
            P("span", None, None),
            P("span", None),
        ),
        out_specs=(
            P(None, None, "normal", "span"),
            P("span", None, None),
            P("span", None),
            P("span", None, None),
            P("span", None),
            P("span", None, None),
            P("span", None),
            P("span"),
        ),
        check_vma=False,
    )
```

```python
import functools

import jax
import jax.numpy as jnp
import numpy as np
from jax import lax
from jax.experimental import pallas as pl
from jax.experimental.pallas import tpu as pltpu
from jax.sharding import PartitionSpec as P

STEPS = 4
CROPS_DEV = 12
GROUP = 6
SX, CZ, CY = 4, 16, 128
EZ, EY = 24, 256
HID = 64
VOX = 512

VELOCITY = (
    (0, 0, 0),
    (1, 0, 0),
    (-1, 0, 0),
    (0, 1, 0),
    (0, -1, 0),
    (0, 0, 1),
    (0, 0, -1),
    (1, 1, 0),
    (-1, -1, 0),
    (1, -1, 0),
    (-1, 1, 0),
    (1, 0, 1),
    (-1, 0, -1),
    (1, 0, -1),
    (-1, 0, 1),
    (0, 1, 1),
    (0, -1, -1),
    (0, 1, -1),
    (0, -1, 1),
)
WEIGHTS = (1.0 / 3.0,) + (1.0 / 18.0,) * 6 + (1.0 / 36.0,) * 12
OPPOSITE = (0, 2, 1, 4, 3, 6, 5, 8, 7, 10, 9, 12, 11, 14, 13, 16, 15, 18, 17)
OMEGA = 1.25
SCALE_DENSITY = 50.0
SCALE_FLOW = 30.0
F32 = jnp.float32
BF16 = jnp.bfloat16
MESH = pl.DeviceIdType.MESH


def signed_sum(entries, factors):
    running = None
    for entry, factor in zip(entries, factors):
        if factor == 0:
            continue
        if running is None:
            running = entry if factor > 0 else -entry
        else:
            running = running + entry if factor > 0 else running - entry
    return running


def moments(states):
    density = states[0]
    for number in range(1, 19):
        density = density + states[number]
    inverse = 1.0 / density
    flows = []
    for axis_id in range(3):
        summed = signed_sum(states, [VELOCITY[number][axis_id] for number in range(19)])
        flows.append(summed * inverse)
    return (density, flows[0], flows[1], flows[2])


def collide(states, wet_cells):
    density, flow_x, flow_y, flow_z = moments(states)
    flows = (flow_x, flow_y, flow_z)
    speed_sq = flow_x * flow_x + flow_y * flow_y + flow_z * flow_z
    base = 1.0 - 1.5 * speed_sq
    result = [None] * 19
    kept = 1.0 - OMEGA
    scaled = {w: (OMEGA * w) * density for w in set(WEIGHTS)}
    relaxed = kept * states[0] + scaled[WEIGHTS[0]] * base
    result[0] = jnp.where(wet_cells, relaxed, states[0])
    for number in range(1, 19, 2):
        other = OPPOSITE[number]
        along = signed_sum(flows, VELOCITY[number])
        weight = scaled[WEIGHTS[number]]
        even = weight * (base + (4.5 * along) * along)
        odd = weight * (3.0 * along)
        forth = kept * states[number] + (even + odd)
        back = kept * states[other] + (even - odd)
        result[number] = jnp.where(wet_cells, forth, states[other])
        result[other] = jnp.where(wet_cells, back, states[number])
    return result


def features(states, fluid):
    density, flow_x, flow_y, flow_z = moments(states)
    return [
        (density - 1.0) * SCALE_DENSITY * fluid,
        flow_x * SCALE_FLOW * fluid,
        flow_y * SCALE_FLOW * fluid,
        flow_z * SCALE_FLOW * fluid,
    ]


NT = (((1,), (1,)), ((), ()))
TN = (((0,), (0,)), ((), ()))


def dot(a, b, dims=(((1,), (0,)), ((), ()))):
    return lax.dot_general(a, b, dims, preferred_element_type=F32)


SHIFTS = [(a, b, c) for a in (-1, 0, 1) for b in (-1, 0, 1) for c in (-1, 0, 1)]


def lattice_part(
    ns,
    nn,
    pop_hbm,
    wall_hbm,
    w_lift,
    b_lift,
    w_mix,
    b_mix,
    w_head,
    b_head,
    anchors_hbm,
    spread_hbm,
    select_hbm,
    choose_hbm,
    inside_hbm,
    more_fetches,
    n_peers,
    meanwhile,
    fin,
    fin_sem,
    patches,
    targets,
    wets,
    wall,
    v_lift,
    v_blift,
    v_mix,
    v_bmix,
    v_head,
    v_bhead,
    anchors,
    spread,
    select,
    choose,
    inside,
    wb,
    small,
    early,
    late,
    windows,
    pack_l,
    pack_r,
    pack_u,
    pack_d,
    got_l,
    got_r,
    got_u,
    got_d,
    got_c,
    weights,
    cells,
    post,
    loads,
    halo_send,
    halo_recv,
    ag_send,
    ag_recv,
    fw_send,
    fw_recv,
):
    s = lax.axis_index("span")
    n = lax.axis_index("normal")
    chips = ns // 2
    chip = s // 2
    core = s % 2
    right, left = (s + 1) % ns, (s + ns - 1) % ns
    up, down = (n + 1) % nn, (n + nn - 1) % nn
    sibling = chip * 2 + (1 - core)

    def place(nn_, ss_):
        return {"normal": nn_, "span": ss_}

    fetches = [
        pltpu.make_async_copy(src, dst, loads.at[i])
        for i, (src, dst) in enumerate(
            (
                (pop_hbm, cells.at[0:19, :, 0:CZ, 0:CY]),
                (wall_hbm, wall),
                (w_lift, v_lift),
                (b_lift, v_blift),
                (w_mix, v_mix),
                (b_mix, v_bmix),
                (w_head, v_head),
                (b_head, v_bhead),
                (anchors_hbm, anchors),
                (spread_hbm, spread),
                (select_hbm, select),
                (choose_hbm, choose),
                (inside_hbm, inside),
                *more_fetches,
            )
        )
    ]
    z_peers = [((chip + k) % chips) * 2 + core for k in range(1, chips)]
    far_z = [((chip + k) % chips) * 2 + core for k in far_first(chips)]
    peers = [place(n, peer) for peer in far_z]
    peers += [place(other, s) for other in n_peers]
    peers += [
        place(up, right),
        place(up, left),
        place(down, right),
        place(down, left),
        place(n, right),
        place(n, left),
        place(n, sibling),
    ]
    barrier = pltpu.get_barrier_semaphore()
    for peer in peers:
        pl.semaphore_signal(barrier, inc=1, device_id=peer, device_id_type=MESH)
    for copy in fetches:
        copy.start()

    sub = lax.broadcasted_iota(jnp.int32, (8, 128), 0)
    low = sub < 4
    wb[...] = jnp.zeros((144, 128), F32)
    small[...] = jnp.zeros((16, 128), F32)
    fetches[0].wait()
    fetches[1].wait()
    cells[19, :, 0:CZ, 0:CY] = wall[...].astype(F32)

    def own_chunk(i, inner):
        x = i // 2
        part = pl.ds(pl.multiple_of((i % 2) * 8, 8), 8)
        states = [cells[q, x, part, 0:CY] for q in range(19)]
        wet = cells[19, x, part, 0:CY] < 0.5
        for q, value in enumerate(collide(states, wet)):
            post[q, x, part, 0:CY] = value
        return inner

    lax.fori_loop(0, 8, own_chunk, 0, unroll=4)

    def source(k):
        return post.at[k] if k < 19 else cells.at[19]

    for k in range(20):
        for j in range(2):
            t0 = source(k)[2 * j, 0:CZ, 0:CY]
            t1 = source(k)[2 * j + 1, 0:CZ, 0:CY]
            pack_u[k, j] = jnp.where(low, pltpu.roll(t1[8:16], 4, 0), t0[8:16])
            pack_d[k, j] = jnp.where(low, t0[0:8], pltpu.roll(t1[0:8], 4, 0))
    pl.semaphore_wait(barrier, len(peers))

    def halo(i, src, dst, peer):
        return pltpu.make_async_remote_copy(
            src_ref=src,
            dst_ref=dst,
            send_sem=halo_send.at[i],
            recv_sem=halo_recv.at[i],
            device_id=peer,
            device_id_type=MESH,
        )

    sends = [
        halo(0, pack_u, got_u, place(up, s)),
        halo(1, pack_d, got_d, place(down, s)),
    ]
    for copy in sends:
        copy.start()
    slot = lax.broadcasted_iota(jnp.int32, (64, 128), 1) // 4
    pl_val = jnp.ones((64, 128), F32)
    pr_val = jnp.ones((64, 128), F32)
    for k in range(20):
        f = source(k)[:, 0:CZ, 0:CY].reshape(64, 128)
        rolled = pltpu.roll(f, 4 * k, 1) if k else f
        pl_val = jnp.where(slot == k, rolled, pl_val)
        pr_val = jnp.where(slot == (k - 1) % 32, rolled, pr_val)
    pack_l[...] = pl_val.reshape(SX, CZ, CY)
    pack_r[...] = pr_val.reshape(SX, CZ, CY)

    top, bottom = pl.ds(8, 8), pl.ds(0, 8)
    more = [
        halo(2, pack_l, got_l, place(n, left)),
        halo(3, pack_r, got_r, place(n, right)),
        halo(4, pack_l.at[:, bottom, :], got_c.at[0], place(down, left)),
        halo(5, pack_l.at[:, top, :], got_c.at[1], place(up, left)),
        halo(6, pack_r.at[:, bottom, :], got_c.at[2], place(down, right)),
        halo(7, pack_r.at[:, top, :], got_c.at[3], place(up, right)),
    ]
    for copy in more:
        copy.start()
    sends += more

    for copy in fetches[2:8]:
        copy.wait()
    wb[0:64, 0:108] = v_lift[0].astype(F32)
    wb[64:128, 0:64] = v_mix[0].astype(F32)
    small[0:1, 0:64] = v_blift[...].astype(F32)
    small[1:2, 0:64] = v_bmix[...].astype(F32)
    small[2:3, 0:4] = v_bhead[...].astype(F32)
    small[4:8, 0:64] = v_head[0].astype(F32)
    row16 = lax.broadcasted_iota(jnp.int32, (16, 128), 0)
    lane16 = lax.broadcasted_iota(jnp.int32, (16, 128), 1)
    head_at = (row16 >= 4) & (row16 < 8)
    head_at = head_at & ((lane16 == row16 + 108) | (lane16 == row16 + 112))
    to_top = ((row16 == 0) & (lane16 == 108)) | head_at
    to_mix = (row16 == 1) & (lane16 == 64)
    to_head = (row16 == 2) & (lane16 == 64)
    rows = small[...].astype(BF16)

    def turned(mask):
        return dot(rows, mask.astype(F32).astype(BF16), TN)

    seat = lax.broadcasted_iota(jnp.int32, (16, 128), 1)
    first = row16 % 12
    held = (row16 < 4) | (row16 >= 12)
    picks = (held & (seat == first)).astype(F32).astype(BF16)
    seat4 = lax.broadcasted_iota(jnp.int32, (16, 16), 1)
    row4 = lax.broadcasted_iota(jnp.int32, (16, 16), 0)
    picks4 = (((row4 < 4) | (row4 >= 12)) & (seat4 == row4 % 12 + 4)).astype(F32).astype(BF16)
    wb[0:64] = wb[0:64] + turned(to_top)[0:64]
    wb[64:128] = wb[64:128] + turned(to_mix)[0:64]
    wb[128:144] = dot(picks4, rows) + dot(picks, turned(to_head).astype(BF16))
    mine = wb[...].astype(BF16)
    weights[s] = mine

    gathers = []
    for k, peer in enumerate(z_peers):
        gathers.append(
            pltpu.make_async_remote_copy(
                src_ref=weights.at[s],
                dst_ref=weights.at[s],
                send_sem=ag_send.at[k],
                recv_sem=ag_recv.at[k],
                device_id=place(n, peer),
                device_id_type=MESH,
            )
        )
    for copy in gathers:
        copy.start()

    def forward(i, owner):
        return pltpu.make_async_remote_copy(
            src_ref=weights.at[owner],
            dst_ref=weights.at[owner],
            send_sem=fw_send.at[i],
            recv_sem=fw_recv.at[i],
            device_id=place(n, sibling),
            device_id_type=MESH,
        )

    forwards = [forward(0, s)]
    forwards[0].start()

    fluid = (1 - wall[...]).astype(F32)
    before = features([cells[q, :, 0:CZ, 0:CY] for q in range(19)], fluid)
    for c in range(4):
        early[:, c] = before[c].astype(BF16)
    early[:, 4] = fluid.astype(BF16)
    for copy in fetches[8:]:
        copy.wait()

    ahead = lax.broadcasted_iota(jnp.int32, (128, 256), 0)
    ahead = ahead - lax.broadcasted_iota(jnp.int32, (128, 256), 1) % 16
    unit_row = (lax.broadcasted_iota(jnp.int32, (40, VOX), 0) == 0).astype(F32)

    def cut(field, count, crop, window):
        ox = anchors[0, 0, 0, crop]
        near = field[ox].reshape(count * CZ, 128)
        far = field[(ox + 1) % SX].reshape(count * CZ, 128)
        wide = dot(jnp.concatenate([near, far], axis=0), window)
        return (wide * spread[0 : count * CZ * 2]).astype(BF16)

    def early_pair(i, carry):
        parts = []
        for j in range(2):
            crop = 2 * i + j
            oy = anchors[0, 1, 0, crop] % CY
            window = (ahead == oy).astype(F32).astype(BF16)
            windows[crop] = window
            parts.append(cut(early, 5, crop, window))
        got = dot(select[...], jnp.concatenate(parts, axis=0))
        x8 = jnp.concatenate([got[0:8], got[8:16]], axis=1)
        wets[i] = jnp.concatenate([got[16:24], got[24:32]], axis=1)
        moved = []
        for dx, dz, dy in SHIFTS:
            shift = (-(dx * 256 + dz * 16 + dy)) % VOX
            moved.append(pltpu.roll(x8, shift, 1) if shift else x8)
        moved.append(unit_row)
        patches[i] = jnp.concatenate(moved, axis=0).astype(BF16) * inside[...]
        return carry

    lax.fori_loop(0, CROPS_DEV // 2, early_pair, 0)

    meanwhile()
    for copy in sends[2:]:
        copy.wait()

    low4 = jnp.broadcast_to(low[None], (SX, 8, 128))
    edge_l = jnp.concatenate([got_l[...], jnp.where(low4, got_c[0], got_c[1])], axis=1)
    edge_r = jnp.concatenate([got_r[...], jnp.where(low4, got_c[2], got_c[3])], axis=1)
    edge_l = edge_l.reshape(SX * EZ, 128)
    edge_r = edge_r.reshape(SX * EZ, 128)
    odd = (lax.broadcasted_iota(jnp.int32, (SX * EZ, 128), 1) // 4) % 2 == 1
    mixed = (jnp.where(odd, edge_r, edge_l), jnp.where(odd, edge_l, edge_r))
    for k in range(20):
        side = mixed[k % 2]
        if k:
            side = pltpu.roll(side, 128 - 4 * k, 1)
        source(k)[:, :, CY:EY] = side.reshape(SX, EZ, 128)
    for copy in sends[:2]:
        copy.wait()
    for k in range(20):
        for j in range(2):
            u, d = got_u[k, j], got_d[k, j]
            source(k)[2 * j, CZ:EZ, 0:CY] = jnp.where(low, d, u)
            source(k)[2 * j + 1, CZ:EZ, 0:CY] = pltpu.roll(jnp.where(low, u, d), 4, 0)

    def one_step(step, carry, last=False):
        def one_chunk(i, inner):
            x = i // 3
            part = pl.ds(pl.multiple_of((i % 3) * 8, 8), 8)
            states = [cells[q, x, part, :] for q in range(19)]
            wet = cells[19, x, part, :] < 0.5
            for q, value in enumerate(collide(states, wet)):
                post[q, x, part, :] = value
            return inner

        lax.fori_loop(0, 12, one_chunk, 0, unroll=6)
        move(last)
        return carry

    def move(last=False):
        def one_slab(x, inner):
            for q in range(19):
                cx, cy, cz = VELOCITY[q]
                slab = post[q, (x + SX - cx) % SX]
                if cz:
                    slab = pltpu.roll(slab, cz % EZ, 0)
                if cy:
                    slab = pltpu.roll(slab, cy % EY, 1)
                if last:
                    fin[q, x] = slab[0:CZ, 0:CY]
                else:
                    cells[q, x] = slab
            return inner

        lax.fori_loop(0, SX, one_slab, 0, unroll=4)

    move()
    one_step(1, 0)
    one_step(2, 0)
    for k in range(1, chips):
        gathers[k - 1].wait()
        owner = ((chip + chips - k) % chips) * 2 + core
        copy = forward(k, owner)
        copy.start()
        forwards.append(copy)
    one_step(3, 0, True)

    final = [fin[q] for q in range(19)]
    after = features(final, fluid)
    for c in range(4):
        late[:, c] = (after[c] - before[c]).astype(BF16)

    cuts = [cut(late, 4, crop, windows[crop]) for crop in range(CROPS_DEV)]
    for i in range(CROPS_DEV // 2):
        got = dot(choose[...], jnp.concatenate(cuts[2 * i : 2 * i + 2], axis=0))
        targets[i] = jnp.concatenate([got[0:8], got[8:16]], axis=1)
    for copy in forwards:
        copy.wait()


def gelu_both(x):
    c1, c2 = 0.7978845608028654, 0.7978845608028654 * 0.044715
    sq = x * x
    half = 0.5 * jnp.tanh(x * (c1 + c2 * sq)) + 0.5
    value = x * half
    slope = half + value * (1.0 - half) * (2.0 * c1 + 6.0 * c2 * sq)
    return value, slope


def constants():
    row = np.arange(160)
    lane = np.arange(256)
    spread = (lane[None, :] // 16 == row[:, None] % 16).astype(np.float32)
    select = np.zeros((32, 320), np.float32)
    choose = np.zeros((16, 256), np.float32)
    for xi in range(2):
        for i in range(8):
            crop, channel = i // 4, i % 4
            start = crop * 160 + xi * 80 + channel * 16
            select[xi * 8 + i, start : start + 16] = 1.0
            start = crop * 160 + xi * 80 + 64
            select[16 + xi * 8 + i, start : start + 16] = 1.0
            start = crop * 128 + xi * 64 + channel * 16
            choose[xi * 8 + i, start : start + 16] = 1.0
    expand = np.zeros((2, 128, 256), np.float32)
    for pos in range(2):
        for k in range(27):
            for c in range(4):
                expand[pos, 4 * k + c, 8 * k + 4 * pos + c] = 1.0
        expand[pos, 108, 216] = 1.0
    voxel = np.arange(VOX)
    vx, vz, vy = voxel // 256, voxel // 16 % 16, voxel % 16
    inside = np.ones((256, VOX), np.float32)
    for k, (dx, dz, dy) in enumerate(SHIFTS):
        good = (
            (vx + dx >= 0)
            & (vx + dx < 2)
            & (vz + dz >= 0)
            & (vz + dz < 16)
            & (vy + dy >= 0)
            & (vy + dy < 16)
        )
        inside[8 * k : 8 * k + 8] = good[None]
    return (
        (
            jnp.asarray(spread),
            jnp.asarray(select, BF16),
            jnp.asarray(choose, BF16),
            jnp.asarray(inside, BF16),
        ),
        (
            jnp.asarray(expand, BF16),
            jnp.asarray(np.transpose(expand, (0, 2, 1)), BF16),
        ),
    )


def train_part(
    ns,
    nn,
    trainers,
    patches_ref,
    targets,
    wets,
    wall_w,
    expand,
    shrink,
    out,
    crops,
    index,
    grads,
    pair,
    held,
    sent,
    parts,
    zparts,
    mine,
    whole,
    pair_send,
    pair_recv,
    rs_send,
    rs_recv,
    z_send,
    z_recv,
    ag_send,
    ag_recv,
):
    s = lax.axis_index("span")
    n = lax.axis_index("normal")
    chips = ns // 2
    chip = s // 2
    core = s % 2
    sibling = chip * 2 + (1 - core)
    rows = 128 // nn
    n_peers = normal_peers(n, nn)
    z_peers = [(chip + k) % chips for k in far_first(chips)]

    def at_span(other):
        return {"span": other, "normal": n}

    def at_normal(other):
        return {"span": s, "normal": other}

    crops[CROPS_DEV] = jnp.zeros((128, 128), F32)
    unit = (lax.broadcasted_iota(jnp.int32, (64, VOX), 0) == 0).astype(F32).astype(BF16)
    lane64 = lax.broadcasted_iota(jnp.int32, (64, 128), 1)
    lane128 = lax.broadcasted_iota(jnp.int32, (128, 128), 1)

    def remote(src, dst, send, recv, peer):
        copy = pltpu.make_async_remote_copy(
            src_ref=src,
            dst_ref=dst,
            send_sem=send,
            recv_sem=recv,
            device_id=peer,
            device_id_type=MESH,
        )
        copy.start()
        return copy

    def member(m):
        return crops[index[m, 0]] + crops[index[m, 1]]

    def send_half(half):
        part = pl.ds(64 * half, 64)
        for z in range(chips):
            m = 2 * z + 1 - core
            value = crops[index[m, 0], part] + crops[index[m, 1], part]
            grads[half, z] = value.astype(BF16)
        return remote(
            grads.at[half],
            pair.at[half],
            pair_send.at[half],
            pair_recv.at[half],
            at_span(sibling),
        )

    def one_group(g):
        wide = range(GROUP)
        both = range(2)
        pairs = [g * GROUP + p for p in wide]
        mats = [[wall_w[trainers[0, 0, 0, 2 * i + j]] for j in both] for i in pairs]
        patches = [patches_ref[i] for i in pairs]
        lift = [[dot(mats[p][j][0:64], expand[j]) for j in both] for p in wide]
        lift = [jnp.concatenate(lift[p], axis=0).astype(BF16) for p in wide]
        z1 = [dot(lift[p], patches[p]) for p in wide]
        h1, slope1 = [], []
        for p in wide:
            value, slope = gelu_both(z1[p])
            h1.append(value.astype(BF16))
            slope1.append(slope)
        own = [[h1[p][64 * j : 64 * j + 64] for j in both] for p in wide]
        ext1 = [[jnp.concatenate([own[p][j], unit], axis=0) for j in both] for p in wide]
        z2 = [[dot(mats[p][j][64:128], ext1[p][j]) for j in both] for p in wide]
        ext2 = [[None, None] for p in wide]
        slope2 = [[None, None] for p in wide]
        for p in wide:
            for j in both:
                value, slope2[p][j] = gelu_both(z2[p][j])
                h2 = (own[p][j].astype(F32) + value).astype(BF16)
                ext2[p][j] = jnp.concatenate([h2, unit], axis=0)
        pred = [
            [dot(mats[p][j][128:144], ext2[p][j])[8 * j : 8 * j + 8] for j in both] for p in wide
        ]
        errors = []
        for p in wide:
            missed = pred[p][0] + pred[p][1] - targets[pairs[p]]
            weighted = wets[pairs[p]] * missed
            loss8 = weighted * missed * (1.0 / (4.0 * VOX))
            dpred = weighted * (2.0 / (4.0 * VOX))
            tail = jnp.concatenate([dpred, loss8], axis=0).astype(BF16)
            errors.append(jnp.concatenate([jnp.zeros((112, VOX), BF16), tail], axis=0))
        head = [
            [jnp.where(keeps[j], mats[p][j][0:64].astype(F32), 0.0).astype(BF16) for j in both]
            for p in wide
        ]
        dh2 = [[dot(head[p][j], errors[p]) for j in both] for p in wide]
        dz2 = [[(dh2[p][j] * slope2[p][j]).astype(BF16) for j in both] for p in wide]
        back = [[dot(mats[p][j][64:128, 0:64], dz2[p][j], TN) for j in both] for p in wide]
        dh1 = [jnp.concatenate([dh2[p][j] + back[p][j] for j in both], axis=0) for p in wide]
        dz1 = [(dh1[p] * slope1[p]).astype(BF16) for p in wide]
        mixed = [[dot(dz2[p][j], ext1[p][j], NT) for j in both] for p in wide]
        heads = [[dot(ext2[p][j], errors[p], NT) for j in both] for p in wide]
        for p in wide:
            for j in both:
                lower = mixed[p][j] + jnp.where(owned[j], heads[p][j], 0.0)[64:128]
                lower = jnp.where(lane64 < 64, lower.astype(BF16).astype(F32), lower)
                crops[2 * pairs[p] + j, 64:128] = lower
        early = send_half(1)
        lifted = [dot(dz1[p], patches[p], NT).astype(BF16) for p in wide]
        less = [[dot(lifted[p][64 * j : 64 * j + 64], shrink[j]) for j in both] for p in wide]
        for p in wide:
            for j in both:
                mine_only = jnp.where(owned[j], heads[p][j], 0.0)
                upper = (less[p][j] + mine_only[0:64]).astype(BF16).astype(F32)
                crops[2 * pairs[p] + j, 0:64] = upper
        return early

    keeps = [(lane64 >= 112 + 4 * j) & (lane64 < 116 + 4 * j) for j in range(2)]
    owned = [(lane128 // 4) % 2 == j for j in range(2)]
    early_half = one_group(0)

    late_half = send_half(0)

    def ours(z, carry):
        held[z] = member(2 * z + core)
        return carry

    lax.fori_loop(0, chips, ours, 0, unroll=chips)
    early_half.wait()
    late_half.wait()
    for z in range(0, chips, 2):
        got = [jnp.concatenate([pair[0, z + i], pair[1, z + i]], axis=0) for i in range(2)]
        two = [held[z + i] + got[i].astype(F32) for i in range(2)]
        two = jnp.concatenate([v.reshape(nn, rows, 128) for v in two], axis=1)
        sent[:, z * rows : (z + 2) * rows, :] = two.astype(BF16)
    seconds = []
    for k, other in enumerate(n_peers):
        seconds.append(
            remote(sent.at[other], parts.at[k], rs_send.at[k], rs_recv.at[k], at_normal(other))
        )
    own = sent[n].astype(F32)
    for k in range(nn - 1):
        seconds[k].wait()
        own = own + parts[k].astype(F32)
    mine[...] = own.reshape(chips, rows, 128)
    thirds = []
    for k, other in enumerate(z_peers):
        thirds.append(
            remote(
                mine.at[other],
                zparts.at[k],
                z_send.at[k],
                z_recv.at[k],
                at_span(other * 2 + core),
            )
        )
    total = mine[chip]
    for k in range(chips - 1):
        thirds[k].wait()
        total = total + zparts[k]
    whole[n] = total * (1.0 / (CROPS_DEV * nn))
    fourths = []
    for k, other in enumerate(n_peers):
        fourths.append(
            remote(
                whole.at[n], whole.at[n], ag_send.at[k], ag_recv.at[k], at_normal(other)
            )
        )
    for copy in fourths:
        copy.wait()
    out[...] = whole[...]


def far_first(count):
    return sorted(range(1, count), key=lambda k: -min(k, count - k))


def normal_peers(n, nn):
    if nn != 16:
        return [(n + k) % nn for k in range(1, nn)]
    moves = [(i, j) for i in range(4) for j in range(4) if i or j]
    moves.sort(key=lambda m: -(min(m[0], 4 - m[0]) + min(m[1], 4 - m[1])))
    return [(n // 4 + i) % 4 * 4 + (n % 4 + j) % 4 for i, j in moves]


def fused_kernel(ns, nn, *refs):
    (
        pop,
        wall,
        w_lift,
        b_lift,
        w_mix,
        b_mix,
        w_head,
        b_head,
        anchors,
        trainers,
        spread,
        select,
        choose,
        inside,
        expand,
        shrink,
        fin,
        total,
    ) = refs[:18]
    fin_sem, v_trainers, v_expand, v_shrink, patches, targets, wets, weights = refs[18:26]
    lattice_refs, train_refs = refs[26:61], refs[61:]
    n = lax.axis_index("normal")
    n_peers = normal_peers(n, nn)
    def meanwhile():
        def remember(m, carry):
            last, before = jnp.int32(CROPS_DEV), jnp.int32(CROPS_DEV)
            for c in range(CROPS_DEV):
                match = v_trainers[0, 0, 0, c] == m
                before = jnp.where(match, last, before)
                last = jnp.where(match, c, last)
            train_refs[1][m, 0] = last
            train_refs[1][m, 1] = before
            return carry

        lax.fori_loop(0, ns, remember, 0)

    lattice_part(
        ns,
        nn,
        pop,
        wall,
        w_lift,
        b_lift,
        w_mix,
        b_mix,
        w_head,
        b_head,
        anchors,
        spread,
        select,
        choose,
        inside,
        ((trainers, v_trainers), (expand, v_expand), (shrink, v_shrink)),
        n_peers,
        meanwhile,
        fin,
        fin_sem,
        patches,
        targets,
        wets,
        *lattice_refs[:26],
        weights,
        *lattice_refs[26:],
    )
    train_part(
        ns,
        nn,
        v_trainers,
        patches,
        targets,
        wets,
        weights,
        v_expand,
        v_shrink,
        total,
        *train_refs,
    )


def unpack_kernel(fin, total, *refs):
    outs, stages, sems = refs[:8], refs[8:15], refs[15]
    o_lift, o_blift, o_mix, o_bmix, o_head, o_bhead, o_loss = stages

    def hop(i, src, dst):
        copy = pltpu.make_async_copy(src, dst, sems.at[i])
        copy.start()
        return copy

    writes = [hop(0, fin, outs[0])]
    whole = total[...].reshape(128, 128)
    turned = whole.T
    o_lift[0] = whole[0:64, 0:108]
    o_mix[0] = whole[64:128, 0:64]
    o_blift[...] = turned[108:109, 0:64]
    o_bmix[...] = turned[64:65, 64:128]
    heads = turned[112:120, 0:64]
    o_head[0] = heads[0:4] + heads[4:8]
    line = whole[64:65]
    o_bhead[...] = line[:, 112:116] + line[:, 116:120]
    lane = lax.broadcasted_iota(jnp.int32, (1, 128), 1)
    o_loss[...] = jnp.sum(jnp.where(lane >= 120, line, 0.0), axis=1, keepdims=True)
    writes += [hop(1 + i, stages[i], outs[1 + i]) for i in range(7)]
    for copy in writes:
        copy.wait()


def local(
    populations, wall_mask, crop_anchors, trainers, w_lift, b_lift, w_mix, b_mix, w_head, b_head
):
    ns, nn = lax.axis_size("span"), lax.axis_size("normal")
    chips = ns // 2
    pairs = CROPS_DEV // 2
    vmem = pl.BlockSpec(memory_space=pltpu.VMEM)
    hbm = pl.BlockSpec(memory_space=pltpu.HBM)
    dma = pltpu.SemaphoreType.DMA
    shape = jax.ShapeDtypeStruct
    cutting, weighing = constants()
    spread, select, choose, inside = cutting
    edge = pltpu.VMEM((SX, CZ, CY), F32)
    flat = pltpu.VMEM((20, 2, 8, 128), F32)
    rows = 128 // nn
    final, total = pl.pallas_call(
        functools.partial(fused_kernel, ns, nn),
        out_shape=(pltpu.VMEM((19, SX, CZ, CY), F32), pltpu.VMEM((nn, rows, 128), F32)),
        in_specs=[hbm] * 16,
        out_specs=(vmem, vmem),
        scratch_shapes=[
            dma,
            pltpu.SMEM((1, 1, 1, CROPS_DEV), jnp.int32),
            pltpu.VMEM((2, 128, 256), BF16),
            pltpu.VMEM((2, 256, 128), BF16),
            pltpu.VMEM((pairs, 256, VOX), BF16),
            pltpu.VMEM((pairs, 8, VOX), F32),
            pltpu.VMEM((pairs, 8, VOX), F32),
            pltpu.VMEM((ns, 144, 128), BF16),
            pltpu.VMEM((SX, CZ, CY), jnp.int32),
            pltpu.VMEM(w_lift.shape, BF16),
            pltpu.VMEM(b_lift.shape, BF16),
            pltpu.VMEM(w_mix.shape, BF16),
            pltpu.VMEM(b_mix.shape, BF16),
            pltpu.VMEM(w_head.shape, BF16),
            pltpu.VMEM(b_head.shape, BF16),
            pltpu.SMEM((1, 3, 1, CROPS_DEV), jnp.int32),
            pltpu.VMEM(spread.shape, F32),
            pltpu.VMEM(select.shape, BF16),
            pltpu.VMEM(choose.shape, BF16),
            pltpu.VMEM(inside.shape, BF16),
            pltpu.VMEM((144, 128), F32),
            pltpu.VMEM((16, 128), F32),
            pltpu.VMEM((SX, 5, CZ, CY), BF16),
            pltpu.VMEM((SX, 4, CZ, CY), BF16),
            pltpu.VMEM((CROPS_DEV, 128, 256), BF16),
            edge,
            edge,
            flat,
            flat,
            edge,
            edge,
            flat,
            flat,
            pltpu.VMEM((4, SX, 8, 128), F32),
            pltpu.VMEM((20, SX, EZ, EY), F32),
            pltpu.VMEM((19, SX, EZ, EY), F32),
            dma((16,)),
            dma((8,)),
            dma((8,)),
            dma((chips,)),
            dma((chips,)),
            dma((chips,)),
            dma((chips,)),
            pltpu.VMEM((CROPS_DEV + 1, 128, 128), F32),
            pltpu.SMEM((ns, 2), jnp.int32),
            pltpu.VMEM((2, chips, 64, 128), BF16),
            pltpu.VMEM((2, chips, 64, 128), BF16),
            pltpu.VMEM((chips, 128, 128), F32),
            pltpu.VMEM((nn, chips * rows, 128), BF16),
            pltpu.VMEM((nn - 1, chips * rows, 128), BF16),
            pltpu.VMEM((chips - 1, rows, 128), F32),
            pltpu.VMEM((chips, rows, 128), F32),
            pltpu.VMEM((nn, rows, 128), F32),
            dma((2,)),
            dma((2,)),
            dma((nn - 1,)),
            dma((nn - 1,)),
            dma((chips - 1,)),
            dma((chips - 1,)),
            dma((nn - 1,)),
            dma((nn - 1,)),
        ],
        compiler_params=pltpu.CompilerParams(
            collective_id=0, has_side_effects=True, vmem_limit_bytes=60 << 20
        ),
        name="channel",
    )(
        populations,
        wall_mask,
        w_lift,
        b_lift,
        w_mix,
        b_mix,
        w_head,
        b_head,
        jnp.transpose(crop_anchors, (0, 3, 1, 2)),
        jnp.swapaxes(trainers, 2, 3),
        spread,
        select,
        choose,
        inside,
        *weighing,
    )
    small = [
        shape(w_lift.shape, F32),
        shape(b_lift.shape, F32),
        shape(w_mix.shape, F32),
        shape(b_mix.shape, F32),
        shape(w_head.shape, F32),
        shape(b_head.shape, F32),
        shape((1, 1), F32),
    ]
    outs = pl.pallas_call(
        unpack_kernel,
        out_shape=[shape(populations.shape, F32)] + small,
        in_specs=[vmem, vmem],
        out_specs=[hbm] * 8,
        scratch_shapes=[pltpu.VMEM(leaf.shape, F32) for leaf in small] + [dma((8,))],
        compiler_params=pltpu.CompilerParams(vmem_limit_bytes=4 << 20),
        name="unpack",
    )(final, total)
    return tuple(outs[:7]) + (outs[7].reshape(1),)


def solution(mesh):
    return jax.shard_map(
        local,
        mesh=mesh,
        in_specs=(
            P(None, None, "normal", "span"),
            P(None, "normal", "span"),
            P("normal", "span", None, None),
            P("normal", "span", None, None),
            P("span", None, None),
            P("span", None),
            P("span", None, None),
            P("span", None),
            P("span", None, None),
            P("span", None),
        ),
        out_specs=(
            P(None, None, "normal", "span"),
            P("span", None, None),
            P("span", None),
            P("span", None, None),
            P("span", None),
            P("span", None, None),
            P("span", None),
            P("span"),
        ),
        check_vma=False,
    )
```
